128 devices in a mesh: blocks: 32 (over x, y, core), slab: 4 (over z).
Axes of the slice: x: 4, y: 4, z: 4, core: 2. Of those that a mesh axis runs over, the one named last changes fastest.
Arguments:
- populations: float32 [19, 4, 32, 4096], P(None, 'slab', 'blocks'), may hold values from -6 to 6
- w_in: bfloat16 [512, 19], replicated, may hold values from -1.25 to 1.25
- w_mid: bfloat16 [1, 512, 512], replicated, may hold values from -0.25 to 0.25
- w_out: bfloat16 [19, 512], replicated, may hold values from -0.25 to 0.25
- cotangent: float32 [19, 4, 32, 4096], P(None, 'slab', 'blocks'), may hold values from -6 to 6
- face_source: int32 [32, 4], replicated, may hold values from 0 to 31, as said below
- face_level: int32 [4, 32, 6], P('slab', 'blocks'), may hold values 0 or 1
- face_quadrant: int32 [4, 32, 6], P('slab', 'blocks'), may hold values from 0 to 3
Outputs:
- final: float32 [19, 4, 32, 4096], P(None, 'slab', 'blocks')
- grad_pops: float32 [19, 4, 32, 4096], P(None, 'slab', 'blocks')
- grad_in: float32 [512, 19], replicated
- grad_mid: float32 [1, 512, 512], replicated
- grad_out: float32 [19, 512], replicated
The draws below stay inside these ranges and needn't reach their ends.
Inputs may be any that keep to these rules, and one draw needn't show every extreme that they name: face_source is symmetric: face_source[face_source[b, f], f xor 1] = b. The +y and -y neighbours of block b are the same block, b xor 1. Every neighbour's index differs from the block's by at most 3 modulo 32, never by 0, and that distance is reached.
All inputs are finite; a program needn't handle non-finite values. No bound on the sum of `face_level` on one device may be relied on, other than what follows from the above.
Results may differ from the reference program's by a relative error of at most 0.0088.
Values sent between devices are 32-bit elements; how exact they have to be, the bound alone decides.
No kernel may reach another device: no remote copies, remote signals or barrier semaphores. Data moves between devices by JAX's collectives and lax.ppermute only.
A program may use at most 128 MiB of HBM per device.

```python
from functools import partial
import jax
import jax.numpy as jnp
from jax import lax

Q = 19
HID = 512
MIDS = 1
S = 16
STEPS = 2
CELLS = 4096
GX = 16
CELLS_ALL = 524288
N_BLOCKS = 32
N_SLAB = 4


def placement_tables(key):
    flips = jax.random.randint(jax.random.fold_in(key, 7), (GX,), 0, 2).astype(jnp.int32)
    anchor = jax.random.randint(jax.random.fold_in(key, 11), (), 0, GX).astype(jnp.int32)
    mirror = jax.random.randint(jax.random.fold_in(key, 13), (), 0, 2).astype(jnp.int32)
    follow = (anchor + 1) % GX
    flips = flips.at[follow].set(1 - flips[anchor])
    location = jnp.arange(GX * 2, dtype=jnp.int32)
    column = location // 2
    stored = location % 2
    parity = jnp.bitwise_xor(stored, flips[column])
    next_column = (column + 1) % GX
    prior_column = (column + GX - 1) % GX
    forward_x = next_column * 2 + jnp.bitwise_xor(parity, flips[next_column])
    backward_x = prior_column * 2 + jnp.bitwise_xor(parity, flips[prior_column])
    plus_x = jnp.where(mirror == 1, backward_x, forward_x)
    minus_x = jnp.where(mirror == 1, forward_x, backward_x)
    other_y = column * 2 + (1 - stored)
    return jnp.stack([plus_x, minus_x, other_y, other_y], axis=1).astype(jnp.int32)


def draw_face_source(key, part):
    return placement_tables(key)


def with_ends(array, key, low, high):
    spot = [jax.random.randint(jax.random.fold_in(key, axis), (), 0, length) for axis, length in enumerate(array.shape)]
    longest = array.shape.index(max(array.shape))
    beside = spot[:longest] + [(spot[longest] + 1) % array.shape[longest]] + spot[longest + 1:]
    return array.at[tuple(spot)].set(low).at[tuple(beside)].set(high)


def level_of(stream_key, dims, shards, low, high):
    def one(dim, shards_of):
        heights = jax.random.uniform(jax.random.fold_in(jax.random.fold_in(stream_key, 6), dim), (shards_of,), jnp.float32, low / len(shards), high / len(shards))
        return jnp.repeat(jnp.exp(heights), dims[dim] // shards_of).reshape((-1,) + (1,) * (len(dims) - dim - 1))

    level = one(*shards[0])
    for cut in shards[1:]:
        level = level * one(*cut)
    return level


def centred(rng, extent, spread, most, split=(), kind=jnp.bfloat16):
    drawn = jax.random.normal(rng, extent, jnp.float32) * spread
    if len(split) > 0:
        drawn = level_of(rng, extent, split, -0.22, 0.18) * drawn
    return jnp.clip(drawn, min=-most, max=most).astype(kind)


def setup_inputs(seed: int = 0) -> dict:
    key_list = jax.random.split(jax.random.key(seed), 9)
    populations = centred(key_list[0], (Q, N_SLAB, N_BLOCKS, CELLS), 1.0, 6.0, ((1, 4), (2, 32)), jnp.float32)
    w_in = centred(key_list[1], (HID, Q), Q ** -0.5, 1.25)
    w_mid = centred(key_list[2], (MIDS, HID, HID), HID ** -0.5, 0.25)
    w_out = centred(key_list[3], (Q, HID), HID ** -0.5, 0.25)
    cotangent = centred(key_list[4], (Q, N_SLAB, N_BLOCKS, CELLS), 1.0, 6.0, ((1, 4), (2, 32)), jnp.float32)
    face_source = draw_face_source(jax.random.fold_in(key_list[8], 71), 0)
    face_level = with_ends((jax.random.randint(key_list[6], (N_SLAB, N_BLOCKS, 6), 0, 2) < 1).astype(jnp.int32), jax.random.fold_in(key_list[6], 1), 0, 1)
    face_quadrant = with_ends(jax.random.randint(key_list[7], (N_SLAB, N_BLOCKS, 6), 0, 4), jax.random.fold_in(key_list[7], 1), 0, 3).astype(jnp.int32)
    return {"populations": populations, "w_in": w_in, "w_mid": w_mid, "w_out": w_out, "cotangent": cotangent, "face_source": face_source, "face_level": face_level, "face_quadrant": face_quadrant}


VELOCITIES = [(0, 0, 0), (1, 0, 0), (-1, 0, 0), (0, 1, 0), (0, -1, 0), (0, 0, 1), (0, 0, -1), (1, 1, 0), (-1, -1, 0), (1, -1, 0), (-1, 1, 0), (1, 0, 1), (-1, 0, -1), (1, 0, -1), (-1, 0, 1), (0, 1, 1), (0, -1, -1), (0, 1, -1), (0, -1, 1)]
OPPOSITE = [0, 2, 1, 4, 3, 6, 5, 8, 7, 10, 9, 12, 11, 14, 13, 16, 15, 18, 17]

def face_members(face_id):
    along = face_id // 2
    sign_value = 1 if face_id % 2 == 0 else -1
    return [which for which in range(19) if VELOCITIES[which][along] == sign_value]

def face_layers(collided, block_side):
    cube_view = collided.reshape(collided.shape[0], block_side, block_side, block_side)
    sheets = []
    for face_id in range(6):
        along = face_id // 2
        layer_index = block_side - 1 if face_id % 2 == 0 else 0
        members = jnp.stack([cube_view[which] for which in face_members(face_id)])
        layer_sheet = lax.index_in_dim(members, layer_index, along + 1, keepdims=False)
        sheets.append(layer_sheet.reshape(5, block_side * block_side))
    return jnp.stack(sheets)

def refine_sheet(layer_sheet, levels, quadrant, block_side):
    square = layer_sheet.reshape(5, block_side, block_side)
    half_side = block_side // 2
    row_start = (quadrant // 2 * half_side).astype(jnp.int32)
    col_start = (quadrant % 2 * half_side).astype(jnp.int32)
    corner_part = lax.dynamic_slice(square, (jnp.zeros((), jnp.int32), row_start, col_start), (5, half_side, half_side))
    enlarged = jnp.repeat(jnp.repeat(corner_part, 2, axis=1), 2, axis=2)
    return jnp.where(levels == 1, enlarged, square).reshape(5, block_side * block_side)

def stream_block(collided, ghosts, block_side):
    cube_view = collided.reshape(collided.shape[0], block_side, block_side, block_side)
    shape3 = (block_side, block_side, block_side)
    coords = [lax.broadcasted_iota(jnp.int32, shape3, along) for along in range(3)]
    results = []
    for which in range(19):
        vector = VELOCITIES[which]
        shifted = jnp.roll(cube_view[which], shift=vector, axis=(0, 1, 2))
        crossed = jnp.zeros(shape3, jnp.int32)
        ghost_sum = jnp.zeros(shape3, jnp.float32)
        for along in range(3):
            if vector[along] != 0:
                leaving = coords[along] == (0 if vector[along] == 1 else block_side - 1)
                face_id = 2 * along + (0 if vector[along] == -1 else 1)
                position = face_members(face_id ^ 1).index(which)
                others = [other for other in range(3) if other != along]
                square = ghosts[face_id, position].reshape(block_side, block_side)
                square = jnp.roll(square, shift=(vector[others[0]], vector[others[1]]), axis=(0, 1))
                volume = jnp.expand_dims(square, along)
                ghost_sum = ghost_sum + jnp.where(leaving, volume, jnp.float32(0.0))
                crossed = crossed + leaving.astype(jnp.int32)
        chosen = jnp.where(crossed == 0, shifted, jnp.where(crossed == 1, ghost_sum, cube_view[OPPOSITE[which]]))
        results.append(chosen.reshape(-1))
    return jnp.stack(results)

def contract(left, right):
    return lax.dot_general(left, right, (((1,), (1,)), ((), ())), preferred_element_type=jnp.float32)

def squared(hidden):
    wide_value = hidden.astype(jnp.float32)
    return wide_value * wide_value

def collide_forward(state, w_in, w_mid, w_out):
    inputs_bf = state.astype(jnp.bfloat16)
    layers = [jnp.tanh(jnp.dot(w_in, inputs_bf, preferred_element_type=jnp.float32)).astype(jnp.bfloat16)]
    for depth in range(w_mid.shape[0]):
        layers.append(jnp.tanh(jnp.dot(w_mid[depth], layers[-1], preferred_element_type=jnp.float32)).astype(jnp.bfloat16))
    collided = state + jnp.dot(w_out, layers[-1], preferred_element_type=jnp.float32)
    return (collided, inputs_bf, layers)

def collide_backward(collided_bar, inputs_bf, layers, w_in, w_mid, w_out):
    delta_bf = collided_bar.astype(jnp.bfloat16)
    grad_out = contract(delta_bf, layers[-1])
    signal = (jnp.dot(w_out.T, delta_bf, preferred_element_type=jnp.float32) * (1.0 - squared(layers[-1]))).astype(jnp.bfloat16)
    mid_parts = []
    for depth in reversed(range(w_mid.shape[0])):
        mid_parts.insert(0, contract(signal, layers[depth]))
        signal = (jnp.dot(w_mid[depth].T, signal, preferred_element_type=jnp.float32) * (1.0 - squared(layers[depth]))).astype(jnp.bfloat16)
    grad_in = contract(signal, inputs_bf)
    state_bar = collided_bar + jnp.dot(w_in.T, signal, preferred_element_type=jnp.float32)
    return (state_bar, grad_in, jnp.stack(mid_parts), grad_out)

def stream_all(collided, face_source, face_level, face_quadrant):
    outward = jax.vmap(jax.vmap(partial(face_layers, block_side=S)))(collided)
    lateral = [jnp.take(outward[:, :, face_id ^ 1], face_source[:, face_id], axis=1) for face_id in range(4)]
    from_above = jnp.roll(outward[:, :, 5], -1, axis=0)
    from_below = jnp.roll(outward[:, :, 4], 1, axis=0)
    sheets = jnp.stack(lateral + [from_above, from_below], axis=2)
    ghosts = jax.vmap(jax.vmap(jax.vmap(partial(refine_sheet, block_side=S))))(sheets, face_level, face_quadrant)
    return jax.vmap(jax.vmap(partial(stream_block, block_side=S)))(collided, ghosts)

def reference(populations, w_in, w_mid, w_out, cotangent, face_source, face_level, face_quadrant):
    state = jnp.transpose(populations, (1, 2, 0, 3))
    whole_shape = state.shape
    flat_shape = (whole_shape[0] * whole_shape[1], Q, CELLS)
    streamer = partial(stream_all, face_source=face_source, face_level=face_level, face_quadrant=face_quadrant)

    def collide_one(block):
        return collide_forward(block, w_in, w_mid, w_out)[0]

    def pull_one(pair):
        block, upstream = pair
        collided, inputs_bf, layers = collide_forward(block, w_in, w_mid, w_out)
        return collide_backward(upstream, inputs_bf, layers, w_in, w_mid, w_out)
    history = []
    for step_id in range(STEPS):
        history.append(state)
        collided = lax.map(collide_one, state.reshape(flat_shape)).reshape(whole_shape)
        state = streamer(collided)
    final_state = state
    state_bar = jnp.transpose(cotangent, (1, 2, 0, 3))
    total_in = jnp.zeros((HID, Q), jnp.float32)
    total_mid = jnp.zeros((MIDS, HID, HID), jnp.float32)
    total_out = jnp.zeros((Q, HID), jnp.float32)
    for step_id in reversed(range(STEPS)):
        earlier_state = history[step_id]
        collided = lax.map(collide_one, earlier_state.reshape(flat_shape)).reshape(whole_shape)
        unused, stream_pull = jax.vjp(streamer, collided)
        collided_bar, = stream_pull(state_bar)
        flat_bar, part_in, part_mid, part_out = lax.map(pull_one, (earlier_state.reshape(flat_shape), collided_bar.reshape(flat_shape)))
        state_bar = flat_bar.reshape(whole_shape)
        total_in = total_in + lax.optimization_barrier(jnp.sum(part_in, axis=0))
        total_mid = total_mid + lax.optimization_barrier(jnp.sum(part_mid, axis=0))
        total_out = total_out + lax.optimization_barrier(jnp.sum(part_out, axis=0))
    grad_scale = float(CELLS_ALL) ** (-0.5)
    return (jnp.transpose(final_state, (2, 0, 1, 3)), jnp.transpose(state_bar, (2, 0, 1, 3)), total_in * grad_scale, total_mid * grad_scale, total_out * grad_scale)
```

```python
from functools import partial

import jax
import jax.numpy as jnp
from jax import lax
from jax.experimental import pallas as pl
from jax.experimental.pallas import tpu as pltpu
from jax.sharding import PartitionSpec as P

Q = 19
HID = 512
CELLS = 4096
ROWS = 32
CHUNK = 1024
TILES = CHUNK // 128
STEPS_GRID = CELLS // CHUNK
NB = 32
NZ = 4
AXES = ("blocks", "slab")
F32 = jnp.float32
BF16 = jnp.bfloat16
PIECE = 72
GROWS = 32 * PIECE
OUT_AT = 4 * HID
IN_AT = OUT_AT + 4 * 24

VELOCITIES = [
    (0, 0, 0),
    (1, 0, 0),
    (-1, 0, 0),
    (0, 1, 0),
    (0, -1, 0),
    (0, 0, 1),
    (0, 0, -1),
    (1, 1, 0),
    (-1, -1, 0),
    (1, -1, 0),
    (-1, 1, 0),
    (1, 0, 1),
    (-1, 0, -1),
    (1, 0, -1),
    (-1, 0, 1),
    (0, 1, 1),
    (0, -1, -1),
    (0, 1, -1),
    (0, -1, 1),
]
OPPOSITE = [0, 2, 1, 4, 3, 6, 5, 8, 7, 10, 9, 12, 11, 14, 13, 16, 15, 18, 17]


def members(face):
    sign = 1 if face % 2 == 0 else -1
    return [q for q in range(Q) if VELOCITIES[q][face // 2] == sign]


def iota(rows, dim):
    return lax.broadcasted_iota(jnp.int32, (rows, 128), dim)


def roll(value, shift, axis):
    shift %= value.shape[axis]
    return value if shift == 0 else pltpu.roll(value, shift, axis)


def shifted(v, velocity):
    cx, cy, cz = velocity
    lane = iota(ROWS, 1)
    if cz:
        v = jnp.where(lane & 15 == (0 if cz == 1 else 15), roll(v, -15 * cz, 1), roll(v, cz, 1))
    if cy:
        t = roll(v, 16 * cy, 1)
        swapped = jnp.where(iota(ROWS, 0) & 1 == 1, roll(t, 1, 0), roll(t, -1, 0))
        v = jnp.where(lane >> 4 == (0 if cy == 1 else 7), swapped, t)
    if cx:
        v = roll(v, 2 * cx, 0)
    return v


def corner(q):
    row, lane = iota(ROWS, 0), iota(ROWS, 1)
    coords = [row >> 1, (row & 1) * 8 + (lane >> 4), lane & 15]
    mask = None
    for axis in range(3):
        c = VELOCITIES[q][axis]
        if c:
            here = coords[axis] == (0 if c == 1 else 15)
            mask = here if mask is None else mask & here
    return mask


def is_edge(q):
    return sum(abs(c) for c in VELOCITIES[q]) == 2


def pack_faces(src, put_x, put_y, put_z):
    lane16, lane32 = iota(16, 1), iota(ROWS, 1)
    for f in (0, 1):
        for i, q in enumerate(members(f)):
            for r in (0, 1):
                put_x(f, r, i, src[q, pl.ds((30 if f == 0 else 0) + r, 1), :])
    for f in (2, 3):
        acc = jnp.zeros((16, 128), F32)
        for i, q in enumerate(members(f)):
            v = src[q, pl.ds(1 if f == 2 else 0, 16, stride=2), :]
            v = roll(v, 16 * i - (112 if f == 2 else 0), 1)
            acc = jnp.where(lane16 >> 4 == i, v, acc)
        put_y(f - 2, acc)
    acc = jnp.zeros((ROWS, 128), F32)
    for f in (4, 5):
        for i, q in enumerate(members(f)):
            slot = i if f == 4 else 8 + i
            v = roll(src[q], slot - (15 if f == 4 else 0), 1)
            acc = jnp.where(lane32 & 15 == slot, v, acc)
    put_z(acc)


def unpack_faces(dst, get_x, y_ref, z, add):
    lane16, lane32 = iota(16, 1), iota(ROWS, 1)
    for f in (0, 1):
        for i, q in enumerate(members(f)):
            for r in (0, 1):
                at = pl.ds((30 if f == 0 else 0) + r, 1)
                v = get_x(f, r, i)
                dst[q, at, :] = dst[q, at, :] + v if add else v
    for f in (2, 3):
        packed = y_ref[f - 2]
        for i, q in enumerate(members(f)):
            at = pl.ds(1 if f == 2 else 0, 16, stride=2)
            v = roll(packed, (112 if f == 2 else 0) - 16 * i, 1)
            old = dst[q, at, :]
            new = old + v if add else v
            dst[q, at, :] = jnp.where(lane16 >> 4 == (7 if f == 2 else 0), new, old)
    for f in (4, 5):
        for i, q in enumerate(members(f)):
            v = roll(z, 15 - i if f == 4 else -(8 + i), 1)
            old = dst[q]
            new = old + v if add else v
            dst[q] = jnp.where(lane32 & 15 == (15 if f == 4 else 0), new, old)


def picked(value, index):
    return jnp.take_along_axis(value, index, axis=1)


def level_of(info, f):
    return info[0, 2 + (f ^ 1)] == 1


def quadrant_of(info, f):
    r = info[0, 8 + (f ^ 1)]
    return r >> 1, r & 1


def refine_x(info, x):
    lane = iota(8, 1)
    for f in (0, 1):
        fine = level_of(info, f)
        qr, qc = quadrant_of(info, f)
        rows = [x[f, 0], x[f, 1]]
        source = jnp.where(qr == 0, rows[0], rows[1])
        for r in (0, 1):
            index = (r * 4 + (lane >> 5)) * 16 + qc * 8 + ((lane & 15) >> 1)
            x[f, r] = jnp.where(fine, picked(source, index), rows[r])


def refine_y(info, y):
    lane = iota(8, 1)
    for f in (2, 3):
        fine = level_of(info, f)
        qr, qc = quadrant_of(info, f)
        whole = y[f - 2]
        source = jnp.where(qr == 0, whole[:8], whole[8:])
        v = picked(source, (lane >> 4) * 16 + qc * 8 + ((lane & 15) >> 1))
        for d in (0, 1):
            at = pl.ds(d, 8, stride=2)
            y[f - 2, at, :] = jnp.where(fine, v, y[f - 2, at, :])


def refine_z(info, z_two):
    lane = iota(8, 1)
    for f in (4, 5):
        z = z_two.at[f - 4]
        fine = level_of(info, f)
        qr, qc = quadrant_of(info, f)
        parts = {(h, p): z[pl.ds(16 * h + p, 8, stride=2), :] for h in (0, 1) for p in (0, 1)}
        halves = [jnp.where(qc == 0, parts[h, 0], parts[h, 1]) for h in (0, 1)]
        source = jnp.where(qr == 0, halves[0], halves[1])
        for p in (0, 1):
            v = picked(source, (p * 4 + (lane >> 5)) * 16 + (lane & 15))
            for d in (0, 1):
                at = pl.ds(2 * d + p, 8, stride=4)
                z[at, :] = jnp.where(fine, v, z[at, :])
    return jnp.where(iota(ROWS, 1) & 15 < 8, z_two[0], z_two[1])


def gather_x(info, x):
    lane = iota(8, 1)
    index = (2 * ((lane >> 4) & 3)) * 16 + 2 * (lane & 7)
    for f in (0, 1):
        fine = level_of(info, f)
        qr, qc = quadrant_of(info, f)
        rows = [x[f, 0], x[f, 1]]
        sums = []
        for v in rows:
            v = v + roll(v, -1, 1)
            v = v + roll(v, -16, 1)
            sums.append(picked(v, index))
        v = jnp.where(lane < 64, sums[0], sums[1])
        v = jnp.where((lane & 15) >> 3 == qc, v, 0.0)
        for r in (0, 1):
            x[f, r] = jnp.where(fine, jnp.where(qr == r, v, 0.0), rows[r])


def gather_y(info, y):
    lane = iota(8, 1)
    index = (lane >> 4) * 16 + 2 * (lane & 7)
    for f in (2, 3):
        fine = level_of(info, f)
        qr, qc = quadrant_of(info, f)
        v = y[f - 2, pl.ds(0, 8, stride=2), :] + y[f - 2, pl.ds(1, 8, stride=2), :]
        v = picked(v + roll(v, -1, 1), index)
        v = jnp.where((lane & 15) >> 3 == qc, v, 0.0)
        for h in (0, 1):
            at = pl.ds(8 * h, 8)
            y[f - 2, at, :] = jnp.where(fine, jnp.where(qr == h, v, 0.0), y[f - 2, at, :])


def gather_z(info, z_two):
    lane = iota(8, 1)
    index = (2 * ((lane >> 4) & 3)) * 16 + (lane & 15)
    for f in (4, 5):
        z = z_two.at[f - 4]
        fine = level_of(info, f)
        qr, qc = quadrant_of(info, f)
        sums = []
        for p in (0, 1):
            v = z[pl.ds(p, 8, stride=4), :] + z[pl.ds(2 + p, 8, stride=4), :]
            sums.append(picked(v + roll(v, -16, 1), index))
        v = jnp.where(lane < 64, sums[0], sums[1])
        for h in (0, 1):
            for p in (0, 1):
                at = pl.ds(16 * h + p, 8, stride=2)
                here = (qr == h) & (qc == p)
                z[at, :] = jnp.where(fine, jnp.where(here, v, 0.0), z[at, :])
    return jnp.where(iota(ROWS, 1) & 15 < 8, z_two[0], z_two[1])


def choose_x(info, face, pieces, kind):
    d = info[0, face]
    even = info[0, 14] == 0
    outer1, outer3 = jnp.where(even, NB - 1, 1), jnp.where(even, NB - 3, 3)
    inner1, inner3 = jnp.where(even, 1, NB - 1), jnp.where(even, 3, NB - 3)
    spots = [inner1, outer1, NB - 2, 2, inner3, outer3]
    return lambda f, r: sum_where(
        [(d == spot, piece[kind * 4 + f * 2 + r]) for spot, piece in zip(spots, pieces)]
    )


def sum_where(cases):
    total = jnp.zeros((8, 128), F32)
    for condition, value in cases:
        total = jnp.where(condition, value, total)
    return total


def stream_back(info, bar, local, xs, xys, zs, work, y_two, z_two):
    for q in range(Q):
        v = bar[q]
        if is_edge(q):
            v = jnp.where(corner(q), 0.0, v)
        work[q] = shifted(v, tuple(-c for c in VELOCITIES[q]))
    x_four = xs.at[1]
    x_four[...] = jnp.zeros(x_four.shape, F32)

    def put_x(f, r, i, v):
        x_four[f, r, pl.ds(i, 1), :] = v

    def put_y(f, v):
        y_two[f] = v

    def put_z(v):
        z_two[0] = v
        z_two[1] = v

    pack_faces(work, put_x, put_y, put_z)
    gather_x(info, x_four)
    gather_y(info, y_two)
    zs[1] = gather_z(info, z_two)
    xys[pl.ds(32, 32), :] = xs[1].reshape(32, 128)
    xys[pl.ds(96, 32), :] = y_two[...].reshape(32, 128)
    row, lane = iota(ROWS, 0), iota(ROWS, 1)
    coords = [row >> 1, (row & 1) * 8 + (lane >> 4), lane & 15]
    for q in range(Q):
        v = work[q]
        leaving = None
        for axis in range(3):
            c = VELOCITIES[q][axis]
            if c:
                here = coords[axis] == (15 if c == 1 else 0)
                leaving = here if leaving is None else leaving | here
        if leaving is not None:
            v = jnp.where(leaving, 0.0, v)
        if is_edge(q):
            v = v + jnp.where(corner(OPPOSITE[q]), bar[OPPOSITE[q]], 0.0)
        local[q] = v


def send_post(post, xs, xys, zs):
    x_four = xs.at[0]
    x_four[...] = jnp.zeros(x_four.shape, F32)

    def put_x(f, r, i, v):
        x_four[f, r, pl.ds(i, 1), :] = v

    def put_y(f, v):
        xys[pl.ds(64 + 16 * f, 16), :] = v

    def put_z(v):
        zs[0] = v

    pack_faces(post, put_x, put_y, put_z)
    xys[pl.ds(0, 32), :] = xs[0].reshape(32, 128)


def stream(info, post, pieces, both, below, above, out, work, x_four, y_two, z_two):
    heads = [both.at[pl.ds(0, 64)]] + list(pieces)
    for f in (0, 1):
        pick = choose_x(info, f ^ 1, [Rows(h) for h in heads], 0)
        for r in (0, 1):
            x_four[f, r] = pick(f, r)
    refine_x(info, x_four)
    y_two[0] = both[pl.ds(64, 16), :]
    y_two[1] = both[pl.ds(80, 16), :]
    refine_y(info, y_two)
    z_two[0] = below[0]
    z_two[1] = above[0]
    z = refine_z(info, z_two)
    work[...] = post[...]
    unpack_faces(work, lambda f, r, i: x_four[f, r, pl.ds(i, 1), :], y_two, z, False)
    for q in range(Q):
        v = shifted(work[q], VELOCITIES[q])
        if is_edge(q):
            v = jnp.where(corner(q), post[OPPOSITE[q]], v)
        out[q] = v


class Rows:
    def __init__(self, ref):
        self.ref = ref

    def __getitem__(self, i):
        return self.ref[pl.ds(8 * i, 8), :]


def take_back(info, bar, pieces, both, below, above, x_four, y_two):
    heads = [both.at[pl.ds(0, 64)]] + list(pieces)
    for f in (0, 1):
        pick = choose_x(info, f, [Rows(h) for h in heads], 1)
        for r in (0, 1):
            x_four[f, r] = pick(f, r)
    y_two[0] = both[pl.ds(96, 16), :]
    y_two[1] = both[pl.ds(112, 16), :]
    z = jnp.where(iota(ROWS, 1) & 15 < 8, above[1], below[1])
    unpack_faces(bar, lambda f, r, i: x_four[f, r, pl.ds(i, 1), :], y_two, z, True)


def dot(a, b, ca=1, cb=0):
    return lax.dot_general(a, b, (((ca,), (cb,)), ((), ())), preferred_element_type=F32)


def cells_of(ref, step):
    parts = [
        ref[:, pl.ds(step * TILES + j, 1), :].reshape(Q, 128) for j in range(TILES)
    ]
    return jnp.concatenate(parts, axis=1)


def put_cells(ref, step, value):
    for j in range(TILES):
        ref[:, pl.ds(step * TILES + j, 1), :] = value[:, j * 128 : (j + 1) * 128].reshape(Q, 1, 128)


def forward(x, w_in_t, w_mid, w_out):
    xb = x.astype(BF16)
    h0 = jnp.tanh(dot(w_in_t, xb, 0, 0)).astype(BF16)
    h1 = jnp.tanh(dot(w_mid, h0)).astype(BF16)
    return xb, h0, h1, x + dot(w_out, h1)


def slope(h):
    h = h.astype(F32)
    return 1.0 - h * h


def backward(pbar, xb, h0, h1, w_in_t, w_mid_t, w_out):
    e = pbar.astype(BF16)
    g_out = dot(e, h1, 1, 1)
    a1 = (dot(w_out, e, 0, 0) * slope(h1)).astype(BF16)
    g_mid = dot(a1, h0, 1, 1)
    a0 = (dot(w_mid_t, a1) * slope(h0)).astype(BF16)
    g_in = dot(xb, a0, 1, 1)
    return pbar + dot(w_in_t, a0), g_in, g_mid, g_out


def add_grads(grads, g_in, g_mid, g_out, first):
    def put(at, rows, value):
        for j in range(4):
            spot = pl.ds(at + j * (HID if rows == HID else 24), rows)
            v = value[:, j * 128 : (j + 1) * 128]
            grads[spot, :] = v if first is None else grads[spot, :] + v

    put(0, HID, g_mid)
    put(OUT_AT, Q, g_out)
    put(IN_AT, Q, g_in)


def first_kernel(info, f0, cot, w_in_t, w_mid, w_out, post, local, xs, xys, zs, h0_out, h1_out,
                 work, y_two, z_two):
    step = pl.program_id(0)

    @pl.when(step == 0)
    def _():
        stream_back(info, cot, local, xs, xys, zs, work, y_two, z_two)

    xb, h0, h1, out = forward(cells_of(f0, step), w_in_t[...], w_mid[...], w_out[...])
    h0_out[...] = h0
    h1_out[...] = h1
    put_cells(post, step, out)

    @pl.when(step == STEPS_GRID - 1)
    def _():
        send_post(post, xs, xys, zs)


def second_kernel(info, post1, local2, p1, p2, p3, p4, p5, both, below, above, w_in_t, w_mid,
                  w_mid_t, w_out, post, local, xs, xys, zs, grads,
                  f1, pbar, fbar, work, x_four, y_two, z_two):
    step = pl.program_id(0)
    pieces = [p1, p2, p3, p4, p5]

    @pl.when(step == 0)
    def _():
        stream(info, post1, pieces, both, below, above, f1, work, x_four, y_two, z_two)
        pbar[...] = local2[...]
        take_back(info, pbar, pieces, both, below, above, x_four, y_two)
        grads[...] = jnp.zeros(grads.shape, F32)

    xb, h0, h1, out = forward(cells_of(f1, step), w_in_t[...], w_mid[...], w_out[...])
    put_cells(post, step, out)
    bar, g_in, g_mid, g_out = backward(
        cells_of(pbar, step), xb, h0, h1, w_in_t[...], w_mid_t[...], w_out[...]
    )
    put_cells(fbar, step, bar)
    add_grads(grads, g_in, g_mid, g_out, False)

    @pl.when(step == STEPS_GRID - 1)
    def _():
        send_post(post, xs, xys, zs)
        stream_back(info, fbar, local, xs, xys, zs, work, y_two, z_two)


def third_kernel(info, f0, local1, p1, p2, p3, p4, p5, both, below, above, w_in_t, w_mid_t, w_out,
                 grads2, h0_in, h1_in, fbar, grads, pbar, x_four, y_two):
    step = pl.program_id(0)

    @pl.when(step == 0)
    def _():
        pbar[...] = local1[...]
        take_back(info, pbar, [p1, p2, p3, p4, p5], both, below, above, x_four, y_two)
        grads[...] = grads2[...]

    bar, g_in, g_mid, g_out = backward(
        cells_of(pbar, step), cells_of(f0, step).astype(BF16), h0_in[...], h1_in[...],
        w_in_t[...], w_mid_t[...], w_out[...],
    )
    put_cells(fbar, step, bar)
    add_grads(grads, g_in, g_mid, g_out, False)


def final_kernel(info, post2, p1, p2, p3, p4, p5, both, below, above, out, work, x_four, y_two,
                 z_two):
    stream(info, post2, [p1, p2, p3, p4, p5], both, below, above, out, work, x_four, y_two, z_two)


def unpack_kernel(whole, g_in, g_mid, g_out):
    scale = float(NB * NZ * CELLS) ** -0.5
    for j in range(4):
        cols = pl.ds(j * 128, 128)
        g_mid[:, cols] = whole[pl.ds(j * HID, HID), :] * scale
        g_out[:, cols] = whole[pl.ds(OUT_AT + 24 * j, Q), :] * scale
        g_in[:, cols] = whole[pl.ds(IN_AT + 24 * j, Q), :] * scale


def vmem(shape, dtype=F32):
    return pltpu.VMEM(shape, dtype)


BLOCK = (Q, ROWS, 128)
SENDS = [
    jax.ShapeDtypeStruct((2, 2, 2, 8, 128), F32),
    jax.ShapeDtypeStruct((128, 128), F32),
    jax.ShapeDtypeStruct((2, ROWS, 128), F32),
]


def run(kernel, args, outs, scratch, grid=None, windows=(), flops=0, out_windows=()):
    spec_kw = dict(memory_space=pltpu.VMEM)

    def spec(shape, windowed):
        if grid is None:
            return pl.BlockSpec(memory_space=pltpu.VMEM)
        if windowed:
            return pl.BlockSpec((shape[0], CHUNK), lambda c: (0, c))
        zeros = (0,) * len(shape)
        return pl.BlockSpec(shape, lambda c: zeros)

    in_specs = [pl.BlockSpec(memory_space=pltpu.SMEM)] if args[0].dtype == jnp.int32 else [
        spec(args[0].shape, False)
    ]
    in_specs += [spec(a.shape, i + 1 in windows) for i, a in enumerate(args[1:])]
    out_specs = [spec(o.shape, i in out_windows) for i, o in enumerate(outs)]
    kw = {} if grid is None else {"grid": grid}
    return pl.pallas_call(
        kernel,
        out_shape=outs,
        in_specs=in_specs,
        out_specs=out_specs,
        scratch_shapes=scratch,
        compiler_params=pltpu.CompilerParams(vmem_limit_bytes=48 * 1024 * 1024),
        cost_estimate=pl.CostEstimate(flops=flops, bytes_accessed=1 << 20, transcendentals=0),
        **kw,
    )(*args)


def send(value, target):
    pairs = [
        (b * NZ + z, nb * NZ + nz)
        for b in range(NB)
        for z in range(NZ)
        for nb, nz in [target(b, z)]
    ]
    return lax.ppermute(value, AXES, pairs)


def exchange(xs, xys, zs):
    x = xs.reshape(64, 128)

    def to(even, odd):
        return lambda b, z: ((b + (even if b % 2 == 0 else odd)) % NB, z)

    both = send(xys, to(1, -1))
    pieces = [
        send(x, to(-1, 1)),
        send(x, to(2, 2)),
        send(x, to(-2, -2)),
        send(x, to(3, -3)),
        send(x, to(-3, 3)),
    ]
    below = send(zs, lambda b, z: (b, (z + 1) % NZ))
    above = send(zs, lambda b, z: (b, (z - 1) % NZ))
    return (*pieces, both, below, above)


def along(axes, d):
    def target(b, z):
        coords = {"x": b // 8, "y": b // 2 % 4, "c": b % 2, "z": z}
        axis = axes[coords["c"]]
        coords[axis] = (coords[axis] + d) % 4
        return coords["x"] * 8 + coords["y"] * 2 + coords["c"], coords["z"]

    return target


ORDER = [("z", "x"), ("y", "y"), ("x", "z")]


def total_over_devices(grads):
    b, z = lax.axis_index("blocks"), lax.axis_index("slab")
    core = b % 2
    coords = {"x": b // 8, "y": b // 2 % 4, "z": z}
    places = [jnp.where(core == 0, coords[a0], coords[a1]) for a0, a1 in ORDER]

    def take(parts, i):
        return lax.dynamic_index_in_dim(parts, i, 0, keepdims=False)

    swap = lambda b, z: (b ^ 1, z)
    halves = grads.reshape(2, GROWS // 2, 128)
    part = take(halves, core) + send(take(halves, 1 - core), swap)
    for level in (0, 1):
        i = places[level]
        quarters = part.reshape(4, -1, 128)
        got = [
            send(take(quarters, (i + d) % 4), along(ORDER[level], d)) for d in (1, 2, 3)
        ]
        part = take(quarters, i) + got[0] + got[1] + got[2]
    got = [send(part, along(ORDER[2], d)) for d in (1, 2, 3)]
    part = part + got[0] + got[1] + got[2]
    for level in (1, 0):
        i = places[level]
        got = [part] + [send(part, along(ORDER[level], d)) for d in (1, 2, 3)]
        stacked = jnp.stack(got)
        order = (i - jnp.arange(4)) % 4
        part = jnp.concatenate([take(stacked, order[k]) for k in range(4)])
    other = send(part, swap)
    first = jnp.where(core == 0, part, other)
    last = jnp.where(core == 0, other, part)
    return jnp.concatenate([first, last])


def shards(populations, w_in, w_mid, w_out, cotangent, face_source, face_level, face_quadrant):
    f0 = populations.reshape(BLOCK)
    cot = cotangent.reshape(BLOCK)
    w_in_t = w_in.T
    w_mid = w_mid[0]
    w_mid_t = w_mid.T
    position = lax.axis_index("blocks")
    near = lax.dynamic_index_in_dim(face_source, position, 0, keepdims=False)[:2]
    distance = (near - position + NB) % NB
    info = jnp.concatenate(
        [distance, face_level[0, 0], face_quadrant[0, 0], jnp.stack([position % 2, position])]
    )[None]
    block = jax.ShapeDtypeStruct(BLOCK, F32)
    hidden = jax.ShapeDtypeStruct((HID, CELLS), BF16)
    grad = jax.ShapeDtypeStruct((GROWS, 128), F32)
    big = 2 * HID * HID * CELLS
    faces = [vmem((2, 2, 8, 128)), vmem((2, 16, 128)), vmem((2, ROWS, 128))]
    grid = (STEPS_GRID,)

    post1, local2, *sends, h0, h1 = run(
        first_kernel, [info, f0, cot, w_in_t, w_mid, w_out], [block, block, *SENDS, hidden, hidden],
        [vmem(BLOCK), *faces[1:]], grid, (), big, (5, 6),
    )
    got = exchange(*sends)
    post2, local1, *sends, grads2 = run(
        second_kernel, [info, post1, local2, *got, w_in_t, w_mid, w_mid_t, w_out],
        [block, block, *SENDS, grad], [vmem(BLOCK)] * 4 + faces, grid, (), 3 * big,
    )
    got = exchange(*sends)
    fbar0, grads = run(
        third_kernel,
        [info, f0, local1, *got, w_in_t, w_mid_t, w_out, grads2, h0, h1],
        [block, grad], [vmem(BLOCK), *faces[:2]], grid, (15, 16), 2 * big,
    )
    post2, grads = lax.optimization_barrier((post2, grads))
    (final,) = run(final_kernel, [info, post2, *got], [block], [vmem(BLOCK), *faces], None, (), 1 << 20)
    whole = total_over_devices(grads)
    g_in, g_mid, g_out = run(
        unpack_kernel, [whole],
        [jax.ShapeDtypeStruct(s, F32) for s in ((Q, HID), (HID, HID), (Q, HID))], [],
    )
    place = (Q, 1, 1, CELLS)
    return final.reshape(place), fbar0.reshape(place), g_in.T, g_mid[None], g_out


def solution(mesh):
    cells = P(None, "slab", "blocks", None)
    local = P("slab", "blocks", None)
    return jax.shard_map(
        shards,
        mesh=mesh,
        in_specs=(cells, P(), P(), P(), cells, P(), local, local),
        out_specs=(cells, cells, P(), P(), P()),
        check_vma=False,
    )
```

```python
import jax
import jax.numpy as jnp
from jax import lax
from jax.experimental import pallas as pl
from jax.experimental.pallas import tpu as pltpu
from jax.sharding import Mesh
from jax.sharding import PartitionSpec as P

Q = 19
HID = 512
CELLS = 4096
ROWS = 32
CHUNK = 1024
TILES = CHUNK // 128
CHUNKS = CELLS // CHUNK
NB = 32
NZ = 4
NX = 4
BLOCKS = ("bx", "by", "core")
AXES = ("bx", "by", "core", "slab")
CHIPS = ("bx", "by", "slab")
F32 = jnp.float32
BF16 = jnp.bfloat16
VMEM_LIMIT = 32 * 1024 * 1024
GROWS = 2304
HALF = GROWS // 2
OUT_AT = 4 * HID
IN_AT = OUT_AT + 4 * 24

VELOCITIES = [
    (0, 0, 0),
    (1, 0, 0),
    (-1, 0, 0),
    (0, 1, 0),
    (0, -1, 0),
    (0, 0, 1),
    (0, 0, -1),
    (1, 1, 0),
    (-1, -1, 0),
    (1, -1, 0),
    (-1, 1, 0),
    (1, 0, 1),
    (-1, 0, -1),
    (1, 0, -1),
    (-1, 0, 1),
    (0, 1, 1),
    (0, -1, -1),
    (0, 1, -1),
    (0, -1, 1),
]
OPPOSITE = [0, 2, 1, 4, 3, 6, 5, 8, 7, 10, 9, 12, 11, 14, 13, 16, 15, 18, 17]


def members(face):
    sign = 1 if face % 2 == 0 else -1
    return [q for q in range(Q) if VELOCITIES[q][face // 2] == sign]


def iota(rows, dim):
    return lax.broadcasted_iota(jnp.int32, (rows, 128), dim)


def roll(value, shift, axis):
    shift %= value.shape[axis]
    return value if shift == 0 else pltpu.roll(value, shift, axis)


def shifted(v, velocity):
    cx, cy, cz = velocity
    lane = iota(ROWS, 1)
    if cz:
        v = jnp.where(lane & 15 == (0 if cz == 1 else 15), roll(v, -15 * cz, 1), roll(v, cz, 1))
    if cy:
        t = roll(v, 16 * cy, 1)
        swapped = jnp.where(iota(ROWS, 0) & 1 == 1, roll(t, 1, 0), roll(t, -1, 0))
        v = jnp.where(lane >> 4 == (0 if cy == 1 else 7), swapped, t)
    if cx:
        v = roll(v, 2 * cx, 0)
    return v


def corner(q):
    row, lane = iota(ROWS, 0), iota(ROWS, 1)
    coords = [row >> 1, (row & 1) * 8 + (lane >> 4), lane & 15]
    mask = None
    for axis in range(3):
        c = VELOCITIES[q][axis]
        if c:
            here = coords[axis] == (0 if c == 1 else 15)
            mask = here if mask is None else mask & here
    return mask


def is_edge(q):
    return sum(abs(c) for c in VELOCITIES[q]) == 2


def pack_faces(src, put_x, put_y, put_z):
    lane16, lane32 = iota(16, 1), iota(ROWS, 1)
    for f in (0, 1):
        for i, q in enumerate(members(f)):
            for r in (0, 1):
                put_x(f, r, i, src[q, pl.ds((30 if f == 0 else 0) + r, 1), :])
    for f in (2, 3):
        acc = jnp.zeros((16, 128), F32)
        for i, q in enumerate(members(f)):
            v = src[q, pl.ds(1 if f == 2 else 0, 16, stride=2), :]
            v = roll(v, 16 * i - (112 if f == 2 else 0), 1)
            acc = jnp.where(lane16 >> 4 == i, v, acc)
        put_y(f - 2, acc)
    acc = jnp.zeros((ROWS, 128), F32)
    for f in (4, 5):
        for i, q in enumerate(members(f)):
            slot = i if f == 4 else 8 + i
            v = roll(src[q], slot - (15 if f == 4 else 0), 1)
            acc = jnp.where(lane32 & 15 == slot, v, acc)
    put_z(acc)


def unpack_faces(dst, get_x, y_ref, z, add):
    lane16, lane32 = iota(16, 1), iota(ROWS, 1)
    for f in (0, 1):
        for i, q in enumerate(members(f)):
            for r in (0, 1):
                at = pl.ds((30 if f == 0 else 0) + r, 1)
                v = get_x(f, r, i)
                dst[q, at, :] = dst[q, at, :] + v if add else v
    for f in (2, 3):
        packed = y_ref[f - 2]
        for i, q in enumerate(members(f)):
            at = pl.ds(1 if f == 2 else 0, 16, stride=2)
            v = roll(packed, (112 if f == 2 else 0) - 16 * i, 1)
            old = dst[q, at, :]
            new = old + v if add else v
            dst[q, at, :] = jnp.where(lane16 >> 4 == (7 if f == 2 else 0), new, old)
    for f in (4, 5):
        for i, q in enumerate(members(f)):
            v = roll(z, 15 - i if f == 4 else -(8 + i), 1)
            old = dst[q]
            new = old + v if add else v
            dst[q] = jnp.where(lane32 & 15 == (15 if f == 4 else 0), new, old)


def picked(value, index):
    return jnp.take_along_axis(value, index, axis=1)


class Tables:
    def __init__(self, place, source, level, quadrant):
        self.place, self.source, self.level, self.quadrant = place, source, level, quadrant

    def block(self):
        return self.place[0]

    def distance(self, face):
        d = self.source[face, self.block()] - self.block()
        return jnp.where(d < 0, d + NB, d)


def level_of(info, f):
    return info.level[0, f ^ 1] == 1


def quadrant_of(info, f):
    r = info.quadrant[0, f ^ 1]
    return r >> 1, r & 1


def refine_x(info, x):
    lane = iota(8, 1)
    for f in (0, 1):
        fine = level_of(info, f)
        qr, qc = quadrant_of(info, f)
        rows = [x[f, 0], x[f, 1]]
        source = jnp.where(qr == 0, rows[0], rows[1])
        for r in (0, 1):
            index = (r * 4 + (lane >> 5)) * 16 + qc * 8 + ((lane & 15) >> 1)
            x[f, r] = jnp.where(fine, picked(source, index), rows[r])


def refine_y(info, y):
    lane = iota(8, 1)
    for f in (2, 3):
        fine = level_of(info, f)
        qr, qc = quadrant_of(info, f)
        whole = y[f - 2]
        source = jnp.where(qr == 0, whole[:8], whole[8:])
        v = picked(source, (lane >> 4) * 16 + qc * 8 + ((lane & 15) >> 1))
        for d in (0, 1):
            at = pl.ds(d, 8, stride=2)
            y[f - 2, at, :] = jnp.where(fine, v, y[f - 2, at, :])


def refine_z(info, z_two):
    lane = iota(8, 1)
    for f in (4, 5):
        z = z_two.at[f - 4]
        fine = level_of(info, f)
        qr, qc = quadrant_of(info, f)
        parts = {(h, p): z[pl.ds(16 * h + p, 8, stride=2), :] for h in (0, 1) for p in (0, 1)}
        halves = [jnp.where(qc == 0, parts[h, 0], parts[h, 1]) for h in (0, 1)]
        source = jnp.where(qr == 0, halves[0], halves[1])
        for p in (0, 1):
            v = picked(source, (p * 4 + (lane >> 5)) * 16 + (lane & 15))
            for d in (0, 1):
                at = pl.ds(2 * d + p, 8, stride=4)
                z[at, :] = jnp.where(fine, v, z[at, :])
    return jnp.where(iota(ROWS, 1) & 15 < 8, z_two[0], z_two[1])


def gather_x(info, x):
    lane = iota(8, 1)
    index = (2 * ((lane >> 4) & 3)) * 16 + 2 * (lane & 7)
    for f in (0, 1):
        fine = level_of(info, f)
        qr, qc = quadrant_of(info, f)
        rows = [x[f, 0], x[f, 1]]
        sums = []
        for v in rows:
            v = v + roll(v, -1, 1)
            v = v + roll(v, -16, 1)
            sums.append(picked(v, index))
        v = jnp.where(lane < 64, sums[0], sums[1])
        v = jnp.where((lane & 15) >> 3 == qc, v, 0.0)
        for r in (0, 1):
            x[f, r] = jnp.where(fine, jnp.where(qr == r, v, 0.0), rows[r])


def gather_y(info, y):
    lane = iota(8, 1)
    index = (lane >> 4) * 16 + 2 * (lane & 7)
    for f in (2, 3):
        fine = level_of(info, f)
        qr, qc = quadrant_of(info, f)
        v = y[f - 2, pl.ds(0, 8, stride=2), :] + y[f - 2, pl.ds(1, 8, stride=2), :]
        v = picked(v + roll(v, -1, 1), index)
        v = jnp.where((lane & 15) >> 3 == qc, v, 0.0)
        for h in (0, 1):
            at = pl.ds(8 * h, 8)
            y[f - 2, at, :] = jnp.where(fine, jnp.where(qr == h, v, 0.0), y[f - 2, at, :])


def gather_z(info, z_two):
    lane = iota(8, 1)
    index = (2 * ((lane >> 4) & 3)) * 16 + (lane & 15)
    for f in (4, 5):
        z = z_two.at[f - 4]
        fine = level_of(info, f)
        qr, qc = quadrant_of(info, f)
        sums = []
        for p in (0, 1):
            v = z[pl.ds(p, 8, stride=4), :] + z[pl.ds(2 + p, 8, stride=4), :]
            sums.append(picked(v + roll(v, -16, 1), index))
        v = jnp.where(lane < 64, sums[0], sums[1])
        for h in (0, 1):
            for p in (0, 1):
                at = pl.ds(16 * h + p, 8, stride=2)
                here = (qr == h) & (qc == p)
                z[at, :] = jnp.where(fine, jnp.where(here, v, 0.0), z[at, :])
    return jnp.where(iota(ROWS, 1) & 15 < 8, z_two[0], z_two[1])


def choose_x(info, face, both, low, high, far, kind):
    d = info.distance(face)
    even = info.block() & 1 == 0
    cases = [
        (jnp.where(even, 1, NB - 1), both, 0),
        (NB - 2, low, 0),
        (jnp.where(even, NB - 1, NB - 3), low, 64),
        (2, high, 0),
        (jnp.where(even, 3, 1), high, 64),
        (jnp.where(even, NB - 3, 3), far, 0),
    ]
    return lambda f, r: sum_where(
        [
            (d == spot, ref[pl.ds(at + 8 * (kind * 4 + f * 2 + r), 8), :])
            for spot, ref, at in cases
        ]
    )


def sum_where(cases):
    total = jnp.zeros((8, 128), F32)
    for condition, value in cases:
        total = jnp.where(condition, value, total)
    return total


def stream_back(info, bar, local, xs, xys, zs, work, y_two, z_two):
    for q in range(Q):
        v = bar[q]
        if is_edge(q):
            v = jnp.where(corner(q), 0.0, v)
        work[q] = shifted(v, tuple(-c for c in VELOCITIES[q]))
    x_four = xs.at[1]
    x_four[...] = jnp.zeros(x_four.shape, F32)

    def put_x(f, r, i, v):
        x_four[f, r, pl.ds(i, 1), :] = v

    def put_y(f, v):
        y_two[f] = v

    def put_z(v):
        z_two[0] = v
        z_two[1] = v

    pack_faces(work, put_x, put_y, put_z)
    gather_x(info, x_four)
    gather_y(info, y_two)
    zs[1] = gather_z(info, z_two)
    xys[pl.ds(32, 32), :] = xs[1].reshape(32, 128)
    xys[pl.ds(96, 32), :] = y_two[...].reshape(32, 128)
    row, lane = iota(ROWS, 0), iota(ROWS, 1)
    coords = [row >> 1, (row & 1) * 8 + (lane >> 4), lane & 15]
    for q in range(Q):
        v = work[q]
        leaving = None
        for axis in range(3):
            c = VELOCITIES[q][axis]
            if c:
                here = coords[axis] == (15 if c == 1 else 0)
                leaving = here if leaving is None else leaving | here
        if leaving is not None:
            v = jnp.where(leaving, 0.0, v)
        if is_edge(q):
            v = v + jnp.where(corner(OPPOSITE[q]), bar[OPPOSITE[q]], 0.0)
        local[q] = v


def send_post(post, xs, xys, zs):
    x_four = xs.at[0]
    x_four[...] = jnp.zeros(x_four.shape, F32)

    def put_x(f, r, i, v):
        x_four[f, r, pl.ds(i, 1), :] = v

    def put_y(f, v):
        xys[pl.ds(64 + 16 * f, 16), :] = v

    def put_z(v):
        zs[0] = v

    pack_faces(post, put_x, put_y, put_z)
    xys[pl.ds(0, 32), :] = xs[0].reshape(32, 128)


def stream(info, post, got, out, work, x_four, y_two, z_two):
    both, low, high, far, below, above = got
    for f in (0, 1):
        pick = choose_x(info, f ^ 1, both, low, high, far, 0)
        for r in (0, 1):
            x_four[f, r] = pick(f, r)
    refine_x(info, x_four)
    y_two[0] = both[pl.ds(64, 16), :]
    y_two[1] = both[pl.ds(80, 16), :]
    refine_y(info, y_two)
    z_two[0] = below[0]
    z_two[1] = above[0]
    z = refine_z(info, z_two)
    work[...] = post[...]
    unpack_faces(work, lambda f, r, i: x_four[f, r, pl.ds(i, 1), :], y_two, z, False)
    for q in range(Q):
        v = shifted(work[q], VELOCITIES[q])
        if is_edge(q):
            v = jnp.where(corner(q), post[OPPOSITE[q]], v)
        out[q] = v


def take_back(info, bar, got, x_four, y_two):
    both, low, high, far, below, above = got
    for f in (0, 1):
        pick = choose_x(info, f, both, low, high, far, 1)
        for r in (0, 1):
            x_four[f, r] = pick(f, r)
    y_two[0] = both[pl.ds(96, 16), :]
    y_two[1] = both[pl.ds(112, 16), :]
    z = jnp.where(iota(ROWS, 1) & 15 < 8, above[1], below[1])
    unpack_faces(bar, lambda f, r, i: x_four[f, r, pl.ds(i, 1), :], y_two, z, True)


def dot(a, b, ca=1, cb=0):
    return lax.dot_general(a, b, (((ca,), (cb,)), ((), ())), preferred_element_type=F32)


def cells_of(ref, step):
    parts = [
        ref[:, pl.ds(step * TILES + j, 1), :].reshape(Q, 128) for j in range(TILES)
    ]
    return jnp.concatenate(parts, axis=1)


def put_cells(ref, step, value):
    for j in range(TILES):
        ref[:, pl.ds(step * TILES + j, 1), :] = value[:, j * 128 : (j + 1) * 128].reshape(Q, 1, 128)


def span(step):
    return pl.ds(step * CHUNK, CHUNK)


def forward(x, w_in_t, w_mid, w_out):
    xb = x.astype(BF16)
    h0 = jnp.tanh(dot(w_in_t, xb, 0, 0)).astype(BF16)
    h1 = jnp.tanh(dot(w_mid, h0)).astype(BF16)
    return h0, h1, x + dot(w_out, h1)


def slope(h):
    h = h.astype(F32)
    return 1.0 - h * h


def signals(pbar, h0, h1, w_mid_t, w_out):
    e = pbar.astype(BF16)
    a1 = (dot(w_out, e, 0, 0) * slope(h1)).astype(BF16)
    a0 = (dot(w_mid_t, a1) * slope(h0)).astype(BF16)
    return e, a1, a0


class Copies:
    def __init__(self, sems):
        self.sems, self.made = sems, []

    def start(self, source, target):
        copy = pltpu.make_async_copy(source, target, self.sems.at[len(self.made)])
        copy.start()
        self.made.append(copy)
        return copy

    def wait(self):
        for copy in self.made:
            copy.wait()


def put_grads(grads, x, e, h0, h1, a0, a1, more):
    def put(at, rows, value):
        for j in range(4):
            spot = pl.ds(at + j * (HID if rows == HID else 24), rows)
            v = value[:, j * 128 : (j + 1) * 128]
            grads[spot, :] = v if more is None else more[spot, :] + v

    put(0, HID, dot(a1[...], h0[...], 1, 1))
    put(OUT_AT, Q, dot(e[...], h1[...], 1, 1))
    put(IN_AT, Q, dot(x[...], a0[...], 1, 1))
    if more is None:
        rest = GROWS - IN_AT - 96
        grads[pl.ds(IN_AT + 96, rest), :] = jnp.zeros((rest, 128), F32)


def first_kernel(place, source_far, level_far, quadrant_far, f0_far, cot_far, w_in_far, w_mid_far,
                 w_out_far, post, local, xs, xys, zs, h0_far, h1_far,
                 source, level, quadrant, f0, cot, w_in_t, w_mid, w_out, h0, h1, work, y_two, z_two,
                 sems, out_sems):
    info = Tables(place, source, level, quadrant)
    copies = Copies(sems)
    for far, near in ((cot_far, cot), (source_far, source), (level_far, level),
                      (quadrant_far, quadrant), (f0_far, f0), (w_in_far, w_in_t),
                      (w_mid_far, w_mid), (w_out_far, w_out)):
        copies.start(far, near)
    for copy in copies.made[:4]:
        copy.wait()
    stream_back(info, cot, local, xs, xys, zs, work, y_two, z_two)
    for copy in copies.made[4:]:
        copy.wait()
    copies = Copies(out_sems)
    for step in range(CHUNKS):
        a, b, out = forward(cells_of(f0, step), w_in_t[...], w_mid[...], w_out[...])
        h0[:, span(step)] = a
        copies.start(h0.at[:, span(step)], h0_far.at[:, span(step)])
        h1[:, span(step)] = b
        copies.start(h1.at[:, span(step)], h1_far.at[:, span(step)])
        put_cells(post, step, out)
    send_post(post, xs, xys, zs)
    copies.wait()


def second_kernel(place, source, level, quadrant, post1, local2, both, low, high, far, below, above,
                  w_in_t, w_mid, w_mid_t, w_out,
                  post, local, xs, xys, zs, x, e, h0_far, h1_far, a0_far, a1_far,
                  h0, h1, a0, a1, f1, pbar, fbar, work, x_four, y_two, z_two, sems):
    info = Tables(place, source, level, quadrant)
    got = (both, low, high, far, below, above)
    stream(info, post1, got, f1, work, x_four, y_two, z_two)
    pbar[...] = local2[...]
    take_back(info, pbar, got, x_four, y_two)
    copies = Copies(sems)
    for step in range(CHUNKS):
        at = span(step)
        f = cells_of(f1, step)
        h0_now, h1_now, out = forward(f, w_in_t[...], w_mid[...], w_out[...])
        put_cells(post, step, out)
        x[:, at] = f.astype(BF16)
        h0[:, at] = h0_now
        copies.start(h0.at[:, at], h0_far.at[:, at])
        h1[:, at] = h1_now
        copies.start(h1.at[:, at], h1_far.at[:, at])
        bar = cells_of(pbar, step)
        e_now, a1_now, a0_now = signals(bar, h0_now, h1_now, w_mid_t[...], w_out[...])
        put_cells(fbar, step, bar + dot(w_in_t[...], a0_now))
        e[:, at] = e_now
        a1[:, at] = a1_now
        copies.start(a1.at[:, at], a1_far.at[:, at])
        a0[:, at] = a0_now
        copies.start(a0.at[:, at], a0_far.at[:, at])
    send_post(post, xs, xys, zs)
    stream_back(info, fbar, local, xs, xys, zs, work, y_two, z_two)
    copies.wait()


def grads_kernel(x, e, h0_far, h1_far, a0_far, a1_far, grads, h0, h1, a0, a1, sems):
    copies = Copies(sems)
    pairs = ((h0_far, h0), (a1_far, a1), (h1_far, h1), (a0_far, a0))
    for step in range(CHUNKS):
        for far, near in pairs:
            copies.start(far.at[:, span(step)], near.at[:, span(step)])
    for step in range(CHUNKS):
        for copy in copies.made[4 * step : 4 * step + 4]:
            copy.wait()
        at = span(step)
        put_grads(grads, x.at[:, at], e.at[:, at], h0.at[:, at], h1.at[:, at], a0.at[:, at],
                  a1.at[:, at], grads if step else None)


def third_kernel(place, source, level, quadrant, f0, local1, both, low, high, far, below, above,
                 w_mid_t, w_out, grads2, h0_far, h1_far,
                 grads, pbar, a0_far, h0, h1, a0, a1, x, e, x_four, y_two, sems):
    info = Tables(place, source, level, quadrant)
    got = (both, low, high, far, below, above)
    copies = Copies(sems)
    for step in range(CHUNKS):
        for hbm, near in ((h1_far, h1), (h0_far, h0)):
            copies.start(hbm.at[:, span(step)], near.at[:, span(step)])
    pbar[...] = local1[...]
    take_back(info, pbar, got, x_four, y_two)
    for step in range(CHUNKS):
        at = span(step)
        for copy in copies.made[2 * step : 2 * step + 2]:
            copy.wait()
        e_now, a1_now, a0_now = signals(
            cells_of(pbar, step), h0[:, at], h1[:, at], w_mid_t[...], w_out[...]
        )
        x[:, at] = cells_of(f0, step).astype(BF16)
        e[:, at] = e_now
        a1[:, at] = a1_now
        a0[:, at] = a0_now
        copies.start(a0.at[:, at], a0_far.at[:, at])
    put_grads(grads, x, e, h0, h1, a0, a1, grads2)
    for copy in copies.made[2 * CHUNKS :]:
        copy.wait()


def final_kernel(place, source, level, quadrant, post2, both, low, high, far, below, above,
                 out, work, x_four, y_two, z_two):
    info = Tables(place, source, level, quadrant)
    stream(info, post2, (both, low, high, far, below, above), out, work, x_four, y_two, z_two)


def bar_kernel(pbar, w_in_t, a0_far, fbar, a0, sems):
    copies = Copies(sems)
    for step in range(CHUNKS):
        copies.start(a0_far.at[:, span(step)], a0.at[:, span(step)])
    for step in range(CHUNKS):
        copies.made[step].wait()
        put_cells(fbar, step, cells_of(pbar, step) + dot(w_in_t[...], a0[:, span(step)]))


def unpack_kernel(place, mine, other, g_in, g_mid, g_out, whole):
    scale = float(NB * NZ * CELLS) ** -0.5
    core = place[0] & 1
    whole[pl.ds(pl.multiple_of(core * HALF, HALF), HALF), :] = mine[...]
    whole[pl.ds(pl.multiple_of((1 - core) * HALF, HALF), HALF), :] = other[...]
    for j in range(4):
        cols = pl.ds(j * 128, 128)
        g_mid[:, cols] = whole[pl.ds(j * HID, HID), :] * scale
        g_out[:, cols] = whole[pl.ds(OUT_AT + 24 * j, Q), :] * scale
        g_in[:, cols] = whole[pl.ds(IN_AT + 24 * j, Q), :] * scale


BLOCK = (Q, ROWS, 128)
HIDDEN = (HID, CELLS)
THIN = (Q, CELLS)
SENDS = [(2, 2, 2, 8, 128), (128, 128), (2, ROWS, 128)]
FACES = [(2, 2, 8, 128), (2, 16, 128), (2, ROWS, 128)]


def run(kernel, tables, args, outs, scratch, mflops, hbm=()):
    def shape(s):
        return jax.ShapeDtypeStruct(s, F32) if isinstance(s, tuple) else s

    def buffer(s):
        return pltpu.VMEM(s, F32) if isinstance(s, tuple) else s

    def out_spec(s):
        far = not isinstance(s, (tuple, jax.ShapeDtypeStruct))
        return pl.BlockSpec(memory_space=pltpu.HBM if far else pltpu.VMEM)

    args = list(args)
    in_specs = [pl.BlockSpec(memory_space=pltpu.SMEM)] * len(tables)
    for i in range(len(args)):
        if i in hbm:
            args[i] = pltpu.with_memory_space_constraint(args[i], pltpu.HBM)
        in_specs.append(pl.BlockSpec(memory_space=pltpu.HBM if i in hbm else pltpu.VMEM))
    return pl.pallas_call(
        kernel,
        out_shape=[shape(s) for s in outs],
        in_specs=in_specs,
        out_specs=[out_spec(s) for s in outs],
        scratch_shapes=[buffer(s) for s in scratch],
        compiler_params=pltpu.CompilerParams(vmem_limit_bytes=VMEM_LIMIT),
        cost_estimate=pl.CostEstimate(
            flops=mflops * 1000000, bytes_accessed=1 << 20, transcendentals=0
        ),
    )(*tables, *args)


def send(value, target):
    pairs = [
        (b * NZ + z, nb % NB * NZ + nz % NZ)
        for b in range(NB)
        for z in range(NZ)
        for nb, nz in [target(b, z)]
    ]
    return lax.ppermute(value, AXES, pairs)


def exchange(xs, xys, zs):
    x = xs.reshape(64, 128)
    below = send(zs, lambda b, z: (b, z + 1))
    above = send(zs, lambda b, z: (b, z - 1))
    both = send(xys, lambda b, z: (b ^ 1, z))
    far = send(x, lambda b, z: (b - 3 if b % 2 == 0 else b + 3, z))
    pair = jnp.concatenate([x, both[:64]])
    low = send(pair, lambda b, z: (b + 2, z))
    high = send(pair, lambda b, z: (b - 2, z))
    return both, low, high, far, below, above


def total_over_devices(grads, core, beside):
    def other_core(v):
        return send(v, lambda b, z: (b ^ 1, z))

    halves = grads.reshape(2, HALF, 128)
    mine = lax.dynamic_index_in_dim(halves, core, 0, keepdims=False)
    given = lax.dynamic_index_in_dim(halves, 1 - core, 0, keepdims=False)
    arrived, beside = lax.optimization_barrier((other_core(given), beside))
    mine = (mine + arrived).reshape(64, 1, HALF * 2)
    mine = lax.all_to_all(mine, CHIPS, 0, 0, tiled=True).sum(axis=0, keepdims=True)
    mine = jnp.broadcast_to(mine, (64, 1, HALF * 2))
    mine = lax.all_to_all(mine, CHIPS, 0, 0, tiled=True).reshape(HALF, 128)
    return mine, other_core(mine), beside


def shards(populations, w_in, w_mid, w_out, cotangent, face_source, face_level, face_quadrant):
    f0 = populations.reshape(BLOCK)
    cot = cotangent.reshape(BLOCK)
    w_in_t = w_in.T
    w_mid = w_mid[0]
    w_mid_t = w_mid.T
    place = lax.axis_index(BLOCKS).astype(jnp.int32).reshape(1)
    tables = [place, face_source.T, face_level[0], face_quadrant[0]]
    hidden = pltpu.HBM(HIDDEN, BF16)
    thin = jax.ShapeDtypeStruct(THIN, BF16)
    grad = (GROWS, 128)
    near = pltpu.VMEM(HIDDEN, BF16)
    near_thin = pltpu.VMEM(THIN, BF16)
    sems = pltpu.SemaphoreType.DMA

    post1, local2, *sends, h0, h1 = run(
        first_kernel, tables[:1], [*tables[1:], f0, cot, w_in_t, w_mid, w_out],
        [BLOCK, BLOCK, *SENDS, hidden, hidden],
        [pltpu.SMEM((4, NB), jnp.int32), pltpu.SMEM((1, 6), jnp.int32),
         pltpu.SMEM((1, 6), jnp.int32),
         BLOCK, BLOCK, pltpu.VMEM((Q, HID), BF16), pltpu.VMEM((HID, HID), BF16),
         pltpu.VMEM((Q, HID), BF16), near, near, BLOCK, *FACES[1:], sems((8,)),
         sems((2 * CHUNKS,))],
        4000, range(8),
    )
    got = exchange(*sends)
    post2, local1, *sends, x2, e2, h0_2, h1_2, a0_2, a1_2 = run(
        second_kernel, tables, [post1, local2, *got, w_in_t, w_mid, w_mid_t, w_out],
        [BLOCK, BLOCK, *SENDS, thin, thin, hidden, hidden, hidden, hidden],
        [near] * 4 + [BLOCK] * 4 + FACES + [sems((4 * CHUNKS,))], 10000,
    )
    got = exchange(*sends)
    (grads2,) = run(
        grads_kernel, [], [x2, e2, h0_2, h1_2, a0_2, a1_2], [grad],
        [near] * 4 + [sems((4 * CHUNKS,))], 4000, (2, 3, 4, 5),
    )
    grads, pbar1, a0 = run(
        third_kernel, tables, [f0, local1, *got, w_mid_t, w_out, grads2, h0, h1],
        [grad, BLOCK, hidden],
        [near] * 4 + [near_thin] * 2 + [*FACES[:2], sems((3 * CHUNKS,))],
        8000, (11, 12),
    )
    post2, grads = lax.optimization_barrier((post2, grads))
    (final,) = run(final_kernel, tables, [post2, *got], [BLOCK], [BLOCK, *FACES], 500)
    (fbar0,) = run(
        bar_kernel, [], [pbar1, w_in_t, a0], [BLOCK], [near, sems((CHUNKS,))], 500, (2,)
    )
    mine, other, final = total_over_devices(grads, place[0] % 2, final)
    g_in, g_mid, g_out = run(
        unpack_kernel, [place], [mine, other], [(Q, HID), (HID, HID), (Q, HID)], [grad], 10
    )
    whole = (Q, 1, 1, CELLS)
    return final.reshape(whole), fbar0.reshape(whole), g_in.T, g_mid[None], g_out


def solution(mesh):
    cells = P(None, "slab", BLOCKS, None)
    local = P("slab", BLOCKS, None)
    split = Mesh(mesh.devices.reshape(NX, NX, 2, NZ), AXES)
    return jax.shard_map(
        shards,
        mesh=split,
        in_specs=(cells, P(), P(), P(), cells, P(), local, local),
        out_specs=(cells, cells, P(), P(), P()),
        check_vma=False,
    )
```

```python
import jax
import jax.numpy as jnp
from jax import lax
from jax.experimental import pallas as pl
from jax.experimental.pallas import tpu as pltpu
from jax.sharding import Mesh
from jax.sharding import PartitionSpec as P

Q = 19
HID = 512
CELLS = 4096
ROWS = 32
CHUNK = 1024
TILES = CHUNK // 128
CHUNKS = CELLS // CHUNK
NB = 32
NZ = 4
NX = 4
BLOCKS = ("bx", "by", "core")
AXES = ("bx", "by", "core", "slab")
CHIPS = ("bx", "by", "slab")
F32 = jnp.float32
BF16 = jnp.bfloat16
GROWS = 2304
HALF = GROWS // 2
OUT_AT = 4 * HID
IN_AT = OUT_AT + 4 * 24

VELOCITIES = [
    (0, 0, 0),
    (1, 0, 0),
    (-1, 0, 0),
    (0, 1, 0),
    (0, -1, 0),
    (0, 0, 1),
    (0, 0, -1),
    (1, 1, 0),
    (-1, -1, 0),
    (1, -1, 0),
    (-1, 1, 0),
    (1, 0, 1),
    (-1, 0, -1),
    (1, 0, -1),
    (-1, 0, 1),
    (0, 1, 1),
    (0, -1, -1),
    (0, 1, -1),
    (0, -1, 1),
]
OPPOSITE = [0, 2, 1, 4, 3, 6, 5, 8, 7, 10, 9, 12, 11, 14, 13, 16, 15, 18, 17]


def members(face):
    sign = 1 if face % 2 == 0 else -1
    return [q for q in range(Q) if VELOCITIES[q][face // 2] == sign]


def iota(rows, dim):
    return lax.broadcasted_iota(jnp.int32, (rows, 128), dim)


def roll(value, shift, axis):
    shift %= value.shape[axis]
    return value if shift == 0 else pltpu.roll(value, shift, axis)


def shifted(v, velocity):
    cx, cy, cz = velocity
    lane = iota(ROWS, 1)
    if cz:
        v = jnp.where(lane & 15 == (0 if cz == 1 else 15), roll(v, -15 * cz, 1), roll(v, cz, 1))
    if cy:
        t = roll(v, 16 * cy, 1)
        swapped = jnp.where(iota(ROWS, 0) & 1 == 1, roll(t, 1, 0), roll(t, -1, 0))
        v = jnp.where(lane >> 4 == (0 if cy == 1 else 7), swapped, t)
    if cx:
        v = roll(v, 2 * cx, 0)
    return v


def corner(q):
    row, lane = iota(ROWS, 0), iota(ROWS, 1)
    coords = [row >> 1, (row & 1) * 8 + (lane >> 4), lane & 15]
    mask = None
    for axis in range(3):
        c = VELOCITIES[q][axis]
        if c:
            here = coords[axis] == (0 if c == 1 else 15)
            mask = here if mask is None else mask & here
    return mask


def is_edge(q):
    return sum(abs(c) for c in VELOCITIES[q]) == 2


def pack_faces(src, put_x, put_y, put_z):
    lane16, lane32 = iota(16, 1), iota(ROWS, 1)
    for f in (0, 1):
        for i, q in enumerate(members(f)):
            for r in (0, 1):
                put_x(f, r, i, src[q, pl.ds((30 if f == 0 else 0) + r, 1), :])
    for f in (2, 3):
        acc = jnp.zeros((16, 128), F32)
        for i, q in enumerate(members(f)):
            v = src[q, pl.ds(1 if f == 2 else 0, 16, stride=2), :]
            v = roll(v, 16 * i - (112 if f == 2 else 0), 1)
            acc = jnp.where(lane16 >> 4 == i, v, acc)
        put_y(f - 2, acc)
    acc = jnp.zeros((ROWS, 128), F32)
    for f in (4, 5):
        for i, q in enumerate(members(f)):
            slot = i if f == 4 else 8 + i
            v = roll(src[q], slot - (15 if f == 4 else 0), 1)
            acc = jnp.where(lane32 & 15 == slot, v, acc)
    put_z(acc)


def unpack_faces(dst, get_x, y_ref, z, add):
    lane16, lane32 = iota(16, 1), iota(ROWS, 1)
    for f in (0, 1):
        for i, q in enumerate(members(f)):
            for r in (0, 1):
                at = pl.ds((30 if f == 0 else 0) + r, 1)
                v = get_x(f, r, i)
                dst[q, at, :] = dst[q, at, :] + v if add else v
    for f in (2, 3):
        packed = y_ref[f - 2]
        for i, q in enumerate(members(f)):
            at = pl.ds(1 if f == 2 else 0, 16, stride=2)
            v = roll(packed, (112 if f == 2 else 0) - 16 * i, 1)
            old = dst[q, at, :]
            new = old + v if add else v
            dst[q, at, :] = jnp.where(lane16 >> 4 == (7 if f == 2 else 0), new, old)
    for f in (4, 5):
        for i, q in enumerate(members(f)):
            v = roll(z, 15 - i if f == 4 else -(8 + i), 1)
            old = dst[q]
            new = old + v if add else v
            dst[q] = jnp.where(lane32 & 15 == (15 if f == 4 else 0), new, old)


def picked(value, index):
    return jnp.take_along_axis(value, index, axis=1)


class Tables:
    def __init__(self, place, source, level, quadrant):
        self.place, self.source, self.level, self.quadrant = place, source, level, quadrant

    def block(self):
        return self.place[0]

    def distance(self, face):
        d = self.source[face, self.block()] - self.block()
        return jnp.where(d < 0, d + NB, d)


def level_of(info, f):
    return info.level[0, f ^ 1] == 1


def quadrant_of(info, f):
    r = info.quadrant[0, f ^ 1]
    return r >> 1, r & 1


def refine_x(info, x):
    lane = iota(8, 1)
    for f in (0, 1):
        fine = level_of(info, f)
        qr, qc = quadrant_of(info, f)
        rows = [x[f, 0], x[f, 1]]
        source = jnp.where(qr == 0, rows[0], rows[1])
        for r in (0, 1):
            index = (r * 4 + (lane >> 5)) * 16 + qc * 8 + ((lane & 15) >> 1)
            x[f, r] = jnp.where(fine, picked(source, index), rows[r])


def refine_y(info, y):
    lane = iota(8, 1)
    for f in (2, 3):
        fine = level_of(info, f)
        qr, qc = quadrant_of(info, f)
        whole = y[f - 2]
        source = jnp.where(qr == 0, whole[:8], whole[8:])
        v = picked(source, (lane >> 4) * 16 + qc * 8 + ((lane & 15) >> 1))
        for d in (0, 1):
            at = pl.ds(d, 8, stride=2)
            y[f - 2, at, :] = jnp.where(fine, v, y[f - 2, at, :])


def refine_z(info, z_two):
    lane = iota(8, 1)
    for f in (4, 5):
        z = z_two.at[f - 4]
        fine = level_of(info, f)
        qr, qc = quadrant_of(info, f)
        parts = {(h, p): z[pl.ds(16 * h + p, 8, stride=2), :] for h in (0, 1) for p in (0, 1)}
        halves = [jnp.where(qc == 0, parts[h, 0], parts[h, 1]) for h in (0, 1)]
        source = jnp.where(qr == 0, halves[0], halves[1])
        for p in (0, 1):
            v = picked(source, (p * 4 + (lane >> 5)) * 16 + (lane & 15))
            for d in (0, 1):
                at = pl.ds(2 * d + p, 8, stride=4)
                z[at, :] = jnp.where(fine, v, z[at, :])
    return jnp.where(iota(ROWS, 1) & 15 < 8, z_two[0], z_two[1])


def gather_x(info, x):
    lane = iota(8, 1)
    index = (2 * ((lane >> 4) & 3)) * 16 + 2 * (lane & 7)
    for f in (0, 1):
        fine = level_of(info, f)
        qr, qc = quadrant_of(info, f)
        rows = [x[f, 0], x[f, 1]]
        sums = []
        for v in rows:
            v = v + roll(v, -1, 1)
            v = v + roll(v, -16, 1)
            sums.append(picked(v, index))
        v = jnp.where(lane < 64, sums[0], sums[1])
        v = jnp.where((lane & 15) >> 3 == qc, v, 0.0)
        for r in (0, 1):
            x[f, r] = jnp.where(fine, jnp.where(qr == r, v, 0.0), rows[r])


def gather_y(info, y):
    lane = iota(8, 1)
    index = (lane >> 4) * 16 + 2 * (lane & 7)
    for f in (2, 3):
        fine = level_of(info, f)
        qr, qc = quadrant_of(info, f)
        v = y[f - 2, pl.ds(0, 8, stride=2), :] + y[f - 2, pl.ds(1, 8, stride=2), :]
        v = picked(v + roll(v, -1, 1), index)
        v = jnp.where((lane & 15) >> 3 == qc, v, 0.0)
        for h in (0, 1):
            at = pl.ds(8 * h, 8)
            y[f - 2, at, :] = jnp.where(fine, jnp.where(qr == h, v, 0.0), y[f - 2, at, :])


def gather_z(info, z_two):
    lane = iota(8, 1)
    index = (2 * ((lane >> 4) & 3)) * 16 + (lane & 15)
    for f in (4, 5):
        z = z_two.at[f - 4]
        fine = level_of(info, f)
        qr, qc = quadrant_of(info, f)
        sums = []
        for p in (0, 1):
            v = z[pl.ds(p, 8, stride=4), :] + z[pl.ds(2 + p, 8, stride=4), :]
            sums.append(picked(v + roll(v, -16, 1), index))
        v = jnp.where(lane < 64, sums[0], sums[1])
        for h in (0, 1):
            for p in (0, 1):
                at = pl.ds(16 * h + p, 8, stride=2)
                here = (qr == h) & (qc == p)
                z[at, :] = jnp.where(fine, jnp.where(here, v, 0.0), z[at, :])
    return jnp.where(iota(ROWS, 1) & 15 < 8, z_two[0], z_two[1])


def choose_x(info, face, got, kind):
    swapped, x_got, z_got, far, passed = got
    d = info.distance(face)
    even = info.block() & 1 == 0

    def at(distance):
        return jnp.where(even, distance % NB, -distance % NB)

    cases = [
        (at(1), swapped, 0),
        (at(-2), x_got, 0),
        (at(-1), x_got, 64),
        (at(3), passed, 0),
        (at(2), passed, 64),
        (at(-3), far, 0),
    ]
    return lambda f, r: sum_where(
        [
            (d == spot, ref[pl.ds(start + 8 * (kind * 4 + f * 2 + r), 8), :])
            for spot, ref, start in cases
        ]
    )


def choose_z(info, got, kind):
    direct = got[2][pl.ds(32 * kind, 32), :]
    passed = got[4][pl.ds(128 + 32 * kind, 32), :]
    even = info.block() & 1 == 0
    return jnp.where(even, direct, passed), jnp.where(even, passed, direct)


def sum_where(cases):
    total = jnp.zeros((8, 128), F32)
    for condition, value in cases:
        total = jnp.where(condition, value, total)
    return total


def stream_back(info, bar, local, xs, sends, work, y_two, z_two):
    for q in range(Q):
        v = bar[q]
        if is_edge(q):
            v = jnp.where(corner(q), 0.0, v)
        work[q] = shifted(v, tuple(-c for c in VELOCITIES[q]))
    x_four = xs.at[1]
    x_four[...] = jnp.zeros(x_four.shape, F32)

    def put_x(f, r, i, v):
        x_four[f, r, pl.ds(i, 1), :] = v

    def put_y(f, v):
        y_two[f] = v

    def put_z(v):
        z_two[0] = v
        z_two[1] = v

    pack_faces(work, put_x, put_y, put_z)
    gather_x(info, x_four)
    gather_y(info, y_two)
    sends[pl.ds(160, 32), :] = gather_z(info, z_two)
    sends[pl.ds(32, 32), :] = xs[1].reshape(32, 128)
    sends[pl.ds(96, 32), :] = y_two[...].reshape(32, 128)
    row, lane = iota(ROWS, 0), iota(ROWS, 1)
    coords = [row >> 1, (row & 1) * 8 + (lane >> 4), lane & 15]
    for q in range(Q):
        v = work[q]
        leaving = None
        for axis in range(3):
            c = VELOCITIES[q][axis]
            if c:
                here = coords[axis] == (15 if c == 1 else 0)
                leaving = here if leaving is None else leaving | here
        if leaving is not None:
            v = jnp.where(leaving, 0.0, v)
        if is_edge(q):
            v = v + jnp.where(corner(OPPOSITE[q]), bar[OPPOSITE[q]], 0.0)
        local[q] = v


def send_post(post, xs, sends):
    x_four = xs.at[0]
    x_four[...] = jnp.zeros(x_four.shape, F32)

    def put_x(f, r, i, v):
        x_four[f, r, pl.ds(i, 1), :] = v

    def put_y(f, v):
        sends[pl.ds(64 + 16 * f, 16), :] = v

    def put_z(v):
        sends[pl.ds(128, 32), :] = v

    pack_faces(post, put_x, put_y, put_z)
    sends[pl.ds(0, 32), :] = xs[0].reshape(32, 128)


def stream(info, post, got, out, work, x_four, y_two, z_two):
    swapped = got[0]
    for f in (0, 1):
        pick = choose_x(info, f ^ 1, got, 0)
        for r in (0, 1):
            x_four[f, r] = pick(f, r)
    refine_x(info, x_four)
    y_two[0] = swapped[pl.ds(64, 16), :]
    y_two[1] = swapped[pl.ds(80, 16), :]
    refine_y(info, y_two)
    z_two[0], z_two[1] = choose_z(info, got, 0)
    z = refine_z(info, z_two)
    work[...] = post[...]
    unpack_faces(work, lambda f, r, i: x_four[f, r, pl.ds(i, 1), :], y_two, z, False)
    for q in range(Q):
        v = shifted(work[q], VELOCITIES[q])
        if is_edge(q):
            v = jnp.where(corner(q), post[OPPOSITE[q]], v)
        out[q] = v


def take_back(info, bar, got, x_four, y_two):
    swapped = got[0]
    for f in (0, 1):
        pick = choose_x(info, f, got, 1)
        for r in (0, 1):
            x_four[f, r] = pick(f, r)
    y_two[0] = swapped[pl.ds(96, 16), :]
    y_two[1] = swapped[pl.ds(112, 16), :]
    below, above = choose_z(info, got, 1)
    z = jnp.where(iota(ROWS, 1) & 15 < 8, above, below)
    unpack_faces(bar, lambda f, r, i: x_four[f, r, pl.ds(i, 1), :], y_two, z, True)


def dot(a, b, ca=1, cb=0):
    return lax.dot_general(a, b, (((ca,), (cb,)), ((), ())), preferred_element_type=F32)


def cells_of(ref, step):
    parts = [
        ref[:, pl.ds(step * TILES + j, 1), :].reshape(Q, 128) for j in range(TILES)
    ]
    return jnp.concatenate(parts, axis=1)


def put_cells(ref, step, value):
    for j in range(TILES):
        ref[:, pl.ds(step * TILES + j, 1), :] = value[:, j * 128 : (j + 1) * 128].reshape(Q, 1, 128)


def span(step):
    return pl.ds(step * CHUNK, CHUNK)


def forward(x, w_in_t, w_mid, w_out):
    xb = x.astype(BF16)
    h0 = jnp.tanh(dot(w_in_t, xb, 0, 0)).astype(BF16)
    h1 = jnp.tanh(dot(w_mid, h0)).astype(BF16)
    return h0, h1, x + dot(w_out, h1)


def slope(h):
    h = h.astype(F32)
    return 1.0 - h * h


def signals(pbar, h0, h1, w_mid_t, w_out):
    e = pbar.astype(BF16)
    a1 = (dot(w_out, e, 0, 0) * slope(h1)).astype(BF16)
    a0 = (dot(w_mid_t, a1) * slope(h0)).astype(BF16)
    return e, a1, a0


class Copies:
    def __init__(self, sems):
        self.sems, self.made = sems, []

    def start(self, source, target):
        copy = pltpu.make_async_copy(source, target, self.sems.at[len(self.made)])
        copy.start()
        self.made.append(copy)
        return copy

    def wait(self):
        for copy in self.made:
            copy.wait()


def put_grads(grads, x, e, h0, h1, a0, a1, more):
    def put(at, rows, value):
        for j in range(4):
            spot = pl.ds(at + j * (HID if rows == HID else 24), rows)
            v = value[:, j * 128 : (j + 1) * 128]
            grads[spot, :] = v if more is None else more[spot, :] + v

    put(0, HID, dot(a1[...], h0[...], 1, 1))
    put(OUT_AT, Q, dot(e[...], h1[...], 1, 1))
    put(IN_AT, Q, dot(x[...], a0[...], 1, 1))
    if more is None:
        rest = GROWS - IN_AT - 96
        grads[pl.ds(IN_AT + 96, rest), :] = jnp.zeros((rest, 128), F32)


def first_kernel(place, source_far, level_far, quadrant_far, f0_far, cot_far, w_in_far, w_mid_far,
                 w_out_far, post, local, sends, h0_far, h1_far,
                 source, level, quadrant, xs, f0, cot, w_in_t, w_mid, w_out, h0, h1, work, y_two, z_two,
                 sems, out_sems):
    info = Tables(place, source, level, quadrant)
    copies = Copies(sems)
    for far, near in ((cot_far, cot), (source_far, source), (level_far, level),
                      (quadrant_far, quadrant), (f0_far, f0), (w_in_far, w_in_t),
                      (w_mid_far, w_mid), (w_out_far, w_out)):
        copies.start(far, near)
    for copy in copies.made[:4]:
        copy.wait()
    stream_back(info, cot, local, xs, sends, work, y_two, z_two)
    for copy in copies.made[4:]:
        copy.wait()
    copies = Copies(out_sems)
    for step in range(CHUNKS):
        a, b, out = forward(cells_of(f0, step), w_in_t[...], w_mid[...], w_out[...])
        h0[:, span(step)] = a
        copies.start(h0.at[:, span(step)], h0_far.at[:, span(step)])
        h1[:, span(step)] = b
        copies.start(h1.at[:, span(step)], h1_far.at[:, span(step)])
        put_cells(post, step, out)
    send_post(post, xs, sends)
    copies.wait()


def second_kernel(place, source, level, quadrant, post1, local2, swapped, x_got, z_got, far, passed,
                  w_in_t, w_mid, w_mid_t, w_out, post, local, sends, grads_far,
                  grads, xs, x, e, h0, h1, a0, a1, f1, pbar, fbar, work, x_four, y_two, z_two, sem):
    info = Tables(place, source, level, quadrant)
    got = (swapped, x_got, z_got, far, passed)
    stream(info, post1, got, f1, work, x_four, y_two, z_two)
    pbar[...] = local2[...]
    take_back(info, pbar, got, x_four, y_two)
    for step in range(CHUNKS):
        at = span(step)
        f = cells_of(f1, step)
        h0_now, h1_now, out = forward(f, w_in_t[...], w_mid[...], w_out[...])
        put_cells(post, step, out)
        bar = cells_of(pbar, step)
        e_now, a1_now, a0_now = signals(bar, h0_now, h1_now, w_mid_t[...], w_out[...])
        put_cells(fbar, step, bar + dot(w_in_t[...], a0_now))
        x[:, at] = f.astype(BF16)
        e[:, at] = e_now
        h0[:, at] = h0_now
        h1[:, at] = h1_now
        a1[:, at] = a1_now
        a0[:, at] = a0_now
    put_grads(grads, x, e, h0, h1, a0, a1, None)
    copies = Copies(sem)
    copies.start(grads, grads_far)
    send_post(post, xs, sends)
    stream_back(info, fbar, local, xs, sends, work, y_two, z_two)
    copies.wait()


def third_kernel(place, source, level, quadrant, f0, local1, swapped, x_got, z_got, far, passed,
                 w_in_t, w_mid_t, w_out, grads2_far, h0_far, h1_far,
                 grads, fbar, pbar, h0, h1, a0, a1, x, e, x_four, y_two, sems):
    info = Tables(place, source, level, quadrant)
    copies = Copies(sems)
    for step in range(CHUNKS):
        for hbm, near in ((h1_far, h1), (h0_far, h0)):
            copies.start(hbm.at[:, span(step)], near.at[:, span(step)])
    copies.start(grads2_far, grads)
    pbar[...] = local1[...]
    take_back(info, pbar, (swapped, x_got, z_got, far, passed), x_four, y_two)
    for step in range(CHUNKS):
        at = span(step)
        for copy in copies.made[2 * step : 2 * step + 2]:
            copy.wait()
        bar = cells_of(pbar, step)
        e_now, a1_now, a0_now = signals(bar, h0[:, at], h1[:, at], w_mid_t[...], w_out[...])
        put_cells(fbar, step, bar + dot(w_in_t[...], a0_now))
        x[:, at] = cells_of(f0, step).astype(BF16)
        e[:, at] = e_now
        a1[:, at] = a1_now
        a0[:, at] = a0_now
    copies.made[-1].wait()
    put_grads(grads, x, e, h0, h1, a0, a1, grads)


def final_kernel(place, source, level, quadrant, post2, swapped, x_got, z_got, far, passed,
                 out, work, x_four, y_two, z_two):
    info = Tables(place, source, level, quadrant)
    stream(info, post2, (swapped, x_got, z_got, far, passed), out, work, x_four, y_two, z_two)


def unpack_kernel(place, mine, other, g_in, g_mid, g_out, whole):
    scale = float(NB * NZ * CELLS) ** -0.5
    core = place[0] & 1
    whole[pl.ds(pl.multiple_of(core * HALF, HALF), HALF), :] = mine[...]
    whole[pl.ds(pl.multiple_of((1 - core) * HALF, HALF), HALF), :] = other[...]
    for j in range(4):
        cols = pl.ds(j * 128, 128)
        g_mid[:, cols] = whole[pl.ds(j * HID, HID), :] * scale
        g_out[:, cols] = whole[pl.ds(OUT_AT + 24 * j, Q), :] * scale
        g_in[:, cols] = whole[pl.ds(IN_AT + 24 * j, Q), :] * scale


BLOCK = (Q, ROWS, 128)
HIDDEN = (HID, CELLS)
THIN = (Q, CELLS)
SENDS = (192, 128)
X_TWO = (2, 2, 2, 8, 128)
FACES = [(2, 2, 8, 128), (2, 16, 128), (2, ROWS, 128)]


def run(kernel, tables, args, outs, scratch, mflops, megabytes, hbm=()):
    def shape(s):
        return jax.ShapeDtypeStruct(s, F32) if isinstance(s, tuple) else s

    def buffer(s):
        return pltpu.VMEM(s, F32) if isinstance(s, tuple) else s

    def out_spec(s):
        far = not isinstance(s, (tuple, jax.ShapeDtypeStruct))
        return pl.BlockSpec(memory_space=pltpu.HBM if far else pltpu.VMEM)

    args = list(args)
    in_specs = [pl.BlockSpec(memory_space=pltpu.SMEM)] * len(tables)
    for i in range(len(args)):
        if i in hbm:
            args[i] = pltpu.with_memory_space_constraint(args[i], pltpu.HBM)
        in_specs.append(pl.BlockSpec(memory_space=pltpu.HBM if i in hbm else pltpu.VMEM))
    return pl.pallas_call(
        kernel,
        out_shape=[shape(s) for s in outs],
        in_specs=in_specs,
        out_specs=[out_spec(s) for s in outs],
        scratch_shapes=[buffer(s) for s in scratch],
        compiler_params=pltpu.CompilerParams(vmem_limit_bytes=megabytes << 20),
        cost_estimate=pl.CostEstimate(
            flops=mflops * 1000000, bytes_accessed=1 << 20, transcendentals=0
        ),
    )(*tables, *args)


def send(value, target):
    pairs = [
        (b * NZ + z, nb % NB * NZ + nz % NZ)
        for b in range(NB)
        for z in range(NZ)
        for nb, nz in [target(b, z)]
    ]
    return lax.ppermute(value, AXES, pairs)


def exchange(sends):
    swapped = send(sends, lambda b, z: (b ^ 1, z))
    far = send(sends[:64], lambda b, z: (b - 3 if b % 2 == 0 else b + 3, z))
    x_got = send(
        jnp.concatenate([sends[:64], swapped[:64]]),
        lambda b, z: (b + 2 if b % 2 == 0 else b - 2, z),
    )
    z_got = send(
        jnp.concatenate([sends[128:], swapped[128:]]),
        lambda b, z: (b, z + 1 if b % 2 == 0 else z - 1),
    )
    x_got, z_got, far = lax.optimization_barrier((x_got, z_got, far))
    passed = send(jnp.concatenate([x_got, z_got[64:]]), lambda b, z: (b ^ 1, z))
    return swapped, x_got, z_got, far, passed


def total_over_devices(grads, core, beside):
    def other_core(v):
        return send(v, lambda b, z: (b ^ 1, z))

    halves = grads.reshape(2, HALF, 128)
    mine = lax.dynamic_index_in_dim(halves, core, 0, keepdims=False)
    given = lax.dynamic_index_in_dim(halves, 1 - core, 0, keepdims=False)
    arrived, beside = lax.optimization_barrier((other_core(given), beside))
    mine = (mine + arrived).reshape(64, 1, HALF * 2)
    mine = lax.all_to_all(mine, CHIPS, 0, 0, tiled=True).sum(axis=0, keepdims=True)
    mine = jnp.broadcast_to(mine, (64, 1, HALF * 2))
    mine = lax.all_to_all(mine, CHIPS, 0, 0, tiled=True).reshape(HALF, 128)
    return mine, other_core(mine), beside


def shards(populations, w_in, w_mid, w_out, cotangent, face_source, face_level, face_quadrant):
    f0 = populations.reshape(BLOCK)
    cot = cotangent.reshape(BLOCK)
    w_in_t = w_in.T
    w_mid = w_mid[0]
    w_mid_t = w_mid.T
    place = lax.axis_index(BLOCKS).astype(jnp.int32).reshape(1)
    tables = [place, face_source.T, face_level[0], face_quadrant[0]]
    hidden = pltpu.HBM(HIDDEN, BF16)
    thin = jax.ShapeDtypeStruct(THIN, BF16)
    grad = (GROWS, 128)
    near = pltpu.VMEM(HIDDEN, BF16)
    near_thin = pltpu.VMEM(THIN, BF16)
    sems = pltpu.SemaphoreType.DMA

    post1, local2, sends, h0, h1 = run(
        first_kernel, tables[:1], [*tables[1:], f0, cot, w_in_t, w_mid, w_out],
        [BLOCK, BLOCK, SENDS, hidden, hidden],
        [pltpu.SMEM((4, NB), jnp.int32), pltpu.SMEM((1, 6), jnp.int32),
         pltpu.SMEM((1, 6), jnp.int32), X_TWO,
         BLOCK, BLOCK, pltpu.VMEM((Q, HID), BF16), pltpu.VMEM((HID, HID), BF16),
         pltpu.VMEM((Q, HID), BF16), near, near, BLOCK, *FACES[1:], sems((8,)),
         sems((2 * CHUNKS,))],
        4000, 32, range(8),
    )
    got = exchange(sends)
    post2, local1, sends, grads2 = run(
        second_kernel, tables, [post1, local2, *got, w_in_t, w_mid, w_mid_t, w_out],
        [BLOCK, BLOCK, SENDS, pltpu.HBM(grad, F32)],
        [grad, X_TWO, near_thin, near_thin, *[near] * 4, *[BLOCK] * 4, *FACES, sems((1,))],
        14000, 32,
    )
    got = exchange(sends)
    grads, fbar0 = run(
        third_kernel, tables, [f0, local1, *got, w_in_t, w_mid_t, w_out, grads2, h0, h1],
        [grad, BLOCK],
        [BLOCK, *[near] * 4, near_thin, near_thin, *FACES[:2], sems((2 * CHUNKS + 1,))],
        8000, 32, (10, 11, 12),
    )
    post2, grads = lax.optimization_barrier((post2, grads))
    (final,) = run(final_kernel, tables, [post2, *got], [BLOCK], [BLOCK, *FACES], 500, 8)
    mine, other, final = total_over_devices(grads, place[0] % 2, final)
    g_in, g_mid, g_out = run(
        unpack_kernel, [place], [mine, other], [(Q, HID), (HID, HID), (Q, HID)], [grad], 10, 8
    )
    whole = (Q, 1, 1, CELLS)
    return final.reshape(whole), fbar0.reshape(whole), g_in.T, g_mid[None], g_out


def solution(mesh):
    cells = P(None, "slab", BLOCKS, None)
    local = P("slab", BLOCKS, None)
    split = Mesh(mesh.devices.reshape(NX, NX, 2, NZ), AXES)
    return jax.shard_map(
        shards,
        mesh=split,
        in_specs=(cells, P(), P(), P(), cells, P(), local, local),
        out_specs=(cells, cells, P(), P(), P()),
        check_vma=False,
    )
```

```python
import jax
import jax.numpy as jnp
from jax import lax
from jax.experimental import pallas as pl
from jax.experimental.pallas import tpu as pltpu
from jax.sharding import Mesh
from jax.sharding import PartitionSpec as P

Q = 19
HID = 512
CELLS = 4096
ROWS = 32
CHUNK = 1024
TILES = CHUNK // 128
CHUNKS = CELLS // CHUNK
NB = 32
NZ = 4
NX = 4
BLOCKS = ("bx", "by", "core")
AXES = ("bx", "by", "core", "slab")
CHIPS = ("bx", "by", "slab")
F32 = jnp.float32
BF16 = jnp.bfloat16
GROWS = 2304
HALF = GROWS // 2
OUT_AT = 4 * HID
IN_AT = OUT_AT + 4 * 24

VELOCITIES = [
    (0, 0, 0),
    (1, 0, 0),
    (-1, 0, 0),
    (0, 1, 0),
    (0, -1, 0),
    (0, 0, 1),
    (0, 0, -1),
    (1, 1, 0),
    (-1, -1, 0),
    (1, -1, 0),
    (-1, 1, 0),
    (1, 0, 1),
    (-1, 0, -1),
    (1, 0, -1),
    (-1, 0, 1),
    (0, 1, 1),
    (0, -1, -1),
    (0, 1, -1),
    (0, -1, 1),
]
OPPOSITE = [0, 2, 1, 4, 3, 6, 5, 8, 7, 10, 9, 12, 11, 14, 13, 16, 15, 18, 17]


def members(face):
    sign = 1 if face % 2 == 0 else -1
    return [q for q in range(Q) if VELOCITIES[q][face // 2] == sign]


def iota(rows, dim):
    return lax.broadcasted_iota(jnp.int32, (rows, 128), dim)


def roll(value, shift, axis):
    shift %= value.shape[axis]
    return value if shift == 0 else pltpu.roll(value, shift, axis)


def shifted(v, velocity):
    cx, cy, cz = velocity
    lane = iota(ROWS, 1)
    if cz:
        v = jnp.where(lane & 15 == (0 if cz == 1 else 15), roll(v, -15 * cz, 1), roll(v, cz, 1))
    if cy:
        t = roll(v, 16 * cy, 1)
        swapped = jnp.where(iota(ROWS, 0) & 1 == 1, roll(t, 1, 0), roll(t, -1, 0))
        v = jnp.where(lane >> 4 == (0 if cy == 1 else 7), swapped, t)
    if cx:
        v = roll(v, 2 * cx, 0)
    return v


def corner(q):
    row, lane = iota(ROWS, 0), iota(ROWS, 1)
    coords = [row >> 1, (row & 1) * 8 + (lane >> 4), lane & 15]
    mask = None
    for axis in range(3):
        c = VELOCITIES[q][axis]
        if c:
            here = coords[axis] == (0 if c == 1 else 15)
            mask = here if mask is None else mask & here
    return mask


def is_edge(q):
    return sum(abs(c) for c in VELOCITIES[q]) == 2


def pack_faces(src, put_x, put_y, put_z):
    lane16, lane32 = iota(16, 1), iota(ROWS, 1)
    for f in (0, 1):
        for i, q in enumerate(members(f)):
            for r in (0, 1):
                put_x(f, r, i, src[q, pl.ds((30 if f == 0 else 0) + r, 1), :])
    for f in (2, 3):
        acc = jnp.zeros((16, 128), F32)
        for i, q in enumerate(members(f)):
            v = src[q, pl.ds(1 if f == 2 else 0, 16, stride=2), :]
            v = roll(v, 16 * i - (112 if f == 2 else 0), 1)
            acc = jnp.where(lane16 >> 4 == i, v, acc)
        put_y(f - 2, acc)
    acc = jnp.zeros((ROWS, 128), F32)
    for f in (4, 5):
        for i, q in enumerate(members(f)):
            slot = i if f == 4 else 8 + i
            v = roll(src[q], slot - (15 if f == 4 else 0), 1)
            acc = jnp.where(lane32 & 15 == slot, v, acc)
    put_z(acc)


def unpack_faces(dst, get_x, y_ref, z, add):
    lane16, lane32 = iota(16, 1), iota(ROWS, 1)
    for f in (0, 1):
        for i, q in enumerate(members(f)):
            for r in (0, 1):
                at = pl.ds((30 if f == 0 else 0) + r, 1)
                v = get_x(f, r, i)
                dst[q, at, :] = dst[q, at, :] + v if add else v
    for f in (2, 3):
        packed = y_ref[f - 2]
        for i, q in enumerate(members(f)):
            at = pl.ds(1 if f == 2 else 0, 16, stride=2)
            v = roll(packed, (112 if f == 2 else 0) - 16 * i, 1)
            old = dst[q, at, :]
            new = old + v if add else v
            dst[q, at, :] = jnp.where(lane16 >> 4 == (7 if f == 2 else 0), new, old)
    for f in (4, 5):
        for i, q in enumerate(members(f)):
            v = roll(z, 15 - i if f == 4 else -(8 + i), 1)
            old = dst[q]
            new = old + v if add else v
            dst[q] = jnp.where(lane32 & 15 == (15 if f == 4 else 0), new, old)


def picked(value, index):
    return jnp.take_along_axis(value, index, axis=1)


class Tables:
    def __init__(self, place, source, level, quadrant):
        self.place, self.source, self.level, self.quadrant = place, source, level, quadrant

    def block(self):
        return self.place[0]

    def distance(self, face):
        d = self.source[face, self.block()] - self.block()
        return jnp.where(d < 0, d + NB, d)


def level_of(info, f):
    return info.level[0, f ^ 1] == 1


def quadrant_of(info, f):
    r = info.quadrant[0, f ^ 1]
    return r >> 1, r & 1


def refine_x(info, x):
    lane = iota(8, 1)
    for f in (0, 1):
        fine = level_of(info, f)
        qr, qc = quadrant_of(info, f)
        rows = [x[f, 0], x[f, 1]]
        source = jnp.where(qr == 0, rows[0], rows[1])
        for r in (0, 1):
            index = (r * 4 + (lane >> 5)) * 16 + qc * 8 + ((lane & 15) >> 1)
            x[f, r] = jnp.where(fine, picked(source, index), rows[r])


def refine_y(info, y):
    lane = iota(8, 1)
    for f in (2, 3):
        fine = level_of(info, f)
        qr, qc = quadrant_of(info, f)
        whole = y[f - 2]
        source = jnp.where(qr == 0, whole[:8], whole[8:])
        v = picked(source, (lane >> 4) * 16 + qc * 8 + ((lane & 15) >> 1))
        for d in (0, 1):
            at = pl.ds(d, 8, stride=2)
            y[f - 2, at, :] = jnp.where(fine, v, y[f - 2, at, :])


def refine_z(info, z_two):
    lane = iota(8, 1)
    for f in (4, 5):
        z = z_two.at[f - 4]
        fine = level_of(info, f)
        qr, qc = quadrant_of(info, f)
        parts = {(h, p): z[pl.ds(16 * h + p, 8, stride=2), :] for h in (0, 1) for p in (0, 1)}
        halves = [jnp.where(qc == 0, parts[h, 0], parts[h, 1]) for h in (0, 1)]
        source = jnp.where(qr == 0, halves[0], halves[1])
        for p in (0, 1):
            v = picked(source, (p * 4 + (lane >> 5)) * 16 + (lane & 15))
            for d in (0, 1):
                at = pl.ds(2 * d + p, 8, stride=4)
                z[at, :] = jnp.where(fine, v, z[at, :])
    return jnp.where(iota(ROWS, 1) & 15 < 8, z_two[0], z_two[1])


def gather_x(info, x):
    lane = iota(8, 1)
    index = (2 * ((lane >> 4) & 3)) * 16 + 2 * (lane & 7)
    for f in (0, 1):
        fine = level_of(info, f)
        qr, qc = quadrant_of(info, f)
        rows = [x[f, 0], x[f, 1]]
        sums = []
        for v in rows:
            v = v + roll(v, -1, 1)
            v = v + roll(v, -16, 1)
            sums.append(picked(v, index))
        v = jnp.where(lane < 64, sums[0], sums[1])
        v = jnp.where((lane & 15) >> 3 == qc, v, 0.0)
        for r in (0, 1):
            x[f, r] = jnp.where(fine, jnp.where(qr == r, v, 0.0), rows[r])


def gather_y(info, y):
    lane = iota(8, 1)
    index = (lane >> 4) * 16 + 2 * (lane & 7)
    for f in (2, 3):
        fine = level_of(info, f)
        qr, qc = quadrant_of(info, f)
        v = y[f - 2, pl.ds(0, 8, stride=2), :] + y[f - 2, pl.ds(1, 8, stride=2), :]
        v = picked(v + roll(v, -1, 1), index)
        v = jnp.where((lane & 15) >> 3 == qc, v, 0.0)
        for h in (0, 1):
            at = pl.ds(8 * h, 8)
            y[f - 2, at, :] = jnp.where(fine, jnp.where(qr == h, v, 0.0), y[f - 2, at, :])


def gather_z(info, z_two):
    lane = iota(8, 1)
    index = (2 * ((lane >> 4) & 3)) * 16 + (lane & 15)
    for f in (4, 5):
        z = z_two.at[f - 4]
        fine = level_of(info, f)
        qr, qc = quadrant_of(info, f)
        sums = []
        for p in (0, 1):
            v = z[pl.ds(p, 8, stride=4), :] + z[pl.ds(2 + p, 8, stride=4), :]
            sums.append(picked(v + roll(v, -16, 1), index))
        v = jnp.where(lane < 64, sums[0], sums[1])
        for h in (0, 1):
            for p in (0, 1):
                at = pl.ds(16 * h + p, 8, stride=2)
                here = (qr == h) & (qc == p)
                z[at, :] = jnp.where(fine, jnp.where(here, v, 0.0), z[at, :])
    return jnp.where(iota(ROWS, 1) & 15 < 8, z_two[0], z_two[1])


def choose_x(info, face, got, kind):
    swapped, x_got, z_got, far, passed = got
    d = info.distance(face)
    even = info.block() & 1 == 0

    def at(distance):
        return jnp.where(even, distance % NB, -distance % NB)

    cases = [
        (at(1), swapped, 0),
        (at(-2), x_got, 0),
        (at(-1), x_got, 64),
        (at(3), passed, 0),
        (at(2), passed, 64),
        (at(-3), far, 0),
    ]
    return lambda f, r: sum_where(
        [
            (d == spot, ref[pl.ds(start + 8 * (kind * 4 + f * 2 + r), 8), :])
            for spot, ref, start in cases
        ]
    )


def choose_z(info, got, kind):
    direct = got[2][pl.ds(32 * kind, 32), :]
    passed = got[4][pl.ds(128 + 32 * kind, 32), :]
    even = info.block() & 1 == 0
    return jnp.where(even, direct, passed), jnp.where(even, passed, direct)


def sum_where(cases):
    total = jnp.zeros((8, 128), F32)
    for condition, value in cases:
        total = jnp.where(condition, value, total)
    return total


def stream_back(info, bar, local, xs, sends, work, y_two, z_two):
    for q in range(Q):
        v = bar[q]
        if is_edge(q):
            v = jnp.where(corner(q), 0.0, v)
        work[q] = shifted(v, tuple(-c for c in VELOCITIES[q]))
    x_four = xs.at[1]
    x_four[...] = jnp.zeros(x_four.shape, F32)

    def put_x(f, r, i, v):
        x_four[f, r, pl.ds(i, 1), :] = v

    def put_y(f, v):
        y_two[f] = v

    def put_z(v):
        z_two[0] = v
        z_two[1] = v

    pack_faces(work, put_x, put_y, put_z)
    gather_x(info, x_four)
    gather_y(info, y_two)
    sends[pl.ds(160, 32), :] = gather_z(info, z_two)
    sends[pl.ds(32, 32), :] = xs[1].reshape(32, 128)
    sends[pl.ds(96, 32), :] = y_two[...].reshape(32, 128)
    row, lane = iota(ROWS, 0), iota(ROWS, 1)
    coords = [row >> 1, (row & 1) * 8 + (lane >> 4), lane & 15]
    for q in range(Q):
        v = work[q]
        leaving = None
        for axis in range(3):
            c = VELOCITIES[q][axis]
            if c:
                here = coords[axis] == (15 if c == 1 else 0)
                leaving = here if leaving is None else leaving | here
        if leaving is not None:
            v = jnp.where(leaving, 0.0, v)
        if is_edge(q):
            v = v + jnp.where(corner(OPPOSITE[q]), bar[OPPOSITE[q]], 0.0)
        local[q] = v


def send_post(post, xs, sends):
    x_four = xs.at[0]
    x_four[...] = jnp.zeros(x_four.shape, F32)

    def put_x(f, r, i, v):
        x_four[f, r, pl.ds(i, 1), :] = v

    def put_y(f, v):
        sends[pl.ds(64 + 16 * f, 16), :] = v

    def put_z(v):
        sends[pl.ds(128, 32), :] = v

    pack_faces(post, put_x, put_y, put_z)
    sends[pl.ds(0, 32), :] = xs[0].reshape(32, 128)


def stream(info, post, got, out, work, x_four, y_two, z_two):
    swapped = got[0]
    for f in (0, 1):
        pick = choose_x(info, f ^ 1, got, 0)
        for r in (0, 1):
            x_four[f, r] = pick(f, r)
    refine_x(info, x_four)
    y_two[0] = swapped[pl.ds(64, 16), :]
    y_two[1] = swapped[pl.ds(80, 16), :]
    refine_y(info, y_two)
    z_two[0], z_two[1] = choose_z(info, got, 0)
    z = refine_z(info, z_two)
    work[...] = post[...]
    unpack_faces(work, lambda f, r, i: x_four[f, r, pl.ds(i, 1), :], y_two, z, False)
    for q in range(Q):
        v = shifted(work[q], VELOCITIES[q])
        if is_edge(q):
            v = jnp.where(corner(q), post[OPPOSITE[q]], v)
        out[q] = v


def take_back(info, bar, got, x_four, y_two):
    swapped = got[0]
    for f in (0, 1):
        pick = choose_x(info, f, got, 1)
        for r in (0, 1):
            x_four[f, r] = pick(f, r)
    y_two[0] = swapped[pl.ds(96, 16), :]
    y_two[1] = swapped[pl.ds(112, 16), :]
    below, above = choose_z(info, got, 1)
    z = jnp.where(iota(ROWS, 1) & 15 < 8, above, below)
    unpack_faces(bar, lambda f, r, i: x_four[f, r, pl.ds(i, 1), :], y_two, z, True)


def dot(a, b, ca=1, cb=0):
    return lax.dot_general(a, b, (((ca,), (cb,)), ((), ())), preferred_element_type=F32)


def cells_of(ref, step):
    parts = [
        ref[:, pl.ds(step * TILES + j, 1), :].reshape(Q, 128) for j in range(TILES)
    ]
    return jnp.concatenate(parts, axis=1)


def put_cells(ref, step, value):
    for j in range(TILES):
        ref[:, pl.ds(step * TILES + j, 1), :] = value[:, j * 128 : (j + 1) * 128].reshape(Q, 1, 128)


def span(step):
    return pl.ds(step * CHUNK, CHUNK)


def forward(x, w_in_t, w_mid, w_out):
    xb = x.astype(BF16)
    h0 = jnp.tanh(dot(w_in_t, xb, 0, 0)).astype(BF16)
    h1 = jnp.tanh(dot(w_mid, h0)).astype(BF16)
    return h0, h1, x + dot(w_out, h1)


def slope(h):
    h = h.astype(F32)
    return 1.0 - h * h


def signals(pbar, h0, h1, w_mid_t, w_out):
    e = pbar.astype(BF16)
    a1 = (dot(w_out, e, 0, 0) * slope(h1)).astype(BF16)
    a0 = (dot(w_mid_t, a1) * slope(h0)).astype(BF16)
    return e, a1, a0


class Copies:
    def __init__(self, sems):
        self.sems, self.made = sems, []

    def start(self, source, target):
        copy = pltpu.make_async_copy(source, target, self.sems.at[len(self.made)])
        copy.start()
        self.made.append(copy)
        return copy

    def wait(self):
        for copy in self.made:
            copy.wait()


def put_grads(grads, x, e, h0, h1, a0, a1, more):
    def put(at, rows, value):
        for j in range(4):
            spot = pl.ds(at + j * (HID if rows == HID else 24), rows)
            v = value[:, j * 128 : (j + 1) * 128]
            grads[spot, :] = v if more is None else more[spot, :] + v

    put(0, HID, dot(a1[...], h0[...], 1, 1))
    put(OUT_AT, Q, dot(e[...], h1[...], 1, 1))
    put(IN_AT, Q, dot(x[...], a0[...], 1, 1))
    if more is None:
        rest = GROWS - IN_AT - 96
        grads[pl.ds(IN_AT + 96, rest), :] = jnp.zeros((rest, 128), F32)


def first_kernel(place, source_far, level_far, quadrant_far, f0_far, cot_far, w_in_far, w_mid_far,
                 w_out_far, post, local, sends, xs, h0_far, h1_far,
                 source, level, quadrant, f0, cot, w_in_t, w_mid, w_out, h0, h1, work, y_two, z_two,
                 sems, out_sems):
    info = Tables(place, source, level, quadrant)
    copies = Copies(sems)
    for far, near in ((cot_far, cot), (source_far, source), (level_far, level),
                      (quadrant_far, quadrant), (f0_far, f0), (w_in_far, w_in_t),
                      (w_mid_far, w_mid), (w_out_far, w_out)):
        copies.start(far, near)
    for copy in copies.made[:4]:
        copy.wait()
    stream_back(info, cot, local, xs, sends, work, y_two, z_two)
    for copy in copies.made[4:]:
        copy.wait()
    copies = Copies(out_sems)
    for step in range(CHUNKS):
        a, b, out = forward(cells_of(f0, step), w_in_t[...], w_mid[...], w_out[...])
        h0[:, span(step)] = a
        copies.start(h0.at[:, span(step)], h0_far.at[:, span(step)])
        h1[:, span(step)] = b
        copies.start(h1.at[:, span(step)], h1_far.at[:, span(step)])
        put_cells(post, step, out)
    send_post(post, xs, sends)
    copies.wait()


def second_kernel(place, source, level, quadrant, post1, local2, swapped, x_got, z_got, far, passed,
                  w_in_t, w_mid, w_mid_t, w_out, post, local, sends, xs, grads_far,
                  grads, x, e, h0, h1, a0, a1, f1, pbar, fbar, work, x_four, y_two, z_two, sem):
    info = Tables(place, source, level, quadrant)
    got = (swapped, x_got, z_got, far, passed)
    stream(info, post1, got, f1, work, x_four, y_two, z_two)
    pbar[...] = local2[...]
    take_back(info, pbar, got, x_four, y_two)
    for step in range(CHUNKS):
        at = span(step)
        f = cells_of(f1, step)
        h0_now, h1_now, out = forward(f, w_in_t[...], w_mid[...], w_out[...])
        put_cells(post, step, out)
        bar = cells_of(pbar, step)
        e_now, a1_now, a0_now = signals(bar, h0_now, h1_now, w_mid_t[...], w_out[...])
        put_cells(fbar, step, bar + dot(w_in_t[...], a0_now))
        x[:, at] = f.astype(BF16)
        e[:, at] = e_now
        h0[:, at] = h0_now
        h1[:, at] = h1_now
        a1[:, at] = a1_now
        a0[:, at] = a0_now
    put_grads(grads, x, e, h0, h1, a0, a1, None)
    copies = Copies(sem)
    copies.start(grads, grads_far)
    send_post(post, xs, sends)
    stream_back(info, fbar, local, xs, sends, work, y_two, z_two)
    copies.wait()


def third_kernel(place, source, level, quadrant, f0, local1, swapped, x_got, z_got, far, passed,
                 w_in_t, w_mid_t, w_out, grads2_far, h0_far, h1_far,
                 grads, fbar, pbar, h0, h1, a0, a1, x, e, x_four, y_two, sems):
    info = Tables(place, source, level, quadrant)
    copies = Copies(sems)
    for step in range(CHUNKS):
        for hbm, near in ((h1_far, h1), (h0_far, h0)):
            copies.start(hbm.at[:, span(step)], near.at[:, span(step)])
    copies.start(grads2_far, grads)
    pbar[...] = local1[...]
    take_back(info, pbar, (swapped, x_got, z_got, far, passed), x_four, y_two)
    for step in range(CHUNKS):
        at = span(step)
        for copy in copies.made[2 * step : 2 * step + 2]:
            copy.wait()
        bar = cells_of(pbar, step)
        e_now, a1_now, a0_now = signals(bar, h0[:, at], h1[:, at], w_mid_t[...], w_out[...])
        put_cells(fbar, step, bar + dot(w_in_t[...], a0_now))
        x[:, at] = cells_of(f0, step).astype(BF16)
        e[:, at] = e_now
        a1[:, at] = a1_now
        a0[:, at] = a0_now
    copies.made[-1].wait()
    put_grads(grads, x, e, h0, h1, a0, a1, grads)


def final_kernel(place, source, level, quadrant, post2, swapped, x_got, z_got, far, passed,
                 out, work, x_four, y_two, z_two):
    info = Tables(place, source, level, quadrant)
    stream(info, post2, (swapped, x_got, z_got, far, passed), out, work, x_four, y_two, z_two)


def add_kernel(place, grads, arrived, mine):
    half = pl.ds(pl.multiple_of((place[0] & 1) * HALF, HALF), HALF)
    mine[...] = grads[half, :] + arrived[...]


def unpack_kernel(place, mine, other, g_in, g_mid, g_out, whole):
    scale = float(NB * NZ * CELLS) ** -0.5
    core = place[0] & 1
    whole[pl.ds(pl.multiple_of(core * HALF, HALF), HALF), :] = mine[...]
    whole[pl.ds(pl.multiple_of((1 - core) * HALF, HALF), HALF), :] = other[...]
    for j in range(4):
        cols = pl.ds(j * 128, 128)
        g_mid[:, cols] = whole[pl.ds(j * HID, HID), :] * scale
        g_out[:, cols] = whole[pl.ds(OUT_AT + 24 * j, Q), :] * scale
        g_in[:, cols] = whole[pl.ds(IN_AT + 24 * j, Q), :] * scale


BLOCK = (Q, ROWS, 128)
HIDDEN = (HID, CELLS)
THIN = (Q, CELLS)
SENDS = (192, 128)
X_TWO = (2, 2, 2, 8, 128)
FACES = [(2, 2, 8, 128), (2, 16, 128), (2, ROWS, 128)]


def run(kernel, tables, args, outs, scratch, mflops, megabytes, hbm=()):
    def shape(s):
        return jax.ShapeDtypeStruct(s, F32) if isinstance(s, tuple) else s

    def buffer(s):
        return pltpu.VMEM(s, F32) if isinstance(s, tuple) else s

    def out_spec(s):
        far = not isinstance(s, (tuple, jax.ShapeDtypeStruct))
        return pl.BlockSpec(memory_space=pltpu.HBM if far else pltpu.VMEM)

    args = list(args)
    in_specs = [pl.BlockSpec(memory_space=pltpu.SMEM)] * len(tables)
    for i in range(len(args)):
        if i in hbm:
            args[i] = pltpu.with_memory_space_constraint(args[i], pltpu.HBM)
        in_specs.append(pl.BlockSpec(memory_space=pltpu.HBM if i in hbm else pltpu.VMEM))
    return pl.pallas_call(
        kernel,
        out_shape=[shape(s) for s in outs],
        in_specs=in_specs,
        out_specs=[out_spec(s) for s in outs],
        scratch_shapes=[buffer(s) for s in scratch],
        compiler_params=pltpu.CompilerParams(vmem_limit_bytes=megabytes << 20),
        cost_estimate=pl.CostEstimate(
            flops=mflops * 1000000, bytes_accessed=1 << 20, transcendentals=0
        ),
    )(*tables, *args)


def send(value, target):
    pairs = [
        (b * NZ + z, nb % NB * NZ + nz % NZ)
        for b in range(NB)
        for z in range(NZ)
        for nb, nz in [target(b, z)]
    ]
    return lax.ppermute(value, AXES, pairs)


def exchange(sends, xs):
    xs = xs.reshape(64, 128)
    swapped = send(sends, lambda b, z: (b ^ 1, z))
    far = send(xs, lambda b, z: (b - 3 if b % 2 == 0 else b + 3, z))
    x_got = send(
        jnp.concatenate([xs, swapped[:64]]),
        lambda b, z: (b + 2 if b % 2 == 0 else b - 2, z),
    )
    z_got = send(
        jnp.concatenate([sends[128:], swapped[128:]]),
        lambda b, z: (b, z + 1 if b % 2 == 0 else z - 1),
    )
    x_got, z_got, far = lax.optimization_barrier((x_got, z_got, far))
    passed = send(jnp.concatenate([x_got, z_got[64:]]), lambda b, z: (b ^ 1, z))
    return swapped, x_got, z_got, far, passed


def total_over_devices(grads, place, beside):
    def other_core(v):
        return send(v, lambda b, z: (b ^ 1, z))

    halves = grads.reshape(2, HALF, 128)
    given = lax.dynamic_index_in_dim(halves, 1 - place[0] % 2, 0, keepdims=False)
    (mine,) = run(add_kernel, [place], [grads, other_core(given)], [(HALF, 128)], [], 10, 8)
    mine = mine.reshape(64, 1, HALF * 2)
    mine = lax.all_to_all(mine, CHIPS, 0, 0, tiled=True).sum(axis=0, keepdims=True)
    mine = jnp.broadcast_to(mine, (64, 1, HALF * 2))
    mine = lax.all_to_all(mine, CHIPS, 0, 0, tiled=True).reshape(HALF, 128)
    other, beside = lax.optimization_barrier((other_core(mine), beside))
    return mine, other, beside


def shards(populations, w_in, w_mid, w_out, cotangent, face_source, face_level, face_quadrant):
    f0 = populations.reshape(BLOCK)
    cot = cotangent.reshape(BLOCK)
    w_in_t = w_in.T
    w_mid = w_mid[0]
    w_mid_t = w_mid.T
    place = lax.axis_index(BLOCKS).astype(jnp.int32).reshape(1)
    tables = [place, face_source.T, face_level[0], face_quadrant[0]]
    hidden = pltpu.HBM(HIDDEN, BF16)
    thin = jax.ShapeDtypeStruct(THIN, BF16)
    grad = (GROWS, 128)
    near = pltpu.VMEM(HIDDEN, BF16)
    near_thin = pltpu.VMEM(THIN, BF16)
    sems = pltpu.SemaphoreType.DMA

    post1, local2, *sends, h0, h1 = run(
        first_kernel, tables[:1], [*tables[1:], f0, cot, w_in_t, w_mid, w_out],
        [BLOCK, BLOCK, SENDS, X_TWO, hidden, hidden],
        [pltpu.SMEM((4, NB), jnp.int32), pltpu.SMEM((1, 6), jnp.int32),
         pltpu.SMEM((1, 6), jnp.int32),
         BLOCK, BLOCK, pltpu.VMEM((Q, HID), BF16), pltpu.VMEM((HID, HID), BF16),
         pltpu.VMEM((Q, HID), BF16), near, near, BLOCK, *FACES[1:], sems((8,)),
         sems((2 * CHUNKS,))],
        4000, 32, range(8),
    )
    got = exchange(*sends)
    post2, local1, *sends, grads2 = run(
        second_kernel, tables, [post1, local2, *got, w_in_t, w_mid, w_mid_t, w_out],
        [BLOCK, BLOCK, SENDS, X_TWO, pltpu.HBM(grad, F32)],
        [grad, near_thin, near_thin, *[near] * 4, *[BLOCK] * 4, *FACES, sems((1,))],
        14000, 32,
    )
    got = exchange(*sends)
    grads, fbar0 = run(
        third_kernel, tables, [f0, local1, *got, w_in_t, w_mid_t, w_out, grads2, h0, h1],
        [grad, BLOCK],
        [BLOCK, *[near] * 4, near_thin, near_thin, *FACES[:2], sems((2 * CHUNKS + 1,))],
        8000, 32, (10, 11, 12),
    )
    post2, grads = lax.optimization_barrier((post2, grads))
    (final,) = run(final_kernel, tables, [post2, *got], [BLOCK], [BLOCK, *FACES], 500, 8)
    mine, other, final = total_over_devices(grads, place, final)
    g_in, g_mid, g_out = run(
        unpack_kernel, [place], [mine, other], [(Q, HID), (HID, HID), (Q, HID)], [grad], 10, 8
    )
    whole = (Q, 1, 1, CELLS)
    return final.reshape(whole), fbar0.reshape(whole), g_in.T, g_mid[None], g_out


def solution(mesh):
    cells = P(None, "slab", BLOCKS, None)
    local = P("slab", BLOCKS, None)
    split = Mesh(mesh.devices.reshape(NX, NX, 2, NZ), AXES)
    return jax.shard_map(
        shards,
        mesh=split,
        in_specs=(cells, P(), P(), P(), cells, P(), local, local),
        out_specs=(cells, cells, P(), P(), P()),
        check_vma=False,
    )
```

```python
import jax
import jax.numpy as jnp
from jax import lax
from jax.experimental import pallas as pl
from jax.experimental.pallas import tpu as pltpu
from jax.sharding import Mesh
from jax.sharding import PartitionSpec as P

Q = 19
HID = 512
CELLS = 4096
ROWS = 32
CHUNK = 1024
TILES = CHUNK // 128
CHUNKS = CELLS // CHUNK
NB = 32
NZ = 4
NX = 4
BLOCKS = ("bx", "by", "core")
AXES = ("bx", "by", "core", "slab")
CHIPS = ("bx", "by", "slab")
F32 = jnp.float32
BF16 = jnp.bfloat16
GROWS = 2304
HALF = GROWS // 2
OUT_AT = 4 * HID
IN_AT = OUT_AT + 4 * 24

VELOCITIES = [
    (0, 0, 0),
    (1, 0, 0),
    (-1, 0, 0),
    (0, 1, 0),
    (0, -1, 0),
    (0, 0, 1),
    (0, 0, -1),
    (1, 1, 0),
    (-1, -1, 0),
    (1, -1, 0),
    (-1, 1, 0),
    (1, 0, 1),
    (-1, 0, -1),
    (1, 0, -1),
    (-1, 0, 1),
    (0, 1, 1),
    (0, -1, -1),
    (0, 1, -1),
    (0, -1, 1),
]
OPPOSITE = [0, 2, 1, 4, 3, 6, 5, 8, 7, 10, 9, 12, 11, 14, 13, 16, 15, 18, 17]


def members(face):
    sign = 1 if face % 2 == 0 else -1
    return [q for q in range(Q) if VELOCITIES[q][face // 2] == sign]


def iota(rows, dim):
    return lax.broadcasted_iota(jnp.int32, (rows, 128), dim)


def roll(value, shift, axis):
    shift %= value.shape[axis]
    return value if shift == 0 else pltpu.roll(value, shift, axis)


def shifted(v, velocity):
    cx, cy, cz = velocity
    lane = iota(ROWS, 1)
    if cz:
        v = jnp.where(lane & 15 == (0 if cz == 1 else 15), roll(v, -15 * cz, 1), roll(v, cz, 1))
    if cy:
        t = roll(v, 16 * cy, 1)
        swapped = jnp.where(iota(ROWS, 0) & 1 == 1, roll(t, 1, 0), roll(t, -1, 0))
        v = jnp.where(lane >> 4 == (0 if cy == 1 else 7), swapped, t)
    if cx:
        v = roll(v, 2 * cx, 0)
    return v


def corner(q):
    row, lane = iota(ROWS, 0), iota(ROWS, 1)
    coords = [row >> 1, (row & 1) * 8 + (lane >> 4), lane & 15]
    mask = None
    for axis in range(3):
        c = VELOCITIES[q][axis]
        if c:
            here = coords[axis] == (0 if c == 1 else 15)
            mask = here if mask is None else mask & here
    return mask


def is_edge(q):
    return sum(abs(c) for c in VELOCITIES[q]) == 2


def pack_faces(src, put_x, put_y, put_z):
    lane16, lane32 = iota(16, 1), iota(ROWS, 1)
    for f in (0, 1):
        for i, q in enumerate(members(f)):
            for r in (0, 1):
                put_x(f, r, i, src[q, pl.ds((30 if f == 0 else 0) + r, 1), :])
    for f in (2, 3):
        acc = jnp.zeros((16, 128), F32)
        for i, q in enumerate(members(f)):
            v = src[q, pl.ds(1 if f == 2 else 0, 16, stride=2), :]
            v = roll(v, 16 * i - (112 if f == 2 else 0), 1)
            acc = jnp.where(lane16 >> 4 == i, v, acc)
        put_y(f - 2, acc)
    acc = jnp.zeros((ROWS, 128), F32)
    for f in (4, 5):
        for i, q in enumerate(members(f)):
            slot = i if f == 4 else 8 + i
            v = roll(src[q], slot - (15 if f == 4 else 0), 1)
            acc = jnp.where(lane32 & 15 == slot, v, acc)
    put_z(acc)


def unpack_faces(dst, get_x, y_ref, z, add):
    lane16, lane32 = iota(16, 1), iota(ROWS, 1)
    for f in (0, 1):
        for i, q in enumerate(members(f)):
            for r in (0, 1):
                at = pl.ds((30 if f == 0 else 0) + r, 1)
                v = get_x(f, r, i)
                dst[q, at, :] = dst[q, at, :] + v if add else v
    for f in (2, 3):
        packed = y_ref[f - 2]
        for i, q in enumerate(members(f)):
            at = pl.ds(1 if f == 2 else 0, 16, stride=2)
            v = roll(packed, (112 if f == 2 else 0) - 16 * i, 1)
            old = dst[q, at, :]
            new = old + v if add else v
            dst[q, at, :] = jnp.where(lane16 >> 4 == (7 if f == 2 else 0), new, old)
    for f in (4, 5):
        for i, q in enumerate(members(f)):
            v = roll(z, 15 - i if f == 4 else -(8 + i), 1)
            old = dst[q]
            new = old + v if add else v
            dst[q] = jnp.where(lane32 & 15 == (15 if f == 4 else 0), new, old)


def picked(value, index):
    return jnp.take_along_axis(value, index, axis=1)


class Tables:
    def __init__(self, place, source, level, quadrant):
        self.place, self.source, self.level, self.quadrant = place, source, level, quadrant

    def block(self):
        return self.place[0]

    def distance(self, face):
        d = self.source[face, self.block()] - self.block()
        return jnp.where(d < 0, d + NB, d)


def level_of(info, f):
    return info.level[0, f ^ 1] == 1


def quadrant_of(info, f):
    r = info.quadrant[0, f ^ 1]
    return r >> 1, r & 1


def refine_x(info, x):
    lane = iota(8, 1)
    for f in (0, 1):
        fine = level_of(info, f)
        qr, qc = quadrant_of(info, f)
        rows = [x[f, 0], x[f, 1]]
        source = jnp.where(qr == 0, rows[0], rows[1])
        for r in (0, 1):
            index = (r * 4 + (lane >> 5)) * 16 + qc * 8 + ((lane & 15) >> 1)
            x[f, r] = jnp.where(fine, picked(source, index), rows[r])


def refine_y(info, y):
    lane = iota(8, 1)
    for f in (2, 3):
        fine = level_of(info, f)
        qr, qc = quadrant_of(info, f)
        whole = y[f - 2]
        source = jnp.where(qr == 0, whole[:8], whole[8:])
        v = picked(source, (lane >> 4) * 16 + qc * 8 + ((lane & 15) >> 1))
        for d in (0, 1):
            at = pl.ds(d, 8, stride=2)
            y[f - 2, at, :] = jnp.where(fine, v, y[f - 2, at, :])


def refine_z(info, z_two):
    lane = iota(8, 1)
    for f in (4, 5):
        z = z_two.at[f - 4]
        fine = level_of(info, f)
        qr, qc = quadrant_of(info, f)
        parts = {(h, p): z[pl.ds(16 * h + p, 8, stride=2), :] for h in (0, 1) for p in (0, 1)}
        halves = [jnp.where(qc == 0, parts[h, 0], parts[h, 1]) for h in (0, 1)]
        source = jnp.where(qr == 0, halves[0], halves[1])
        for p in (0, 1):
            v = picked(source, (p * 4 + (lane >> 5)) * 16 + (lane & 15))
            for d in (0, 1):
                at = pl.ds(2 * d + p, 8, stride=4)
                z[at, :] = jnp.where(fine, v, z[at, :])
    return jnp.where(iota(ROWS, 1) & 15 < 8, z_two[0], z_two[1])


def gather_x(info, x):
    lane = iota(8, 1)
    index = (2 * ((lane >> 4) & 3)) * 16 + 2 * (lane & 7)
    for f in (0, 1):
        fine = level_of(info, f)
        qr, qc = quadrant_of(info, f)
        rows = [x[f, 0], x[f, 1]]
        sums = []
        for v in rows:
            v = v + roll(v, -1, 1)
            v = v + roll(v, -16, 1)
            sums.append(picked(v, index))
        v = jnp.where(lane < 64, sums[0], sums[1])
        v = jnp.where((lane & 15) >> 3 == qc, v, 0.0)
        for r in (0, 1):
            x[f, r] = jnp.where(fine, jnp.where(qr == r, v, 0.0), rows[r])


def gather_y(info, y):
    lane = iota(8, 1)
    index = (lane >> 4) * 16 + 2 * (lane & 7)
    for f in (2, 3):
        fine = level_of(info, f)
        qr, qc = quadrant_of(info, f)
        v = y[f - 2, pl.ds(0, 8, stride=2), :] + y[f - 2, pl.ds(1, 8, stride=2), :]
        v = picked(v + roll(v, -1, 1), index)
        v = jnp.where((lane & 15) >> 3 == qc, v, 0.0)
        for h in (0, 1):
            at = pl.ds(8 * h, 8)
            y[f - 2, at, :] = jnp.where(fine, jnp.where(qr == h, v, 0.0), y[f - 2, at, :])


def gather_z(info, z_two):
    lane = iota(8, 1)
    index = (2 * ((lane >> 4) & 3)) * 16 + (lane & 15)
    for f in (4, 5):
        z = z_two.at[f - 4]
        fine = level_of(info, f)
        qr, qc = quadrant_of(info, f)
        sums = []
        for p in (0, 1):
            v = z[pl.ds(p, 8, stride=4), :] + z[pl.ds(2 + p, 8, stride=4), :]
            sums.append(picked(v + roll(v, -16, 1), index))
        v = jnp.where(lane < 64, sums[0], sums[1])
        for h in (0, 1):
            for p in (0, 1):
                at = pl.ds(16 * h + p, 8, stride=2)
                here = (qr == h) & (qc == p)
                z[at, :] = jnp.where(fine, jnp.where(here, v, 0.0), z[at, :])
    return jnp.where(iota(ROWS, 1) & 15 < 8, z_two[0], z_two[1])


def choose_x(info, face, got, kind):
    swapped, x_got, z_got, far, passed = got
    d = info.distance(face)
    even = info.block() & 1 == 0

    def at(distance):
        return jnp.where(even, distance % NB, -distance % NB)

    cases = [
        (at(1), swapped, 0),
        (at(-2), x_got, 0),
        (at(-1), x_got, 64),
        (at(3), passed, 0),
        (at(2), passed, 64),
        (at(-3), far, 0),
    ]
    return lambda f, r: sum_where(
        [
            (d == spot, ref[pl.ds(start + 8 * (kind * 4 + f * 2 + r), 8), :])
            for spot, ref, start in cases
        ]
    )


def choose_z(info, got, kind):
    direct = got[2][pl.ds(32 * kind, 32), :]
    passed = got[4][pl.ds(128 + 32 * kind, 32), :]
    even = info.block() & 1 == 0
    return jnp.where(even, direct, passed), jnp.where(even, passed, direct)


def sum_where(cases):
    total = jnp.zeros((8, 128), F32)
    for condition, value in cases:
        total = jnp.where(condition, value, total)
    return total


def stream_back(info, bar, local, xs, sends, work, y_two, z_two):
    for q in range(Q):
        v = bar[q]
        if is_edge(q):
            v = jnp.where(corner(q), 0.0, v)
        work[q] = shifted(v, tuple(-c for c in VELOCITIES[q]))
    x_four = xs.at[1]
    x_four[...] = jnp.zeros(x_four.shape, F32)

    def put_x(f, r, i, v):
        x_four[f, r, pl.ds(i, 1), :] = v

    def put_y(f, v):
        y_two[f] = v

    def put_z(v):
        z_two[0] = v
        z_two[1] = v

    pack_faces(work, put_x, put_y, put_z)
    gather_x(info, x_four)
    gather_y(info, y_two)
    sends[pl.ds(160, 32), :] = gather_z(info, z_two)
    sends[pl.ds(32, 32), :] = xs[1].reshape(32, 128)
    sends[pl.ds(96, 32), :] = y_two[...].reshape(32, 128)
    row, lane = iota(ROWS, 0), iota(ROWS, 1)
    coords = [row >> 1, (row & 1) * 8 + (lane >> 4), lane & 15]
    for q in range(Q):
        v = work[q]
        leaving = None
        for axis in range(3):
            c = VELOCITIES[q][axis]
            if c:
                here = coords[axis] == (15 if c == 1 else 0)
                leaving = here if leaving is None else leaving | here
        if leaving is not None:
            v = jnp.where(leaving, 0.0, v)
        if is_edge(q):
            v = v + jnp.where(corner(OPPOSITE[q]), bar[OPPOSITE[q]], 0.0)
        local[q] = v


def send_post(post, xs, sends):
    x_four = xs.at[0]
    x_four[...] = jnp.zeros(x_four.shape, F32)

    def put_x(f, r, i, v):
        x_four[f, r, pl.ds(i, 1), :] = v

    def put_y(f, v):
        sends[pl.ds(64 + 16 * f, 16), :] = v

    def put_z(v):
        sends[pl.ds(128, 32), :] = v

    pack_faces(post, put_x, put_y, put_z)
    sends[pl.ds(0, 32), :] = xs[0].reshape(32, 128)


def stream(info, post, got, out, work, x_four, y_two, z_two):
    swapped = got[0]
    for f in (0, 1):
        pick = choose_x(info, f ^ 1, got, 0)
        for r in (0, 1):
            x_four[f, r] = pick(f, r)
    refine_x(info, x_four)
    y_two[0] = swapped[pl.ds(64, 16), :]
    y_two[1] = swapped[pl.ds(80, 16), :]
    refine_y(info, y_two)
    z_two[0], z_two[1] = choose_z(info, got, 0)
    z = refine_z(info, z_two)
    work[...] = post[...]
    unpack_faces(work, lambda f, r, i: x_four[f, r, pl.ds(i, 1), :], y_two, z, False)
    for q in range(Q):
        v = shifted(work[q], VELOCITIES[q])
        if is_edge(q):
            v = jnp.where(corner(q), post[OPPOSITE[q]], v)
        out[q] = v


def take_back(info, bar, got, x_four, y_two):
    swapped = got[0]
    for f in (0, 1):
        pick = choose_x(info, f, got, 1)
        for r in (0, 1):
            x_four[f, r] = pick(f, r)
    y_two[0] = swapped[pl.ds(96, 16), :]
    y_two[1] = swapped[pl.ds(112, 16), :]
    below, above = choose_z(info, got, 1)
    z = jnp.where(iota(ROWS, 1) & 15 < 8, above, below)
    unpack_faces(bar, lambda f, r, i: x_four[f, r, pl.ds(i, 1), :], y_two, z, True)


def dot(a, b, ca=1, cb=0):
    return lax.dot_general(a, b, (((ca,), (cb,)), ((), ())), preferred_element_type=F32)


def cells_of(ref, step):
    parts = [
        ref[:, pl.ds(step * TILES + j, 1), :].reshape(Q, 128) for j in range(TILES)
    ]
    return jnp.concatenate(parts, axis=1)


def put_cells(ref, step, value):
    for j in range(TILES):
        ref[:, pl.ds(step * TILES + j, 1), :] = value[:, j * 128 : (j + 1) * 128].reshape(Q, 1, 128)


def span(step):
    return pl.ds(step * CHUNK, CHUNK)


def forward(x, w_in_t, w_mid, w_out):
    xb = x.astype(BF16)
    h0 = jnp.tanh(dot(w_in_t, xb, 0, 0)).astype(BF16)
    h1 = jnp.tanh(dot(w_mid, h0)).astype(BF16)
    return h0, h1, x + dot(w_out, h1)


def slope(h):
    h = h.astype(F32)
    return 1.0 - h * h


def signals(pbar, h0, h1, w_mid_t, w_out):
    e = pbar.astype(BF16)
    a1 = (dot(w_out, e, 0, 0) * slope(h1)).astype(BF16)
    a0 = (dot(w_mid_t, a1) * slope(h0)).astype(BF16)
    return e, a1, a0


class Copies:
    def __init__(self, sems):
        self.sems, self.made = sems, []

    def start(self, source, target):
        copy = pltpu.make_async_copy(source, target, self.sems.at[len(self.made)])
        copy.start()
        self.made.append(copy)
        return copy

    def wait(self):
        for copy in self.made:
            copy.wait()


def put_grads(grads, x, e, h0, h1, a0, a1, more):
    def put(at, rows, value):
        for j in range(4):
            spot = pl.ds(at + j * (HID if rows == HID else 24), rows)
            v = value[:, j * 128 : (j + 1) * 128]
            grads[spot, :] = v if more is None else more[spot, :] + v

    put(0, HID, dot(a1[...], h0[...], 1, 1))
    put(OUT_AT, Q, dot(e[...], h1[...], 1, 1))
    put(IN_AT, Q, dot(x[...], a0[...], 1, 1))
    if more is None:
        rest = GROWS - IN_AT - 96
        grads[pl.ds(IN_AT + 96, rest), :] = jnp.zeros((rest, 128), F32)


def first_kernel(place, source_far, level_far, quadrant_far, f0_far, cot_far, w_in_far, w_mid_far,
                 w_out_far, post, local, sends, xs, h0_far, h1_far,
                 source, level, quadrant, f0, cot, w_in_t, w_mid, w_out, h0, h1, work, y_two, z_two,
                 sems, out_sems):
    info = Tables(place, source, level, quadrant)
    copies = Copies(sems)
    for far, near in ((cot_far, cot), (source_far, source), (level_far, level),
                      (quadrant_far, quadrant), (f0_far, f0), (w_in_far, w_in_t),
                      (w_mid_far, w_mid), (w_out_far, w_out)):
        copies.start(far, near)
    for copy in copies.made[:4]:
        copy.wait()
    stream_back(info, cot, local, xs, sends, work, y_two, z_two)
    for copy in copies.made[4:]:
        copy.wait()
    copies = Copies(out_sems)
    for step in range(CHUNKS):
        a, b, out = forward(cells_of(f0, step), w_in_t[...], w_mid[...], w_out[...])
        h0[:, span(step)] = a
        copies.start(h0.at[:, span(step)], h0_far.at[:, span(step)])
        h1[:, span(step)] = b
        copies.start(h1.at[:, span(step)], h1_far.at[:, span(step)])
        put_cells(post, step, out)
    send_post(post, xs, sends)
    copies.wait()


def second_kernel(place, source, level, quadrant, post1, local2, swapped, x_got, z_got, far, passed,
                  w_in_t, w_mid, w_mid_t, w_out, post, local, sends, xs, grads_far,
                  grads, x, e, h0, h1, a0, a1, f1, pbar, fbar, work, x_four, y_two, z_two, sem):
    info = Tables(place, source, level, quadrant)
    got = (swapped, x_got, z_got, far, passed)
    stream(info, post1, got, f1, work, x_four, y_two, z_two)
    pbar[...] = local2[...]
    take_back(info, pbar, got, x_four, y_two)
    for step in range(CHUNKS):
        at = span(step)
        f = cells_of(f1, step)
        h0_now, h1_now, out = forward(f, w_in_t[...], w_mid[...], w_out[...])
        put_cells(post, step, out)
        bar = cells_of(pbar, step)
        e_now, a1_now, a0_now = signals(bar, h0_now, h1_now, w_mid_t[...], w_out[...])
        put_cells(fbar, step, bar + dot(w_in_t[...], a0_now))
        x[:, at] = f.astype(BF16)
        e[:, at] = e_now
        h0[:, at] = h0_now
        h1[:, at] = h1_now
        a1[:, at] = a1_now
        a0[:, at] = a0_now
    put_grads(grads, x, e, h0, h1, a0, a1, None)
    copies = Copies(sem)
    copies.start(grads, grads_far)
    send_post(post, xs, sends)
    stream_back(info, fbar, local, xs, sends, work, y_two, z_two)
    copies.wait()


def third_kernel(place, source, level, quadrant, f0, local1, swapped, x_got, z_got, far, passed,
                 w_in_t, w_mid_t, w_out, grads2_far, h0_far, h1_far,
                 grads, fbar, pbar, h0, h1, a0, a1, x, e, x_four, y_two, sems):
    info = Tables(place, source, level, quadrant)
    copies = Copies(sems)
    for step in range(CHUNKS):
        for hbm, near in ((h1_far, h1), (h0_far, h0)):
            copies.start(hbm.at[:, span(step)], near.at[:, span(step)])
    copies.start(grads2_far, grads)
    pbar[...] = local1[...]
    take_back(info, pbar, (swapped, x_got, z_got, far, passed), x_four, y_two)
    for step in range(CHUNKS):
        at = span(step)
        for copy in copies.made[2 * step : 2 * step + 2]:
            copy.wait()
        bar = cells_of(pbar, step)
        e_now, a1_now, a0_now = signals(bar, h0[:, at], h1[:, at], w_mid_t[...], w_out[...])
        put_cells(fbar, step, bar + dot(w_in_t[...], a0_now))
        x[:, at] = cells_of(f0, step).astype(BF16)
        e[:, at] = e_now
        a1[:, at] = a1_now
        a0[:, at] = a0_now
    copies.made[-1].wait()
    put_grads(grads, x, e, h0, h1, a0, a1, grads)


def final_kernel(place, source, level, quadrant, post2, swapped, x_got, z_got, far, passed,
                 out, work, x_four, y_two, z_two):
    info = Tables(place, source, level, quadrant)
    stream(info, post2, (swapped, x_got, z_got, far, passed), out, work, x_four, y_two, z_two)


def add_kernel(place, grads, arrived, mine):
    half = pl.ds(pl.multiple_of((place[0] & 1) * HALF, HALF), HALF)
    mine[...] = grads[half, :] + arrived[...]


def unpack_kernel(place, mine, other, g_in, g_mid, g_out, whole):
    scale = float(NB * NZ * CELLS) ** -0.5
    core = place[0] & 1
    whole[pl.ds(pl.multiple_of(core * HALF, HALF), HALF), :] = mine[...]
    whole[pl.ds(pl.multiple_of((1 - core) * HALF, HALF), HALF), :] = other[...]
    for j in range(4):
        cols = pl.ds(j * 128, 128)
        g_mid[:, cols] = whole[pl.ds(j * HID, HID), :] * scale
        g_out[:, cols] = whole[pl.ds(OUT_AT + 24 * j, Q), :] * scale
        g_in[:, cols] = whole[pl.ds(IN_AT + 24 * j, Q), :] * scale


BLOCK = (Q, ROWS, 128)
HIDDEN = (HID, CELLS)
THIN = (Q, CELLS)
SENDS = (192, 128)
X_TWO = (2, 2, 2, 8, 128)
FACES = [(2, 2, 8, 128), (2, 16, 128), (2, ROWS, 128)]


def run(kernel, tables, args, outs, scratch, mflops, megabytes, hbm=()):
    def shape(s):
        return jax.ShapeDtypeStruct(s, F32) if isinstance(s, tuple) else s

    def buffer(s):
        return pltpu.VMEM(s, F32) if isinstance(s, tuple) else s

    def out_spec(s):
        far = not isinstance(s, (tuple, jax.ShapeDtypeStruct))
        return pl.BlockSpec(memory_space=pltpu.HBM if far else pltpu.VMEM)

    args = list(args)
    in_specs = [pl.BlockSpec(memory_space=pltpu.SMEM)] * len(tables)
    for i in range(len(args)):
        if i in hbm:
            args[i] = pltpu.with_memory_space_constraint(args[i], pltpu.HBM)
        in_specs.append(pl.BlockSpec(memory_space=pltpu.HBM if i in hbm else pltpu.VMEM))
    return pl.pallas_call(
        kernel,
        out_shape=[shape(s) for s in outs],
        in_specs=in_specs,
        out_specs=[out_spec(s) for s in outs],
        scratch_shapes=[buffer(s) for s in scratch],
        compiler_params=pltpu.CompilerParams(vmem_limit_bytes=megabytes << 20),
        cost_estimate=pl.CostEstimate(
            flops=mflops * 1000000, bytes_accessed=1 << 20, transcendentals=0
        ),
    )(*tables, *args)


def send(value, target):
    pairs = [
        (b * NZ + z, nb % NB * NZ + nz % NZ)
        for b in range(NB)
        for z in range(NZ)
        for nb, nz in [target(b, z)]
    ]
    return lax.ppermute(value, AXES, pairs)


def exchange(sends, xs):
    def next_chip(b, z):
        return (b + 2 if b % 2 == 0 else b - 2, z)

    swapped = send(sends, lambda b, z: (b ^ 1, z))
    x_got = send(jnp.concatenate([xs.reshape(64, 128), swapped[:64]]), next_chip)
    z_got = send(
        jnp.concatenate([sends[128:], swapped[128:]]),
        lambda b, z: (b, z + 1 if b % 2 == 0 else z - 1),
    )
    far = send(x_got[64:], next_chip)
    passed = send(jnp.concatenate([x_got, z_got[64:]]), lambda b, z: (b ^ 1, z))
    return swapped, x_got, z_got, far, passed


def total_over_devices(grads, place, beside):
    def other_core(v):
        return send(v, lambda b, z: (b ^ 1, z))

    halves = grads.reshape(2, HALF, 128)
    given = lax.dynamic_index_in_dim(halves, 1 - place[0] % 2, 0, keepdims=False)
    (mine,) = run(add_kernel, [place], [grads, other_core(given)], [(HALF, 128)], [], 10, 8)
    mine = mine.reshape(64, 1, HALF * 2)
    mine = lax.all_to_all(mine, CHIPS, 0, 0, tiled=True).sum(axis=0, keepdims=True)
    mine = jnp.broadcast_to(mine, (64, 1, HALF * 2))
    mine = lax.all_to_all(mine, CHIPS, 0, 0, tiled=True).reshape(HALF, 128)
    other, beside = lax.optimization_barrier((other_core(mine), beside))
    return mine, other, beside


def shards(populations, w_in, w_mid, w_out, cotangent, face_source, face_level, face_quadrant):
    f0 = populations.reshape(BLOCK)
    cot = cotangent.reshape(BLOCK)
    w_in_t = w_in.T
    w_mid = w_mid[0]
    w_mid_t = w_mid.T
    place = lax.axis_index(BLOCKS).astype(jnp.int32).reshape(1)
    tables = [place, face_source.T, face_level[0], face_quadrant[0]]
    hidden = pltpu.HBM(HIDDEN, BF16)
    thin = jax.ShapeDtypeStruct(THIN, BF16)
    grad = (GROWS, 128)
    near = pltpu.VMEM(HIDDEN, BF16)
    near_thin = pltpu.VMEM(THIN, BF16)
    sems = pltpu.SemaphoreType.DMA

    post1, local2, *sends, h0, h1 = run(
        first_kernel, tables[:1], [*tables[1:], f0, cot, w_in_t, w_mid, w_out],
        [BLOCK, BLOCK, SENDS, X_TWO, hidden, hidden],
        [pltpu.SMEM((4, NB), jnp.int32), pltpu.SMEM((1, 6), jnp.int32),
         pltpu.SMEM((1, 6), jnp.int32),
         BLOCK, BLOCK, pltpu.VMEM((Q, HID), BF16), pltpu.VMEM((HID, HID), BF16),
         pltpu.VMEM((Q, HID), BF16), near, near, BLOCK, *FACES[1:], sems((8,)),
         sems((2 * CHUNKS,))],
        4000, 32, range(8),
    )
    got = exchange(*sends)
    post2, local1, *sends, grads2 = run(
        second_kernel, tables, [post1, local2, *got, w_in_t, w_mid, w_mid_t, w_out],
        [BLOCK, BLOCK, SENDS, X_TWO, pltpu.HBM(grad, F32)],
        [grad, near_thin, near_thin, *[near] * 4, *[BLOCK] * 4, *FACES, sems((1,))],
        14000, 32,
    )
    got = exchange(*sends)
    grads, fbar0 = run(
        third_kernel, tables, [f0, local1, *got, w_in_t, w_mid_t, w_out, grads2, h0, h1],
        [grad, BLOCK],
        [BLOCK, *[near] * 4, near_thin, near_thin, *FACES[:2], sems((2 * CHUNKS + 1,))],
        8000, 32, (10, 11, 12),
    )
    post2, grads = lax.optimization_barrier((post2, grads))
    (final,) = run(final_kernel, tables, [post2, *got], [BLOCK], [BLOCK, *FACES], 500, 8)
    mine, other, final = total_over_devices(grads, place, final)
    g_in, g_mid, g_out = run(
        unpack_kernel, [place], [mine, other], [(Q, HID), (HID, HID), (Q, HID)], [grad], 10, 8
    )
    whole = (Q, 1, 1, CELLS)
    return final.reshape(whole), fbar0.reshape(whole), g_in.T, g_mid[None], g_out


def solution(mesh):
    cells = P(None, "slab", BLOCKS, None)
    local = P("slab", BLOCKS, None)
    split = Mesh(mesh.devices.reshape(NX, NX, 2, NZ), AXES)
    return jax.shard_map(
        shards,
        mesh=split,
        in_specs=(cells, P(), P(), P(), cells, P(), local, local),
        out_specs=(cells, cells, P(), P(), P()),
        check_vma=False,
    )
```

```python
import jax
import jax.numpy as jnp
from jax import lax
from jax.experimental import pallas as pl
from jax.experimental.pallas import tpu as pltpu
from jax.sharding import Mesh
from jax.sharding import PartitionSpec as P

Q = 19
HID = 512
CELLS = 4096
ROWS = 32
CHUNK = 1024
TILES = CHUNK // 128
CHUNKS = CELLS // CHUNK
NB = 32
NZ = 4
NX = 4
BLOCKS = ("bx", "by", "core")
AXES = ("bx", "by", "core", "slab")
CHIPS = ("bx", "by", "slab")
F32 = jnp.float32
BF16 = jnp.bfloat16
GROWS = 2304
HALF = GROWS // 2
OUT_AT = 4 * HID
IN_AT = OUT_AT + 4 * 24

VELOCITIES = [
    (0, 0, 0),
    (1, 0, 0),
    (-1, 0, 0),
    (0, 1, 0),
    (0, -1, 0),
    (0, 0, 1),
    (0, 0, -1),
    (1, 1, 0),
    (-1, -1, 0),
    (1, -1, 0),
    (-1, 1, 0),
    (1, 0, 1),
    (-1, 0, -1),
    (1, 0, -1),
    (-1, 0, 1),
    (0, 1, 1),
    (0, -1, -1),
    (0, 1, -1),
    (0, -1, 1),
]
OPPOSITE = [0, 2, 1, 4, 3, 6, 5, 8, 7, 10, 9, 12, 11, 14, 13, 16, 15, 18, 17]


def members(face):
    sign = 1 if face % 2 == 0 else -1
    return [q for q in range(Q) if VELOCITIES[q][face // 2] == sign]


def iota(rows, dim):
    return lax.broadcasted_iota(jnp.int32, (rows, 128), dim)


def roll(value, shift, axis):
    shift %= value.shape[axis]
    return value if shift == 0 else pltpu.roll(value, shift, axis)


def shifted(v, velocity):
    cx, cy, cz = velocity
    lane = iota(ROWS, 1)
    if cz:
        v = jnp.where(lane & 15 == (0 if cz == 1 else 15), roll(v, -15 * cz, 1), roll(v, cz, 1))
    if cy:
        t = roll(v, 16 * cy, 1)
        swapped = jnp.where(iota(ROWS, 0) & 1 == 1, roll(t, 1, 0), roll(t, -1, 0))
        v = jnp.where(lane >> 4 == (0 if cy == 1 else 7), swapped, t)
    if cx:
        v = roll(v, 2 * cx, 0)
    return v


def corner(q):
    row, lane = iota(ROWS, 0), iota(ROWS, 1)
    coords = [row >> 1, (row & 1) * 8 + (lane >> 4), lane & 15]
    mask = None
    for axis in range(3):
        c = VELOCITIES[q][axis]
        if c:
            here = coords[axis] == (0 if c == 1 else 15)
            mask = here if mask is None else mask & here
    return mask


def is_edge(q):
    return sum(abs(c) for c in VELOCITIES[q]) == 2


def pack_faces(src, put_x, put_y, put_z):
    lane16, lane32 = iota(16, 1), iota(ROWS, 1)
    for f in (0, 1):
        for i, q in enumerate(members(f)):
            for r in (0, 1):
                put_x(f, r, i, src[q, pl.ds((30 if f == 0 else 0) + r, 1), :])
    for f in (2, 3):
        acc = jnp.zeros((16, 128), F32)
        for i, q in enumerate(members(f)):
            v = src[q, pl.ds(1 if f == 2 else 0, 16, stride=2), :]
            v = roll(v, 16 * i - (112 if f == 2 else 0), 1)
            acc = jnp.where(lane16 >> 4 == i, v, acc)
        put_y(f - 2, acc)
    acc = jnp.zeros((ROWS, 128), F32)
    for f in (4, 5):
        for i, q in enumerate(members(f)):
            slot = i if f == 4 else 8 + i
            v = roll(src[q], slot - (15 if f == 4 else 0), 1)
            acc = jnp.where(lane32 & 15 == slot, v, acc)
    put_z(acc)


def unpack_faces(dst, get_x, y_ref, z, add):
    lane16, lane32 = iota(16, 1), iota(ROWS, 1)
    for f in (0, 1):
        for i, q in enumerate(members(f)):
            for r in (0, 1):
                at = pl.ds((30 if f == 0 else 0) + r, 1)
                v = get_x(f, r, i)
                dst[q, at, :] = dst[q, at, :] + v if add else v
    for f in (2, 3):
        packed = y_ref[f - 2]
        for i, q in enumerate(members(f)):
            at = pl.ds(1 if f == 2 else 0, 16, stride=2)
            v = roll(packed, (112 if f == 2 else 0) - 16 * i, 1)
            old = dst[q, at, :]
            new = old + v if add else v
            dst[q, at, :] = jnp.where(lane16 >> 4 == (7 if f == 2 else 0), new, old)
    for f in (4, 5):
        for i, q in enumerate(members(f)):
            v = roll(z, 15 - i if f == 4 else -(8 + i), 1)
            old = dst[q]
            new = old + v if add else v
            dst[q] = jnp.where(lane32 & 15 == (15 if f == 4 else 0), new, old)


def picked(value, index):
    return jnp.take_along_axis(value, index, axis=1)


class Tables:
    def __init__(self, place, source, level, quadrant):
        self.place, self.source, self.level, self.quadrant = place, source, level, quadrant

    def block(self):
        return self.place[0]

    def distance(self, face):
        d = self.source[face, self.block()] - self.block()
        return jnp.where(d < 0, d + NB, d)


def level_of(info, f):
    return info.level[0, f ^ 1] == 1


def quadrant_of(info, f):
    r = info.quadrant[0, f ^ 1]
    return r >> 1, r & 1


def refine_x(info, x):
    lane = iota(8, 1)
    for f in (0, 1):
        fine = level_of(info, f)
        qr, qc = quadrant_of(info, f)
        rows = [x[f, 0], x[f, 1]]
        source = jnp.where(qr == 0, rows[0], rows[1])
        for r in (0, 1):
            index = (r * 4 + (lane >> 5)) * 16 + qc * 8 + ((lane & 15) >> 1)
            x[f, r] = jnp.where(fine, picked(source, index), rows[r])


def refine_y(info, y):
    lane = iota(8, 1)
    for f in (2, 3):
        fine = level_of(info, f)
        qr, qc = quadrant_of(info, f)
        whole = y[f - 2]
        source = jnp.where(qr == 0, whole[:8], whole[8:])
        v = picked(source, (lane >> 4) * 16 + qc * 8 + ((lane & 15) >> 1))
        for d in (0, 1):
            at = pl.ds(d, 8, stride=2)
            y[f - 2, at, :] = jnp.where(fine, v, y[f - 2, at, :])


def refine_z(info, z_two):
    lane = iota(8, 1)
    for f in (4, 5):
        z = z_two.at[f - 4]
        fine = level_of(info, f)
        qr, qc = quadrant_of(info, f)
        parts = {(h, p): z[pl.ds(16 * h + p, 8, stride=2), :] for h in (0, 1) for p in (0, 1)}
        halves = [jnp.where(qc == 0, parts[h, 0], parts[h, 1]) for h in (0, 1)]
        source = jnp.where(qr == 0, halves[0], halves[1])
        for p in (0, 1):
            v = picked(source, (p * 4 + (lane >> 5)) * 16 + (lane & 15))
            for d in (0, 1):
                at = pl.ds(2 * d + p, 8, stride=4)
                z[at, :] = jnp.where(fine, v, z[at, :])
    return jnp.where(iota(ROWS, 1) & 15 < 8, z_two[0], z_two[1])


def gather_x(info, x):
    lane = iota(8, 1)
    index = (2 * ((lane >> 4) & 3)) * 16 + 2 * (lane & 7)
    for f in (0, 1):
        fine = level_of(info, f)
        qr, qc = quadrant_of(info, f)
        rows = [x[f, 0], x[f, 1]]
        sums = []
        for v in rows:
            v = v + roll(v, -1, 1)
            v = v + roll(v, -16, 1)
            sums.append(picked(v, index))
        v = jnp.where(lane < 64, sums[0], sums[1])
        v = jnp.where((lane & 15) >> 3 == qc, v, 0.0)
        for r in (0, 1):
            x[f, r] = jnp.where(fine, jnp.where(qr == r, v, 0.0), rows[r])


def gather_y(info, y):
    lane = iota(8, 1)
    index = (lane >> 4) * 16 + 2 * (lane & 7)
    for f in (2, 3):
        fine = level_of(info, f)
        qr, qc = quadrant_of(info, f)
        v = y[f - 2, pl.ds(0, 8, stride=2), :] + y[f - 2, pl.ds(1, 8, stride=2), :]
        v = picked(v + roll(v, -1, 1), index)
        v = jnp.where((lane & 15) >> 3 == qc, v, 0.0)
        for h in (0, 1):
            at = pl.ds(8 * h, 8)
            y[f - 2, at, :] = jnp.where(fine, jnp.where(qr == h, v, 0.0), y[f - 2, at, :])


def gather_z(info, z_two):
    lane = iota(8, 1)
    index = (2 * ((lane >> 4) & 3)) * 16 + (lane & 15)
    for f in (4, 5):
        z = z_two.at[f - 4]
        fine = level_of(info, f)
        qr, qc = quadrant_of(info, f)
        sums = []
        for p in (0, 1):
            v = z[pl.ds(p, 8, stride=4), :] + z[pl.ds(2 + p, 8, stride=4), :]
            sums.append(picked(v + roll(v, -16, 1), index))
        v = jnp.where(lane < 64, sums[0], sums[1])
        for h in (0, 1):
            for p in (0, 1):
                at = pl.ds(16 * h + p, 8, stride=2)
                here = (qr == h) & (qc == p)
                z[at, :] = jnp.where(fine, jnp.where(here, v, 0.0), z[at, :])
    return jnp.where(iota(ROWS, 1) & 15 < 8, z_two[0], z_two[1])


def choose_x(info, face, got, kind):
    swapped, x_got, z_got, far, passed = got
    d = info.distance(face)
    even = info.block() & 1 == 0

    def at(distance):
        return jnp.where(even, distance % NB, -distance % NB)

    cases = [
        (at(1), swapped, 0),
        (at(-2), x_got, 0),
        (at(-1), x_got, 64),
        (at(3), passed, 0),
        (at(2), passed, 64),
        (at(-3), far, 0),
    ]
    return lambda f, r: sum_where(
        [
            (d == spot, ref[pl.ds(start + 8 * (kind * 4 + f * 2 + r), 8), :])
            for spot, ref, start in cases
        ]
    )


def choose_z(info, got, kind):
    direct = got[2][pl.ds(32 * kind, 32), :]
    passed = got[4][pl.ds(128 + 32 * kind, 32), :]
    even = info.block() & 1 == 0
    return jnp.where(even, direct, passed), jnp.where(even, passed, direct)


def sum_where(cases):
    total = jnp.zeros((8, 128), F32)
    for condition, value in cases:
        total = jnp.where(condition, value, total)
    return total


def stream_back(info, bar, local, xs, sends, work, y_two, z_two):
    for q in range(Q):
        v = bar[q]
        if is_edge(q):
            v = jnp.where(corner(q), 0.0, v)
        work[q] = shifted(v, tuple(-c for c in VELOCITIES[q]))
    x_four = xs.at[1]
    x_four[...] = jnp.zeros(x_four.shape, F32)

    def put_x(f, r, i, v):
        x_four[f, r, pl.ds(i, 1), :] = v

    def put_y(f, v):
        y_two[f] = v

    def put_z(v):
        z_two[0] = v
        z_two[1] = v

    pack_faces(work, put_x, put_y, put_z)
    gather_x(info, x_four)
    gather_y(info, y_two)
    sends[pl.ds(160, 32), :] = gather_z(info, z_two)
    sends[pl.ds(32, 32), :] = xs[1].reshape(32, 128)
    sends[pl.ds(96, 32), :] = y_two[...].reshape(32, 128)
    row, lane = iota(ROWS, 0), iota(ROWS, 1)
    coords = [row >> 1, (row & 1) * 8 + (lane >> 4), lane & 15]
    for q in range(Q):
        v = work[q]
        leaving = None
        for axis in range(3):
            c = VELOCITIES[q][axis]
            if c:
                here = coords[axis] == (15 if c == 1 else 0)
                leaving = here if leaving is None else leaving | here
        if leaving is not None:
            v = jnp.where(leaving, 0.0, v)
        if is_edge(q):
            v = v + jnp.where(corner(OPPOSITE[q]), bar[OPPOSITE[q]], 0.0)
        local[q] = v


def send_post(post, xs, sends):
    x_four = xs.at[0]
    x_four[...] = jnp.zeros(x_four.shape, F32)

    def put_x(f, r, i, v):
        x_four[f, r, pl.ds(i, 1), :] = v

    def put_y(f, v):
        sends[pl.ds(64 + 16 * f, 16), :] = v

    def put_z(v):
        sends[pl.ds(128, 32), :] = v

    pack_faces(post, put_x, put_y, put_z)
    sends[pl.ds(0, 32), :] = xs[0].reshape(32, 128)


def stream(info, post, got, out, work, x_four, y_two, z_two):
    swapped = got[0]
    for f in (0, 1):
        pick = choose_x(info, f ^ 1, got, 0)
        for r in (0, 1):
            x_four[f, r] = pick(f, r)
    refine_x(info, x_four)
    y_two[0] = swapped[pl.ds(64, 16), :]
    y_two[1] = swapped[pl.ds(80, 16), :]
    refine_y(info, y_two)
    z_two[0], z_two[1] = choose_z(info, got, 0)
    z = refine_z(info, z_two)
    work[...] = post[...]
    unpack_faces(work, lambda f, r, i: x_four[f, r, pl.ds(i, 1), :], y_two, z, False)
    for q in range(Q):
        v = shifted(work[q], VELOCITIES[q])
        if is_edge(q):
            v = jnp.where(corner(q), post[OPPOSITE[q]], v)
        out[q] = v


def take_back(info, bar, got, x_four, y_two):
    swapped = got[0]
    for f in (0, 1):
        pick = choose_x(info, f, got, 1)
        for r in (0, 1):
            x_four[f, r] = pick(f, r)
    y_two[0] = swapped[pl.ds(96, 16), :]
    y_two[1] = swapped[pl.ds(112, 16), :]
    below, above = choose_z(info, got, 1)
    z = jnp.where(iota(ROWS, 1) & 15 < 8, above, below)
    unpack_faces(bar, lambda f, r, i: x_four[f, r, pl.ds(i, 1), :], y_two, z, True)


def dot(a, b, ca=1, cb=0):
    return lax.dot_general(a, b, (((ca,), (cb,)), ((), ())), preferred_element_type=F32)


def cells_of(ref, step):
    parts = [
        ref[:, pl.ds(step * TILES + j, 1), :].reshape(Q, 128) for j in range(TILES)
    ]
    return jnp.concatenate(parts, axis=1)


def put_cells(ref, step, value):
    for j in range(TILES):
        ref[:, pl.ds(step * TILES + j, 1), :] = value[:, j * 128 : (j + 1) * 128].reshape(Q, 1, 128)


def span(step):
    return pl.ds(step * CHUNK, CHUNK)


def forward(x, w_in_t, w_mid, w_out):
    xb = x.astype(BF16)
    h0 = jnp.tanh(dot(w_in_t, xb, 0, 0)).astype(BF16)
    h1 = jnp.tanh(dot(w_mid, h0)).astype(BF16)
    return h0, h1, x + dot(w_out, h1)


def slope(h):
    h = h.astype(F32)
    return 1.0 - h * h


def signals(pbar, h0, h1, w_mid_t, w_out):
    e = pbar.astype(BF16)
    a1 = (dot(w_out, e, 0, 0) * slope(h1)).astype(BF16)
    a0 = (dot(w_mid_t, a1) * slope(h0)).astype(BF16)
    return e, a1, a0


class Copies:
    def __init__(self, sems):
        self.sems, self.made = sems, []

    def start(self, source, target):
        copy = pltpu.make_async_copy(source, target, self.sems.at[len(self.made)])
        copy.start()
        self.made.append(copy)
        return copy

    def wait(self):
        for copy in self.made:
            copy.wait()


def put_grads(grads, x, e, h0, h1, a0, a1, more):
    def put(at, rows, value):
        for j in range(4):
            spot = pl.ds(at + j * (HID if rows == HID else 24), rows)
            v = value[:, j * 128 : (j + 1) * 128]
            grads[spot, :] = v if more is None else more[spot, :] + v

    put(0, HID, dot(a1[...], h0[...], 1, 1))
    put(OUT_AT, Q, dot(e[...], h1[...], 1, 1))
    put(IN_AT, Q, dot(x[...], a0[...], 1, 1))
    if more is None:
        rest = GROWS - IN_AT - 96
        grads[pl.ds(IN_AT + 96, rest), :] = jnp.zeros((rest, 128), F32)


def first_kernel(place, source_far, level_far, quadrant_far, f0_far, cot_far, w_in_far, w_mid_far,
                 w_out_far, post, local, sends, xs, h0_far, h1_far,
                 source, level, quadrant, f0, cot, w_in_t, w_mid, w_out, h0, h1, work, y_two, z_two,
                 sems, out_sems):
    info = Tables(place, source, level, quadrant)
    copies = Copies(sems)
    for far, near in ((cot_far, cot), (source_far, source), (level_far, level),
                      (quadrant_far, quadrant), (f0_far, f0), (w_in_far, w_in_t),
                      (w_mid_far, w_mid), (w_out_far, w_out)):
        copies.start(far, near)
    for copy in copies.made[:4]:
        copy.wait()
    stream_back(info, cot, local, xs, sends, work, y_two, z_two)
    for copy in copies.made[4:]:
        copy.wait()
    copies = Copies(out_sems)
    for step in range(CHUNKS):
        a, b, out = forward(cells_of(f0, step), w_in_t[...], w_mid[...], w_out[...])
        h0[:, span(step)] = a
        copies.start(h0.at[:, span(step)], h0_far.at[:, span(step)])
        h1[:, span(step)] = b
        copies.start(h1.at[:, span(step)], h1_far.at[:, span(step)])
        put_cells(post, step, out)
    send_post(post, xs, sends)
    copies.wait()


def second_kernel(place, source, level, quadrant, post1, local2, swapped, x_got, z_got, far, passed,
                  w_in_t, w_mid, w_mid_t, w_out, post, local, sends, xs, grads_far,
                  grads, x, e, h0, h1, a0, a1, f1, pbar, fbar, work, x_four, y_two, z_two, sem):
    info = Tables(place, source, level, quadrant)
    got = (swapped, x_got, z_got, far, passed)
    stream(info, post1, got, f1, work, x_four, y_two, z_two)
    pbar[...] = local2[...]
    take_back(info, pbar, got, x_four, y_two)
    for step in range(CHUNKS):
        at = span(step)
        f = cells_of(f1, step)
        h0_now, h1_now, out = forward(f, w_in_t[...], w_mid[...], w_out[...])
        put_cells(post, step, out)
        bar = cells_of(pbar, step)
        e_now, a1_now, a0_now = signals(bar, h0_now, h1_now, w_mid_t[...], w_out[...])
        put_cells(fbar, step, bar + dot(w_in_t[...], a0_now))
        x[:, at] = f.astype(BF16)
        e[:, at] = e_now
        h0[:, at] = h0_now
        h1[:, at] = h1_now
        a1[:, at] = a1_now
        a0[:, at] = a0_now
    put_grads(grads, x, e, h0, h1, a0, a1, None)
    copies = Copies(sem)
    copies.start(grads, grads_far)
    send_post(post, xs, sends)
    stream_back(info, fbar, local, xs, sends, work, y_two, z_two)
    copies.wait()


def third_kernel(place, source, level, quadrant, f0, local1, swapped, x_got, z_got, far, passed,
                 w_in_t, w_mid_t, w_out, grads2_far, h0_far, h1_far,
                 grads, fbar, pbar, h0, h1, a0, a1, x, e, x_four, y_two, sems):
    info = Tables(place, source, level, quadrant)
    copies = Copies(sems)
    for step in range(CHUNKS):
        for hbm, near in ((h1_far, h1), (h0_far, h0)):
            copies.start(hbm.at[:, span(step)], near.at[:, span(step)])
    copies.start(grads2_far, grads)
    pbar[...] = local1[...]
    take_back(info, pbar, (swapped, x_got, z_got, far, passed), x_four, y_two)
    for step in range(CHUNKS):
        at = span(step)
        for copy in copies.made[2 * step : 2 * step + 2]:
            copy.wait()
        bar = cells_of(pbar, step)
        e_now, a1_now, a0_now = signals(bar, h0[:, at], h1[:, at], w_mid_t[...], w_out[...])
        put_cells(fbar, step, bar + dot(w_in_t[...], a0_now))
        x[:, at] = cells_of(f0, step).astype(BF16)
        e[:, at] = e_now
        a1[:, at] = a1_now
        a0[:, at] = a0_now
    copies.made[-1].wait()
    put_grads(grads, x, e, h0, h1, a0, a1, grads)


def final_kernel(place, source, level, quadrant, post2, swapped, x_got, z_got, far, passed,
                 out, work, x_four, y_two, z_two):
    info = Tables(place, source, level, quadrant)
    stream(info, post2, (swapped, x_got, z_got, far, passed), out, work, x_four, y_two, z_two)


def add_kernel(place, grads, arrived, mine):
    half = pl.ds(pl.multiple_of((place[0] & 1) * HALF, HALF), HALF)
    mine[...] = grads[half, :] + arrived[...]


def unpack_kernel(place, mine, other, g_in, g_mid, g_out, whole):
    scale = float(NB * NZ * CELLS) ** -0.5
    core = place[0] & 1
    whole[pl.ds(pl.multiple_of(core * HALF, HALF), HALF), :] = mine[...]
    whole[pl.ds(pl.multiple_of((1 - core) * HALF, HALF), HALF), :] = other[...]
    for j in range(4):
        cols = pl.ds(j * 128, 128)
        g_mid[:, cols] = whole[pl.ds(j * HID, HID), :] * scale
        g_out[:, cols] = whole[pl.ds(OUT_AT + 24 * j, Q), :] * scale
        g_in[:, cols] = whole[pl.ds(IN_AT + 24 * j, Q), :] * scale


BLOCK = (Q, ROWS, 128)
HIDDEN = (HID, CELLS)
THIN = (Q, CELLS)
SENDS = (192, 128)
X_TWO = (2, 2, 2, 8, 128)
FACES = [(2, 2, 8, 128), (2, 16, 128), (2, ROWS, 128)]


def run(kernel, tables, args, outs, scratch, mflops, megabytes, hbm=()):
    def shape(s):
        return jax.ShapeDtypeStruct(s, F32) if isinstance(s, tuple) else s

    def buffer(s):
        return pltpu.VMEM(s, F32) if isinstance(s, tuple) else s

    def out_spec(s):
        far = not isinstance(s, (tuple, jax.ShapeDtypeStruct))
        return pl.BlockSpec(memory_space=pltpu.HBM if far else pltpu.VMEM)

    args = list(args)
    in_specs = [pl.BlockSpec(memory_space=pltpu.SMEM)] * len(tables)
    for i in range(len(args)):
        if i in hbm:
            args[i] = pltpu.with_memory_space_constraint(args[i], pltpu.HBM)
        in_specs.append(pl.BlockSpec(memory_space=pltpu.HBM if i in hbm else pltpu.VMEM))
    return pl.pallas_call(
        kernel,
        out_shape=[shape(s) for s in outs],
        in_specs=in_specs,
        out_specs=[out_spec(s) for s in outs],
        scratch_shapes=[buffer(s) for s in scratch],
        compiler_params=pltpu.CompilerParams(vmem_limit_bytes=megabytes << 20),
        cost_estimate=pl.CostEstimate(
            flops=mflops * 1000000, bytes_accessed=1 << 20, transcendentals=0
        ),
    )(*tables, *args)


def send(value, target):
    pairs = [
        (b * NZ + z, nb % NB * NZ + nz % NZ)
        for b in range(NB)
        for z in range(NZ)
        for nb, nz in [target(b, z)]
    ]
    return lax.ppermute(value, AXES, pairs)


def exchange(sends, xs):
    swapped = send(sends, lambda b, z: (b ^ 1, z))
    far = send(sends, lambda b, z: (b - 3 if b % 2 == 0 else b + 3, z))
    x_got = send(
        jnp.concatenate([xs.reshape(64, 128), swapped[:64]]),
        lambda b, z: (b + 2 if b % 2 == 0 else b - 2, z),
    )
    z_got = send(
        jnp.concatenate([sends[128:], swapped[128:]]),
        lambda b, z: (b, z + 1 if b % 2 == 0 else z - 1),
    )
    x_got, z_got, far = lax.optimization_barrier((x_got, z_got, far))
    passed = send(jnp.concatenate([x_got, z_got[64:]]), lambda b, z: (b ^ 1, z))
    return swapped, x_got, z_got, far, passed


def total_over_devices(grads, place, beside):
    def other_core(v):
        return send(v, lambda b, z: (b ^ 1, z))

    halves = grads.reshape(2, HALF, 128)
    given = lax.dynamic_index_in_dim(halves, 1 - place[0] % 2, 0, keepdims=False)
    (mine,) = run(add_kernel, [place], [grads, other_core(given)], [(HALF, 128)], [], 10, 8)
    mine = mine.reshape(64, 1, HALF * 2)
    mine = lax.all_to_all(mine, CHIPS, 0, 0, tiled=True).sum(axis=0, keepdims=True)
    mine = jnp.broadcast_to(mine, (64, 1, HALF * 2))
    mine = lax.all_to_all(mine, CHIPS, 0, 0, tiled=True).reshape(HALF, 128)
    other, beside = lax.optimization_barrier((other_core(mine), beside))
    return mine, other, beside


def shards(populations, w_in, w_mid, w_out, cotangent, face_source, face_level, face_quadrant):
    f0 = populations.reshape(BLOCK)
    cot = cotangent.reshape(BLOCK)
    w_in_t = w_in.T
    w_mid = w_mid[0]
    w_mid_t = w_mid.T
    place = lax.axis_index(BLOCKS).astype(jnp.int32).reshape(1)
    tables = [place, face_source.T, face_level[0], face_quadrant[0]]
    hidden = pltpu.HBM(HIDDEN, BF16)
    thin = jax.ShapeDtypeStruct(THIN, BF16)
    grad = (GROWS, 128)
    near = pltpu.VMEM(HIDDEN, BF16)
    near_thin = pltpu.VMEM(THIN, BF16)
    sems = pltpu.SemaphoreType.DMA

    post1, local2, *sends, h0, h1 = run(
        first_kernel, tables[:1], [*tables[1:], f0, cot, w_in_t, w_mid, w_out],
        [BLOCK, BLOCK, SENDS, X_TWO, hidden, hidden],
        [pltpu.SMEM((4, NB), jnp.int32), pltpu.SMEM((1, 6), jnp.int32),
         pltpu.SMEM((1, 6), jnp.int32),
         BLOCK, BLOCK, pltpu.VMEM((Q, HID), BF16), pltpu.VMEM((HID, HID), BF16),
         pltpu.VMEM((Q, HID), BF16), near, near, BLOCK, *FACES[1:], sems((8,)),
         sems((2 * CHUNKS,))],
        4000, 32, range(8),
    )
    got = exchange(*sends)
    post2, local1, *sends, grads2 = run(
        second_kernel, tables, [post1, local2, *got, w_in_t, w_mid, w_mid_t, w_out],
        [BLOCK, BLOCK, SENDS, X_TWO, pltpu.HBM(grad, F32)],
        [grad, near_thin, near_thin, *[near] * 4, *[BLOCK] * 4, *FACES, sems((1,))],
        14000, 32,
    )
    got = exchange(*sends)
    grads, fbar0 = run(
        third_kernel, tables, [f0, local1, *got, w_in_t, w_mid_t, w_out, grads2, h0, h1],
        [grad, BLOCK],
        [BLOCK, *[near] * 4, near_thin, near_thin, *FACES[:2], sems((2 * CHUNKS + 1,))],
        8000, 32, (10, 11, 12),
    )
    post2, grads = lax.optimization_barrier((post2, grads))
    (final,) = run(final_kernel, tables, [post2, *got], [BLOCK], [BLOCK, *FACES], 500, 8)
    mine, other, final = total_over_devices(grads, place, final)
    g_in, g_mid, g_out = run(
        unpack_kernel, [place], [mine, other], [(Q, HID), (HID, HID), (Q, HID)], [grad], 10, 8
    )
    whole = (Q, 1, 1, CELLS)
    return final.reshape(whole), fbar0.reshape(whole), g_in.T, g_mid[None], g_out


def solution(mesh):
    cells = P(None, "slab", BLOCKS, None)
    local = P("slab", BLOCKS, None)
    split = Mesh(mesh.devices.reshape(NX, NX, 2, NZ), AXES)
    return jax.shard_map(
        shards,
        mesh=split,
        in_specs=(cells, P(), P(), P(), cells, P(), local, local),
        out_specs=(cells, cells, P(), P(), P()),
        check_vma=False,
    )
```

```python
import jax
import jax.numpy as jnp
from jax import lax
from jax.experimental import pallas as pl
from jax.experimental.pallas import tpu as pltpu
from jax.sharding import Mesh
from jax.sharding import PartitionSpec as P

Q = 19
HID = 512
CELLS = 4096
ROWS = 32
CHUNK = 1024
TILES = CHUNK // 128
CHUNKS = CELLS // CHUNK
NB = 32
NZ = 4
NX = 4
BLOCKS = ("bx", "by", "core")
AXES = ("bx", "by", "core", "slab")
CHIPS = ("bx", "by", "slab")
F32 = jnp.float32
BF16 = jnp.bfloat16
GROWS = 2304
HALF = GROWS // 2
Y_AT = 48
Z_AT = Y_AT + 64
FAR_ROWS = 104
OUT_AT = 4 * HID
IN_AT = OUT_AT + 4 * 24

VELOCITIES = [
    (0, 0, 0),
    (1, 0, 0),
    (-1, 0, 0),
    (0, 1, 0),
    (0, -1, 0),
    (0, 0, 1),
    (0, 0, -1),
    (1, 1, 0),
    (-1, -1, 0),
    (1, -1, 0),
    (-1, 1, 0),
    (1, 0, 1),
    (-1, 0, -1),
    (1, 0, -1),
    (-1, 0, 1),
    (0, 1, 1),
    (0, -1, -1),
    (0, 1, -1),
    (0, -1, 1),
]
OPPOSITE = [0, 2, 1, 4, 3, 6, 5, 8, 7, 10, 9, 12, 11, 14, 13, 16, 15, 18, 17]


def members(face):
    sign = 1 if face % 2 == 0 else -1
    return [q for q in range(Q) if VELOCITIES[q][face // 2] == sign]


def iota(rows, dim):
    return lax.broadcasted_iota(jnp.int32, (rows, 128), dim)


def roll(value, shift, axis):
    shift %= value.shape[axis]
    return value if shift == 0 else pltpu.roll(value, shift, axis)


def shifted(v, velocity):
    cx, cy, cz = velocity
    lane = iota(ROWS, 1)
    if cz:
        v = jnp.where(lane & 15 == (0 if cz == 1 else 15), roll(v, -15 * cz, 1), roll(v, cz, 1))
    if cy:
        t = roll(v, 16 * cy, 1)
        swapped = jnp.where(iota(ROWS, 0) & 1 == 1, roll(t, 1, 0), roll(t, -1, 0))
        v = jnp.where(lane >> 4 == (0 if cy == 1 else 7), swapped, t)
    if cx:
        v = roll(v, 2 * cx, 0)
    return v


def corner(q):
    row, lane = iota(ROWS, 0), iota(ROWS, 1)
    coords = [row >> 1, (row & 1) * 8 + (lane >> 4), lane & 15]
    mask = None
    for axis in range(3):
        c = VELOCITIES[q][axis]
        if c:
            here = coords[axis] == (0 if c == 1 else 15)
            mask = here if mask is None else mask & here
    return mask


def is_edge(q):
    return sum(abs(c) for c in VELOCITIES[q]) == 2


def pack_faces(src, put_x, put_y, put_z):
    lane16, lane32 = iota(16, 1), iota(ROWS, 1)
    for f in (0, 1):
        for i, q in enumerate(members(f)):
            for r in (0, 1):
                put_x(f, r, i, src[q, pl.ds((30 if f == 0 else 0) + r, 1), :])
    for f in (2, 3):
        acc = jnp.zeros((16, 128), F32)
        for i, q in enumerate(members(f)):
            v = src[q, pl.ds(1 if f == 2 else 0, 16, stride=2), :]
            v = roll(v, 16 * i - (112 if f == 2 else 0), 1)
            acc = jnp.where(lane16 >> 4 == i, v, acc)
        put_y(f - 2, acc)
    acc = jnp.zeros((ROWS, 128), F32)
    for f in (4, 5):
        for i, q in enumerate(members(f)):
            slot = i if f == 4 else 8 + i
            v = roll(src[q], slot - (15 if f == 4 else 0), 1)
            acc = jnp.where(lane32 & 15 == slot, v, acc)
    put_z(acc)


def unpack_faces(dst, get_x, y_ref, z, add):
    lane16, lane32 = iota(16, 1), iota(ROWS, 1)
    for f in (0, 1):
        for i, q in enumerate(members(f)):
            for r in (0, 1):
                at = pl.ds((30 if f == 0 else 0) + r, 1)
                v = get_x(f, r, i)
                dst[q, at, :] = dst[q, at, :] + v if add else v
    for f in (2, 3):
        packed = y_ref[f - 2]
        for i, q in enumerate(members(f)):
            at = pl.ds(1 if f == 2 else 0, 16, stride=2)
            v = roll(packed, (112 if f == 2 else 0) - 16 * i, 1)
            old = dst[q, at, :]
            new = old + v if add else v
            dst[q, at, :] = jnp.where(lane16 >> 4 == (7 if f == 2 else 0), new, old)
    for f in (4, 5):
        for i, q in enumerate(members(f)):
            v = roll(z, 15 - i if f == 4 else -(8 + i), 1)
            old = dst[q]
            new = old + v if add else v
            dst[q] = jnp.where(lane32 & 15 == (15 if f == 4 else 0), new, old)


def picked(value, index):
    return jnp.take_along_axis(value, index, axis=1)


class Tables:
    def __init__(self, place, source, level, quadrant):
        self.place, self.source, self.level, self.quadrant = place, source, level, quadrant

    def block(self):
        return self.place[0]

    def distance(self, face):
        d = self.source[face, self.block()] - self.block()
        return jnp.where(d < 0, d + NB, d)


def level_of(info, f):
    return info.level[0, f ^ 1] == 1


def quadrant_of(info, f):
    r = info.quadrant[0, f ^ 1]
    return r >> 1, r & 1


def refine_x(info, x):
    lane = iota(8, 1)
    for f in (0, 1):
        fine = level_of(info, f)
        qr, qc = quadrant_of(info, f)
        rows = [x[f, 0], x[f, 1]]
        source = jnp.where(qr == 0, rows[0], rows[1])
        for r in (0, 1):
            index = (r * 4 + (lane >> 5)) * 16 + qc * 8 + ((lane & 15) >> 1)
            x[f, r] = jnp.where(fine, picked(source, index), rows[r])


def refine_y(info, y):
    lane = iota(8, 1)
    for f in (2, 3):
        fine = level_of(info, f)
        qr, qc = quadrant_of(info, f)
        whole = y[f - 2]
        source = jnp.where(qr == 0, whole[:8], whole[8:])
        v = picked(source, (lane >> 4) * 16 + qc * 8 + ((lane & 15) >> 1))
        for d in (0, 1):
            at = pl.ds(d, 8, stride=2)
            y[f - 2, at, :] = jnp.where(fine, v, y[f - 2, at, :])


def refine_z(info, z_two):
    lane = iota(8, 1)
    for f in (4, 5):
        z = z_two.at[f - 4]
        fine = level_of(info, f)
        qr, qc = quadrant_of(info, f)
        parts = {(h, p): z[pl.ds(16 * h + p, 8, stride=2), :] for h in (0, 1) for p in (0, 1)}
        halves = [jnp.where(qc == 0, parts[h, 0], parts[h, 1]) for h in (0, 1)]
        source = jnp.where(qr == 0, halves[0], halves[1])
        for p in (0, 1):
            v = picked(source, (p * 4 + (lane >> 5)) * 16 + (lane & 15))
            for d in (0, 1):
                at = pl.ds(2 * d + p, 8, stride=4)
                z[at, :] = jnp.where(fine, v, z[at, :])
    return jnp.where(iota(ROWS, 1) & 15 < 8, z_two[0], z_two[1])


def gather_x(info, x):
    lane = iota(8, 1)
    index = (2 * ((lane >> 4) & 3)) * 16 + 2 * (lane & 7)
    for f in (0, 1):
        fine = level_of(info, f)
        qr, qc = quadrant_of(info, f)
        rows = [x[f, 0], x[f, 1]]
        sums = []
        for v in rows:
            v = v + roll(v, -1, 1)
            v = v + roll(v, -16, 1)
            sums.append(picked(v, index))
        v = jnp.where(lane < 64, sums[0], sums[1])
        v = jnp.where((lane & 15) >> 3 == qc, v, 0.0)
        for r in (0, 1):
            x[f, r] = jnp.where(fine, jnp.where(qr == r, v, 0.0), rows[r])


def gather_y(info, y):
    lane = iota(8, 1)
    index = (lane >> 4) * 16 + 2 * (lane & 7)
    for f in (2, 3):
        fine = level_of(info, f)
        qr, qc = quadrant_of(info, f)
        v = y[f - 2, pl.ds(0, 8, stride=2), :] + y[f - 2, pl.ds(1, 8, stride=2), :]
        v = picked(v + roll(v, -1, 1), index)
        v = jnp.where((lane & 15) >> 3 == qc, v, 0.0)
        for h in (0, 1):
            at = pl.ds(8 * h, 8)
            y[f - 2, at, :] = jnp.where(fine, jnp.where(qr == h, v, 0.0), y[f - 2, at, :])


def gather_z(info, z_two):
    lane = iota(8, 1)
    index = (2 * ((lane >> 4) & 3)) * 16 + (lane & 15)
    for f in (4, 5):
        z = z_two.at[f - 4]
        fine = level_of(info, f)
        qr, qc = quadrant_of(info, f)
        sums = []
        for p in (0, 1):
            v = z[pl.ds(p, 8, stride=4), :] + z[pl.ds(2 + p, 8, stride=4), :]
            sums.append(picked(v + roll(v, -16, 1), index))
        v = jnp.where(lane < 64, sums[0], sums[1])
        for h in (0, 1):
            for p in (0, 1):
                at = pl.ds(16 * h + p, 8, stride=2)
                here = (qr == h) & (qc == p)
                z[at, :] = jnp.where(fine, jnp.where(here, v, 0.0), z[at, :])
    return jnp.where(iota(ROWS, 1) & 15 < 8, z_two[0], z_two[1])


def choose_x(info, face, got, kind):
    swapped, x_got, z_got, far, passed = got
    d = info.distance(face)
    even = info.block() & 1 == 0

    def at(distance):
        return jnp.where(even, distance % NB, -distance % NB)

    cases = [
        (at(1), swapped, 0),
        (at(-2), x_got, 0),
        (at(-1), x_got, Y_AT),
        (at(3), passed, 0),
        (at(2), passed, Y_AT),
        (at(-3), far, 0),
    ]
    return lambda f, r: sum_where(
        [
            (d == spot, ref[pl.ds(start + 5 * (kind * 4 + f * 2 + r), 8), :])
            for spot, ref, start in cases
        ]
    )


def choose_z(info, got):
    direct = got[2][pl.ds(0, 32), :]
    passed = got[4][pl.ds(2 * Y_AT, 32), :]
    even = info.block() & 1 == 0
    return jnp.where(even, direct, passed), jnp.where(even, passed, direct)


def sum_where(cases):
    total = jnp.zeros((8, 128), F32)
    for condition, value in cases:
        total = jnp.where(condition, value, total)
    return total


def put_x_rows(sends, xs, kind):
    for f in (0, 1):
        for r in (0, 1):
            sends[pl.ds(5 * (kind * 4 + f * 2 + r), 5), :] = xs[kind, f, r, pl.ds(0, 5), :]


def put_z_rows(info, sends, z_keep):
    low = iota(ROWS, 1) & 15 < 8
    up = jnp.where(low, z_keep[0], z_keep[1])
    down = jnp.where(low, z_keep[1], z_keep[0])
    even = info.block() & 1 == 0
    sends[pl.ds(Z_AT, 32), :] = jnp.where(even, up, down)
    sends[pl.ds(Z_AT + 32, 32), :] = jnp.where(even, down, up)


def stream_back(info, bar, local, xs, sends, z_keep, work, y_two, z_two):
    for q in range(Q):
        v = bar[q]
        if is_edge(q):
            v = jnp.where(corner(q), 0.0, v)
        work[q] = shifted(v, tuple(-c for c in VELOCITIES[q]))
    x_four = xs.at[1]
    x_four[...] = jnp.zeros(x_four.shape, F32)

    def put_x(f, r, i, v):
        x_four[f, r, pl.ds(i, 1), :] = v

    def put_y(f, v):
        y_two[f] = v

    def put_z(v):
        z_two[0] = v
        z_two[1] = v

    pack_faces(work, put_x, put_y, put_z)
    gather_x(info, x_four)
    gather_y(info, y_two)
    z_keep[1] = gather_z(info, z_two)
    put_x_rows(sends, xs, 1)
    sends[pl.ds(Y_AT + 32, 32), :] = y_two[...].reshape(32, 128)
    row, lane = iota(ROWS, 0), iota(ROWS, 1)
    coords = [row >> 1, (row & 1) * 8 + (lane >> 4), lane & 15]
    for q in range(Q):
        v = work[q]
        leaving = None
        for axis in range(3):
            c = VELOCITIES[q][axis]
            if c:
                here = coords[axis] == (15 if c == 1 else 0)
                leaving = here if leaving is None else leaving | here
        if leaving is not None:
            v = jnp.where(leaving, 0.0, v)
        if is_edge(q):
            v = v + jnp.where(corner(OPPOSITE[q]), bar[OPPOSITE[q]], 0.0)
        local[q] = v


def send_post(post, xs, sends, z_keep):
    x_four = xs.at[0]
    x_four[...] = jnp.zeros(x_four.shape, F32)

    def put_x(f, r, i, v):
        x_four[f, r, pl.ds(i, 1), :] = v

    def put_y(f, v):
        sends[pl.ds(Y_AT + 16 * f, 16), :] = v

    def put_z(v):
        z_keep[0] = v

    pack_faces(post, put_x, put_y, put_z)
    put_x_rows(sends, xs, 0)


def stream(info, post, got, out, work, x_four, y_two, z_two):
    swapped = got[0]
    for f in (0, 1):
        pick = choose_x(info, f ^ 1, got, 0)
        for r in (0, 1):
            x_four[f, r] = pick(f, r)
    refine_x(info, x_four)
    y_two[0] = swapped[pl.ds(Y_AT, 16), :]
    y_two[1] = swapped[pl.ds(Y_AT + 16, 16), :]
    refine_y(info, y_two)
    z_two[0], z_two[1] = choose_z(info, got)
    z = refine_z(info, z_two)
    work[...] = post[...]
    unpack_faces(work, lambda f, r, i: x_four[f, r, pl.ds(i, 1), :], y_two, z, False)
    for q in range(Q):
        v = shifted(work[q], VELOCITIES[q])
        if is_edge(q):
            v = jnp.where(corner(q), post[OPPOSITE[q]], v)
        out[q] = v


def take_back(info, bar, got, x_four, y_two):
    swapped = got[0]
    for f in (0, 1):
        pick = choose_x(info, f, got, 1)
        for r in (0, 1):
            x_four[f, r] = pick(f, r)
    y_two[0] = swapped[pl.ds(Y_AT + 32, 16), :]
    y_two[1] = swapped[pl.ds(Y_AT + 48, 16), :]
    below, above = choose_z(info, got)
    z = jnp.where(iota(ROWS, 1) & 15 < 8, above, below)
    unpack_faces(bar, lambda f, r, i: x_four[f, r, pl.ds(i, 1), :], y_two, z, True)


def dot(a, b, ca=1, cb=0):
    return lax.dot_general(a, b, (((ca,), (cb,)), ((), ())), preferred_element_type=F32)


def cells_of(ref, step):
    parts = [
        ref[:, pl.ds(step * TILES + j, 1), :].reshape(Q, 128) for j in range(TILES)
    ]
    return jnp.concatenate(parts, axis=1)


def put_cells(ref, step, value):
    for j in range(TILES):
        ref[:, pl.ds(step * TILES + j, 1), :] = value[:, j * 128 : (j + 1) * 128].reshape(Q, 1, 128)


def span(step):
    return pl.ds(step * CHUNK, CHUNK)


def forward(x, w_in_t, w_mid, w_out):
    xb = x.astype(BF16)
    h0 = jnp.tanh(dot(w_in_t, xb, 0, 0)).astype(BF16)
    h1 = jnp.tanh(dot(w_mid, h0)).astype(BF16)
    return h0, h1, x + dot(w_out, h1)


def slope(h):
    h = h.astype(F32)
    return 1.0 - h * h


def signals(pbar, h0, h1, w_mid_t, w_out):
    e = pbar.astype(BF16)
    a1 = (dot(w_out, e, 0, 0) * slope(h1)).astype(BF16)
    a0 = (dot(w_mid_t, a1) * slope(h0)).astype(BF16)
    return e, a1, a0


class Copies:
    def __init__(self, sems):
        self.sems, self.made = sems, []

    def start(self, source, target):
        copy = pltpu.make_async_copy(source, target, self.sems.at[len(self.made)])
        copy.start()
        self.made.append(copy)
        return copy

    def wait(self):
        for copy in self.made:
            copy.wait()


def put_grads(grads, x, e, h0, h1, a0, a1, more):
    def put(at, rows, value):
        for j in range(4):
            spot = pl.ds(at + j * (HID if rows == HID else 24), rows)
            v = value[:, j * 128 : (j + 1) * 128]
            grads[spot, :] = v if more is None else more[spot, :] + v

    put(0, HID, dot(a1[...], h0[...], 1, 1))
    put(OUT_AT, Q, dot(e[...], h1[...], 1, 1))
    put(IN_AT, Q, dot(x[...], a0[...], 1, 1))
    if more is None:
        rest = GROWS - IN_AT - 96
        grads[pl.ds(IN_AT + 96, rest), :] = jnp.zeros((rest, 128), F32)


def first_kernel(place, source_far, level_far, quadrant_far, f0_far, cot_far, w_in_far, w_mid_far,
                 w_out_far, post, local, sends, h0_far, h1_far,
                 source, level, quadrant, xs, f0, cot, w_in_t, w_mid, w_out, h0, h1, work, y_two, z_two,
                 z_keep, sems, out_sems):
    info = Tables(place, source, level, quadrant)
    copies = Copies(sems)
    for far, near in ((cot_far, cot), (source_far, source), (level_far, level),
                      (quadrant_far, quadrant), (f0_far, f0), (w_in_far, w_in_t),
                      (w_mid_far, w_mid), (w_out_far, w_out)):
        copies.start(far, near)
    for copy in copies.made[:4]:
        copy.wait()
    stream_back(info, cot, local, xs, sends, z_keep, work, y_two, z_two)
    for copy in copies.made[4:]:
        copy.wait()
    copies = Copies(out_sems)
    for step in range(CHUNKS):
        a, b, out = forward(cells_of(f0, step), w_in_t[...], w_mid[...], w_out[...])
        h0[:, span(step)] = a
        copies.start(h0.at[:, span(step)], h0_far.at[:, span(step)])
        h1[:, span(step)] = b
        copies.start(h1.at[:, span(step)], h1_far.at[:, span(step)])
        put_cells(post, step, out)
    send_post(post, xs, sends, z_keep)
    put_z_rows(info, sends, z_keep)
    copies.wait()


def second_kernel(place, source, level, quadrant, post1, local2, swapped, x_got, z_got, far, passed,
                  w_in_t, w_mid, w_mid_t, w_out, post, local, sends, grads_far,
                  grads, xs, x, e, h0, h1, a0, a1, f1, pbar, fbar, work, x_four, y_two, z_two, z_keep, sem):
    info = Tables(place, source, level, quadrant)
    got = (swapped, x_got, z_got, far, passed)
    stream(info, post1, got, f1, work, x_four, y_two, z_two)
    pbar[...] = local2[...]
    take_back(info, pbar, got, x_four, y_two)
    for step in range(CHUNKS):
        at = span(step)
        f = cells_of(f1, step)
        h0_now, h1_now, out = forward(f, w_in_t[...], w_mid[...], w_out[...])
        put_cells(post, step, out)
        bar = cells_of(pbar, step)
        e_now, a1_now, a0_now = signals(bar, h0_now, h1_now, w_mid_t[...], w_out[...])
        put_cells(fbar, step, bar + dot(w_in_t[...], a0_now))
        x[:, at] = f.astype(BF16)
        e[:, at] = e_now
        h0[:, at] = h0_now
        h1[:, at] = h1_now
        a1[:, at] = a1_now
        a0[:, at] = a0_now
    put_grads(grads, x, e, h0, h1, a0, a1, None)
    copies = Copies(sem)
    copies.start(grads, grads_far)
    send_post(post, xs, sends, z_keep)
    stream_back(info, fbar, local, xs, sends, z_keep, work, y_two, z_two)
    put_z_rows(info, sends, z_keep)
    copies.wait()


def third_kernel(place, source, level, quadrant, f0, local1, swapped, x_got, z_got, far, passed,
                 w_in_t, w_mid_t, w_out, grads2_far, h0_far, h1_far,
                 grads, fbar, pbar, h0, h1, a0, a1, x, e, x_four, y_two, sems):
    info = Tables(place, source, level, quadrant)
    copies = Copies(sems)
    for step in range(CHUNKS):
        for hbm, near in ((h1_far, h1), (h0_far, h0)):
            copies.start(hbm.at[:, span(step)], near.at[:, span(step)])
    copies.start(grads2_far, grads)
    pbar[...] = local1[...]
    take_back(info, pbar, (swapped, x_got, z_got, far, passed), x_four, y_two)
    for step in range(CHUNKS):
        at = span(step)
        for copy in copies.made[2 * step : 2 * step + 2]:
            copy.wait()
        bar = cells_of(pbar, step)
        e_now, a1_now, a0_now = signals(bar, h0[:, at], h1[:, at], w_mid_t[...], w_out[...])
        put_cells(fbar, step, bar + dot(w_in_t[...], a0_now))
        x[:, at] = cells_of(f0, step).astype(BF16)
        e[:, at] = e_now
        a1[:, at] = a1_now
        a0[:, at] = a0_now
    copies.made[-1].wait()
    put_grads(grads, x, e, h0, h1, a0, a1, grads)


def final_kernel(place, source, level, quadrant, post2, swapped, x_got, z_got, far, passed,
                 out, work, x_four, y_two, z_two):
    info = Tables(place, source, level, quadrant)
    stream(info, post2, (swapped, x_got, z_got, far, passed), out, work, x_four, y_two, z_two)


def add_kernel(place, grads, arrived, mine):
    half = pl.ds(pl.multiple_of((place[0] & 1) * HALF, HALF), HALF)
    mine[...] = grads[half, :] + arrived[...]


def unpack_kernel(place, mine, other, g_in, g_mid, g_out, whole):
    scale = float(NB * NZ * CELLS) ** -0.5
    core = place[0] & 1
    whole[pl.ds(pl.multiple_of(core * HALF, HALF), HALF), :] = mine[...]
    whole[pl.ds(pl.multiple_of((1 - core) * HALF, HALF), HALF), :] = other[...]
    for j in range(4):
        cols = pl.ds(j * 128, 128)
        g_mid[:, cols] = whole[pl.ds(j * HID, HID), :] * scale
        g_out[:, cols] = whole[pl.ds(OUT_AT + 24 * j, Q), :] * scale
        g_in[:, cols] = whole[pl.ds(IN_AT + 24 * j, Q), :] * scale


BLOCK = (Q, ROWS, 128)
HIDDEN = (HID, CELLS)
THIN = (Q, CELLS)
SENDS = (Z_AT + 64, 128)
X_TWO = (2, 2, 2, 8, 128)
FACES = [(2, 2, 8, 128), (2, 16, 128), (2, ROWS, 128)]


def run(kernel, tables, args, outs, scratch, mflops, megabytes, hbm=()):
    def shape(s):
        return jax.ShapeDtypeStruct(s, F32) if isinstance(s, tuple) else s

    def buffer(s):
        return pltpu.VMEM(s, F32) if isinstance(s, tuple) else s

    def out_spec(s):
        far = not isinstance(s, (tuple, jax.ShapeDtypeStruct))
        return pl.BlockSpec(memory_space=pltpu.HBM if far else pltpu.VMEM)

    args = list(args)
    in_specs = [pl.BlockSpec(memory_space=pltpu.SMEM)] * len(tables)
    for i in range(len(args)):
        if i in hbm:
            args[i] = pltpu.with_memory_space_constraint(args[i], pltpu.HBM)
        in_specs.append(pl.BlockSpec(memory_space=pltpu.HBM if i in hbm else pltpu.VMEM))
    return pl.pallas_call(
        kernel,
        out_shape=[shape(s) for s in outs],
        in_specs=in_specs,
        out_specs=[out_spec(s) for s in outs],
        scratch_shapes=[buffer(s) for s in scratch],
        compiler_params=pltpu.CompilerParams(vmem_limit_bytes=megabytes << 20),
        cost_estimate=pl.CostEstimate(
            flops=mflops * 1000000, bytes_accessed=1 << 20, transcendentals=0
        ),
    )(*tables, *args)


def send(value, target):
    pairs = [
        (b * NZ + z, nb % NB * NZ + nz % NZ)
        for b in range(NB)
        for z in range(NZ)
        for nb, nz in [target(b, z)]
    ]
    return lax.ppermute(value, AXES, pairs)


def exchange(sends):
    swapped = send(sends, lambda b, z: (b ^ 1, z))
    far = send(sends[:FAR_ROWS], lambda b, z: (b - 3 if b % 2 == 0 else b + 3, z))
    x_got = send(
        jnp.concatenate([sends[:Y_AT], swapped[:Y_AT]]),
        lambda b, z: (b + 2 if b % 2 == 0 else b - 2, z),
    )
    z_got = send(
        jnp.concatenate([sends[Z_AT : Z_AT + 32], swapped[Z_AT + 32 :]]),
        lambda b, z: (b, z + 1 if b % 2 == 0 else z - 1),
    )
    x_got, z_got, far = lax.optimization_barrier((x_got, z_got, far))
    passed = send(jnp.concatenate([x_got, z_got[32:]]), lambda b, z: (b ^ 1, z))
    return swapped, x_got, z_got, far, passed


def total_over_devices(grads, place, beside):
    def other_core(v):
        return send(v, lambda b, z: (b ^ 1, z))

    halves = grads.reshape(2, HALF, 128)
    given = lax.dynamic_index_in_dim(halves, 1 - place[0] % 2, 0, keepdims=False)
    (mine,) = run(add_kernel, [place], [grads, other_core(given)], [(HALF, 128)], [], 10, 8)
    mine = mine.reshape(64, 1, HALF * 2)
    mine = lax.all_to_all(mine, CHIPS, 0, 0, tiled=True).sum(axis=0, keepdims=True)
    mine = jnp.broadcast_to(mine, (64, 1, HALF * 2))
    mine = lax.all_to_all(mine, CHIPS, 0, 0, tiled=True).reshape(HALF, 128)
    other, beside = lax.optimization_barrier((other_core(mine), beside))
    return mine, other, beside


def shards(populations, w_in, w_mid, w_out, cotangent, face_source, face_level, face_quadrant):
    f0 = populations.reshape(BLOCK)
    cot = cotangent.reshape(BLOCK)
    w_in_t = w_in.T
    w_mid = w_mid[0]
    w_mid_t = w_mid.T
    place = lax.axis_index(BLOCKS).astype(jnp.int32).reshape(1)
    tables = [place, face_source.T, face_level[0], face_quadrant[0]]
    hidden = pltpu.HBM(HIDDEN, BF16)
    thin = jax.ShapeDtypeStruct(THIN, BF16)
    grad = (GROWS, 128)
    near = pltpu.VMEM(HIDDEN, BF16)
    near_thin = pltpu.VMEM(THIN, BF16)
    sems = pltpu.SemaphoreType.DMA

    post1, local2, sends, h0, h1 = run(
        first_kernel, tables[:1], [*tables[1:], f0, cot, w_in_t, w_mid, w_out],
        [BLOCK, BLOCK, SENDS, hidden, hidden],
        [pltpu.SMEM((4, NB), jnp.int32), pltpu.SMEM((1, 6), jnp.int32),
         pltpu.SMEM((1, 6), jnp.int32), X_TWO,
         BLOCK, BLOCK, pltpu.VMEM((Q, HID), BF16), pltpu.VMEM((HID, HID), BF16),
         pltpu.VMEM((Q, HID), BF16), near, near, BLOCK, *FACES[1:], FACES[2], sems((8,)),
         sems((2 * CHUNKS,))],
        4000, 32, range(8),
    )
    got = exchange(sends)
    post2, local1, sends, grads2 = run(
        second_kernel, tables, [post1, local2, *got, w_in_t, w_mid, w_mid_t, w_out],
        [BLOCK, BLOCK, SENDS, pltpu.HBM(grad, F32)],
        [grad, X_TWO, near_thin, near_thin, *[near] * 4, *[BLOCK] * 4, *FACES, FACES[2], sems((1,))],
        14000, 32,
    )
    got = exchange(sends)
    grads, fbar0 = run(
        third_kernel, tables, [f0, local1, *got, w_in_t, w_mid_t, w_out, grads2, h0, h1],
        [grad, BLOCK],
        [BLOCK, *[near] * 4, near_thin, near_thin, *FACES[:2], sems((2 * CHUNKS + 1,))],
        8000, 32, (10, 11, 12),
    )
    post2, grads = lax.optimization_barrier((post2, grads))
    (final,) = run(final_kernel, tables, [post2, *got], [BLOCK], [BLOCK, *FACES], 500, 8)
    mine, other, final = total_over_devices(grads, place, final)
    g_in, g_mid, g_out = run(
        unpack_kernel, [place], [mine, other], [(Q, HID), (HID, HID), (Q, HID)], [grad], 10, 8
    )
    whole = (Q, 1, 1, CELLS)
    return final.reshape(whole), fbar0.reshape(whole), g_in.T, g_mid[None], g_out


def solution(mesh):
    cells = P(None, "slab", BLOCKS, None)
    local = P("slab", BLOCKS, None)
    split = Mesh(mesh.devices.reshape(NX, NX, 2, NZ), AXES)
    return jax.shard_map(
        shards,
        mesh=split,
        in_specs=(cells, P(), P(), P(), cells, P(), local, local),
        out_specs=(cells, cells, P(), P(), P()),
        check_vma=False,
    )
```

```python
import jax
import jax.numpy as jnp
from jax import lax
from jax.experimental import pallas as pl
from jax.experimental.pallas import tpu as pltpu
from jax.sharding import Mesh
from jax.sharding import PartitionSpec as P

Q = 19
HID = 512
CELLS = 4096
ROWS = 32
CHUNK = 1024
TILES = CHUNK // 128
CHUNKS = CELLS // CHUNK
NB = 32
NZ = 4
NX = 4
BLOCKS = ("bx", "by", "core")
AXES = ("bx", "by", "core", "slab")
CHIPS = ("bx", "by", "slab")
F32 = jnp.float32
BF16 = jnp.bfloat16
GROWS = 2304
HALF = GROWS // 2
Y_AT = 48
Z_AT = Y_AT + 64
FAR_ROWS = 104
OUT_AT = 4 * HID
IN_AT = OUT_AT + 4 * 24

VELOCITIES = [
    (0, 0, 0),
    (1, 0, 0),
    (-1, 0, 0),
    (0, 1, 0),
    (0, -1, 0),
    (0, 0, 1),
    (0, 0, -1),
    (1, 1, 0),
    (-1, -1, 0),
    (1, -1, 0),
    (-1, 1, 0),
    (1, 0, 1),
    (-1, 0, -1),
    (1, 0, -1),
    (-1, 0, 1),
    (0, 1, 1),
    (0, -1, -1),
    (0, 1, -1),
    (0, -1, 1),
]
OPPOSITE = [0, 2, 1, 4, 3, 6, 5, 8, 7, 10, 9, 12, 11, 14, 13, 16, 15, 18, 17]


def members(face):
    sign = 1 if face % 2 == 0 else -1
    return [q for q in range(Q) if VELOCITIES[q][face // 2] == sign]


def iota(rows, dim):
    return lax.broadcasted_iota(jnp.int32, (rows, 128), dim)


def roll(value, shift, axis):
    shift %= value.shape[axis]
    return value if shift == 0 else pltpu.roll(value, shift, axis)


def shifted(v, velocity):
    cx, cy, cz = velocity
    lane = iota(ROWS, 1)
    if cz:
        v = jnp.where(lane & 15 == (0 if cz == 1 else 15), roll(v, -15 * cz, 1), roll(v, cz, 1))
    if cy:
        t = roll(v, 16 * cy, 1)
        swapped = jnp.where(iota(ROWS, 0) & 1 == 1, roll(t, 1, 0), roll(t, -1, 0))
        v = jnp.where(lane >> 4 == (0 if cy == 1 else 7), swapped, t)
    if cx:
        v = roll(v, 2 * cx, 0)
    return v


def corner(q):
    row, lane = iota(ROWS, 0), iota(ROWS, 1)
    coords = [row >> 1, (row & 1) * 8 + (lane >> 4), lane & 15]
    mask = None
    for axis in range(3):
        c = VELOCITIES[q][axis]
        if c:
            here = coords[axis] == (0 if c == 1 else 15)
            mask = here if mask is None else mask & here
    return mask


def is_edge(q):
    return sum(abs(c) for c in VELOCITIES[q]) == 2


def pack_faces(src, put_x, put_y, put_z):
    lane16, lane32 = iota(16, 1), iota(ROWS, 1)
    for f in (0, 1):
        for i, q in enumerate(members(f)):
            for r in (0, 1):
                put_x(f, r, i, src[q, pl.ds((30 if f == 0 else 0) + r, 1), :])
    for f in (2, 3):
        acc = jnp.zeros((16, 128), F32)
        for i, q in enumerate(members(f)):
            v = src[q, pl.ds(1 if f == 2 else 0, 16, stride=2), :]
            v = roll(v, 16 * i - (112 if f == 2 else 0), 1)
            acc = jnp.where(lane16 >> 4 == i, v, acc)
        put_y(f - 2, acc)
    acc = jnp.zeros((ROWS, 128), F32)
    for f in (4, 5):
        for i, q in enumerate(members(f)):
            slot = i if f == 4 else 8 + i
            v = roll(src[q], slot - (15 if f == 4 else 0), 1)
            acc = jnp.where(lane32 & 15 == slot, v, acc)
    put_z(acc)


def unpack_faces(dst, get_x, y_ref, z, add):
    lane16, lane32 = iota(16, 1), iota(ROWS, 1)
    for f in (0, 1):
        for i, q in enumerate(members(f)):
            for r in (0, 1):
                at = pl.ds((30 if f == 0 else 0) + r, 1)
                v = get_x(f, r, i)
                dst[q, at, :] = dst[q, at, :] + v if add else v
    for f in (2, 3):
        packed = y_ref[f - 2]
        for i, q in enumerate(members(f)):
            at = pl.ds(1 if f == 2 else 0, 16, stride=2)
            v = roll(packed, (112 if f == 2 else 0) - 16 * i, 1)
            old = dst[q, at, :]
            new = old + v if add else v
            dst[q, at, :] = jnp.where(lane16 >> 4 == (7 if f == 2 else 0), new, old)
    for f in (4, 5):
        for i, q in enumerate(members(f)):
            v = roll(z, 15 - i if f == 4 else -(8 + i), 1)
            old = dst[q]
            new = old + v if add else v
            dst[q] = jnp.where(lane32 & 15 == (15 if f == 4 else 0), new, old)


def picked(value, index):
    return jnp.take_along_axis(value, index, axis=1)


class Tables:
    def __init__(self, place, source, level, quadrant):
        self.place, self.source, self.level, self.quadrant = place, source, level, quadrant

    def block(self):
        return self.place[0]

    def distance(self, face):
        d = self.source[face, self.block()] - self.block()
        return jnp.where(d < 0, d + NB, d)


def level_of(info, f):
    return info.level[0, f ^ 1] == 1


def quadrant_of(info, f):
    r = info.quadrant[0, f ^ 1]
    return r >> 1, r & 1


def refine_x(info, x):
    lane = iota(8, 1)
    for f in (0, 1):
        fine = level_of(info, f)
        qr, qc = quadrant_of(info, f)
        rows = [x[f, 0], x[f, 1]]
        source = jnp.where(qr == 0, rows[0], rows[1])
        for r in (0, 1):
            index = (r * 4 + (lane >> 5)) * 16 + qc * 8 + ((lane & 15) >> 1)
            x[f, r] = jnp.where(fine, picked(source, index), rows[r])


def refine_y(info, y):
    lane = iota(8, 1)
    for f in (2, 3):
        fine = level_of(info, f)
        qr, qc = quadrant_of(info, f)
        whole = y[f - 2]
        source = jnp.where(qr == 0, whole[:8], whole[8:])
        v = picked(source, (lane >> 4) * 16 + qc * 8 + ((lane & 15) >> 1))
        for d in (0, 1):
            at = pl.ds(d, 8, stride=2)
            y[f - 2, at, :] = jnp.where(fine, v, y[f - 2, at, :])


def refine_z(info, z_two):
    lane = iota(8, 1)
    for f in (4, 5):
        z = z_two.at[f - 4]
        fine = level_of(info, f)
        qr, qc = quadrant_of(info, f)
        parts = {(h, p): z[pl.ds(16 * h + p, 8, stride=2), :] for h in (0, 1) for p in (0, 1)}
        halves = [jnp.where(qc == 0, parts[h, 0], parts[h, 1]) for h in (0, 1)]
        source = jnp.where(qr == 0, halves[0], halves[1])
        for p in (0, 1):
            v = picked(source, (p * 4 + (lane >> 5)) * 16 + (lane & 15))
            for d in (0, 1):
                at = pl.ds(2 * d + p, 8, stride=4)
                z[at, :] = jnp.where(fine, v, z[at, :])
    return jnp.where(iota(ROWS, 1) & 15 < 8, z_two[0], z_two[1])


def gather_x(info, x):
    lane = iota(8, 1)
    index = (2 * ((lane >> 4) & 3)) * 16 + 2 * (lane & 7)
    for f in (0, 1):
        fine = level_of(info, f)
        qr, qc = quadrant_of(info, f)
        rows = [x[f, 0], x[f, 1]]
        sums = []
        for v in rows:
            v = v + roll(v, -1, 1)
            v = v + roll(v, -16, 1)
            sums.append(picked(v, index))
        v = jnp.where(lane < 64, sums[0], sums[1])
        v = jnp.where((lane & 15) >> 3 == qc, v, 0.0)
        for r in (0, 1):
            x[f, r] = jnp.where(fine, jnp.where(qr == r, v, 0.0), rows[r])


def gather_y(info, y):
    lane = iota(8, 1)
    index = (lane >> 4) * 16 + 2 * (lane & 7)
    for f in (2, 3):
        fine = level_of(info, f)
        qr, qc = quadrant_of(info, f)
        v = y[f - 2, pl.ds(0, 8, stride=2), :] + y[f - 2, pl.ds(1, 8, stride=2), :]
        v = picked(v + roll(v, -1, 1), index)
        v = jnp.where((lane & 15) >> 3 == qc, v, 0.0)
        for h in (0, 1):
            at = pl.ds(8 * h, 8)
            y[f - 2, at, :] = jnp.where(fine, jnp.where(qr == h, v, 0.0), y[f - 2, at, :])


def gather_z(info, z_two):
    lane = iota(8, 1)
    index = (2 * ((lane >> 4) & 3)) * 16 + (lane & 15)
    for f in (4, 5):
        z = z_two.at[f - 4]
        fine = level_of(info, f)
        qr, qc = quadrant_of(info, f)
        sums = []
        for p in (0, 1):
            v = z[pl.ds(p, 8, stride=4), :] + z[pl.ds(2 + p, 8, stride=4), :]
            sums.append(picked(v + roll(v, -16, 1), index))
        v = jnp.where(lane < 64, sums[0], sums[1])
        for h in (0, 1):
            for p in (0, 1):
                at = pl.ds(16 * h + p, 8, stride=2)
                here = (qr == h) & (qc == p)
                z[at, :] = jnp.where(fine, jnp.where(here, v, 0.0), z[at, :])
    return jnp.where(iota(ROWS, 1) & 15 < 8, z_two[0], z_two[1])


def choose_x(info, face, got, kind):
    swapped, x_got, z_got, far, passed = got
    d = info.distance(face)
    even = info.block() & 1 == 0

    def at(distance):
        return jnp.where(even, distance % NB, -distance % NB)

    cases = [
        (at(1), swapped, 0),
        (at(-2), x_got, 0),
        (at(-1), x_got, Y_AT),
        (at(3), passed, 0),
        (at(2), passed, Y_AT),
        (at(-3), far, 0),
    ]
    return lambda f, r: sum_where(
        [
            (d == spot, ref[pl.ds(start + 5 * (kind * 4 + f * 2 + r), 8), :])
            for spot, ref, start in cases
        ]
    )


def choose_z(info, got):
    direct = got[2][pl.ds(0, 32), :]
    passed = got[4][pl.ds(2 * Y_AT, 32), :]
    even = info.block() & 1 == 0
    return jnp.where(even, direct, passed), jnp.where(even, passed, direct)


def sum_where(cases):
    total = jnp.zeros((8, 128), F32)
    for condition, value in cases:
        total = jnp.where(condition, value, total)
    return total


def put_x_rows(sends, xs, kind):
    for f in (0, 1):
        for r in (0, 1):
            sends[pl.ds(5 * (kind * 4 + f * 2 + r), 5), :] = xs[kind, f, r, pl.ds(0, 5), :]


def put_z_rows(info, sends, z_keep):
    low = iota(ROWS, 1) & 15 < 8
    up = jnp.where(low, z_keep[0], z_keep[1])
    down = jnp.where(low, z_keep[1], z_keep[0])
    even = info.block() & 1 == 0
    sends[pl.ds(Z_AT, 32), :] = jnp.where(even, up, down)
    sends[pl.ds(Z_AT + 32, 32), :] = jnp.where(even, down, up)


def stream_back(info, bar, local, xs, sends, z_keep, work, y_two, z_two):
    for q in range(Q):
        v = bar[q]
        if is_edge(q):
            v = jnp.where(corner(q), 0.0, v)
        work[q] = shifted(v, tuple(-c for c in VELOCITIES[q]))
    x_four = xs.at[1]
    x_four[...] = jnp.zeros(x_four.shape, F32)

    def put_x(f, r, i, v):
        x_four[f, r, pl.ds(i, 1), :] = v

    def put_y(f, v):
        y_two[f] = v

    def put_z(v):
        z_two[0] = v
        z_two[1] = v

    pack_faces(work, put_x, put_y, put_z)
    gather_x(info, x_four)
    gather_y(info, y_two)
    z_keep[1] = gather_z(info, z_two)
    put_x_rows(sends, xs, 1)
    sends[pl.ds(Y_AT + 32, 32), :] = y_two[...].reshape(32, 128)
    row, lane = iota(ROWS, 0), iota(ROWS, 1)
    coords = [row >> 1, (row & 1) * 8 + (lane >> 4), lane & 15]
    for q in range(Q):
        v = work[q]
        leaving = None
        for axis in range(3):
            c = VELOCITIES[q][axis]
            if c:
                here = coords[axis] == (15 if c == 1 else 0)
                leaving = here if leaving is None else leaving | here
        if leaving is not None:
            v = jnp.where(leaving, 0.0, v)
        if is_edge(q):
            v = v + jnp.where(corner(OPPOSITE[q]), bar[OPPOSITE[q]], 0.0)
        local[q] = v


def send_post(post, xs, sends, z_keep):
    x_four = xs.at[0]
    x_four[...] = jnp.zeros(x_four.shape, F32)

    def put_x(f, r, i, v):
        x_four[f, r, pl.ds(i, 1), :] = v

    def put_y(f, v):
        sends[pl.ds(Y_AT + 16 * f, 16), :] = v

    def put_z(v):
        z_keep[0] = v

    pack_faces(post, put_x, put_y, put_z)
    put_x_rows(sends, xs, 0)


def stream(info, post, got, out, work, x_four, y_two, z_two):
    swapped = got[0]
    for f in (0, 1):
        pick = choose_x(info, f ^ 1, got, 0)
        for r in (0, 1):
            x_four[f, r] = pick(f, r)
    refine_x(info, x_four)
    y_two[0] = swapped[pl.ds(Y_AT, 16), :]
    y_two[1] = swapped[pl.ds(Y_AT + 16, 16), :]
    refine_y(info, y_two)
    z_two[0], z_two[1] = choose_z(info, got)
    z = refine_z(info, z_two)
    work[...] = post[...]
    unpack_faces(work, lambda f, r, i: x_four[f, r, pl.ds(i, 1), :], y_two, z, False)
    for q in range(Q):
        v = shifted(work[q], VELOCITIES[q])
        if is_edge(q):
            v = jnp.where(corner(q), post[OPPOSITE[q]], v)
        out[q] = v


def take_back(info, bar, got, x_four, y_two):
    swapped = got[0]
    for f in (0, 1):
        pick = choose_x(info, f, got, 1)
        for r in (0, 1):
            x_four[f, r] = pick(f, r)
    y_two[0] = swapped[pl.ds(Y_AT + 32, 16), :]
    y_two[1] = swapped[pl.ds(Y_AT + 48, 16), :]
    below, above = choose_z(info, got)
    z = jnp.where(iota(ROWS, 1) & 15 < 8, above, below)
    unpack_faces(bar, lambda f, r, i: x_four[f, r, pl.ds(i, 1), :], y_two, z, True)


def dot(a, b, ca=1, cb=0):
    return lax.dot_general(a, b, (((ca,), (cb,)), ((), ())), preferred_element_type=F32)


def cells_of(ref, step):
    parts = [
        ref[:, pl.ds(step * TILES + j, 1), :].reshape(Q, 128) for j in range(TILES)
    ]
    return jnp.concatenate(parts, axis=1)


def put_cells(ref, step, value):
    for j in range(TILES):
        ref[:, pl.ds(step * TILES + j, 1), :] = value[:, j * 128 : (j + 1) * 128].reshape(Q, 1, 128)


def span(step):
    return pl.ds(step * CHUNK, CHUNK)


def forward(x, w_in_t, w_mid, w_out):
    xb = x.astype(BF16)
    h0 = jnp.tanh(dot(w_in_t, xb, 0, 0)).astype(BF16)
    h1 = jnp.tanh(dot(w_mid, h0)).astype(BF16)
    return h0, h1, x + dot(w_out, h1)


def slope(h):
    h = h.astype(F32)
    return 1.0 - h * h


def signals(pbar, h0, h1, w_mid_t, w_out):
    e = pbar.astype(BF16)
    a1 = (dot(w_out, e, 0, 0) * slope(h1)).astype(BF16)
    a0 = (dot(w_mid_t, a1) * slope(h0)).astype(BF16)
    return e, a1, a0


class Copies:
    def __init__(self, sems):
        self.sems, self.made = sems, []

    def start(self, source, target):
        copy = pltpu.make_async_copy(source, target, self.sems.at[len(self.made)])
        copy.start()
        self.made.append(copy)
        return copy

    def wait(self):
        for copy in self.made:
            copy.wait()


def put_grads(grads, x, e, h0, h1, a0, a1, more):
    def put(at, rows, value):
        for j in range(4):
            spot = pl.ds(at + j * (HID if rows == HID else 24), rows)
            v = value[:, j * 128 : (j + 1) * 128]
            grads[spot, :] = v if more is None else more[spot, :] + v

    put(0, HID, dot(a1[...], h0[...], 1, 1))
    put(OUT_AT, Q, dot(e[...], h1[...], 1, 1))
    put(IN_AT, Q, dot(x[...], a0[...], 1, 1))
    if more is None:
        rest = GROWS - IN_AT - 96
        grads[pl.ds(IN_AT + 96, rest), :] = jnp.zeros((rest, 128), F32)


def first_kernel(place, source_far, level_far, quadrant_far, f0_far, cot_far, w_in_far, w_mid_far,
                 w_out_far, post, local, sends, h0_far, h1_far,
                 source, level, quadrant, xs, f0, cot, w_in_t, w_mid, w_out, h0, h1, work, y_two, z_two,
                 z_keep, sems, out_sems):
    info = Tables(place, source, level, quadrant)
    copies = Copies(sems)
    for far, near in ((cot_far, cot), (source_far, source), (level_far, level),
                      (quadrant_far, quadrant), (f0_far, f0), (w_in_far, w_in_t),
                      (w_mid_far, w_mid), (w_out_far, w_out)):
        copies.start(far, near)
    for copy in copies.made[:4]:
        copy.wait()
    stream_back(info, cot, local, xs, sends, z_keep, work, y_two, z_two)
    for copy in copies.made[4:]:
        copy.wait()
    copies = Copies(out_sems)
    for step in range(CHUNKS):
        a, b, out = forward(cells_of(f0, step), w_in_t[...], w_mid[...], w_out[...])
        h0[step] = a
        copies.start(h0.at[step], h0_far.at[step])
        h1[step] = b
        copies.start(h1.at[step], h1_far.at[step])
        put_cells(post, step, out)
    send_post(post, xs, sends, z_keep)
    put_z_rows(info, sends, z_keep)
    copies.wait()


def second_kernel(place, source, level, quadrant, post1, local2, swapped, x_got, z_got, far, passed,
                  w_in_t, w_mid, w_mid_t, w_out, post, local, sends, grads_far,
                  grads, xs, x, e, h0, h1, a0, a1, f1, pbar, fbar, work, x_four, y_two, z_two, z_keep, sem):
    info = Tables(place, source, level, quadrant)
    got = (swapped, x_got, z_got, far, passed)
    stream(info, post1, got, f1, work, x_four, y_two, z_two)
    pbar[...] = local2[...]
    take_back(info, pbar, got, x_four, y_two)
    for step in range(CHUNKS):
        at = span(step)
        f = cells_of(f1, step)
        h0_now, h1_now, out = forward(f, w_in_t[...], w_mid[...], w_out[...])
        put_cells(post, step, out)
        bar = cells_of(pbar, step)
        e_now, a1_now, a0_now = signals(bar, h0_now, h1_now, w_mid_t[...], w_out[...])
        put_cells(fbar, step, bar + dot(w_in_t[...], a0_now))
        x[:, at] = f.astype(BF16)
        e[:, at] = e_now
        h0[:, at] = h0_now
        h1[:, at] = h1_now
        a1[:, at] = a1_now
        a0[:, at] = a0_now
    put_grads(grads, x, e, h0, h1, a0, a1, None)
    copies = Copies(sem)
    copies.start(grads, grads_far)
    send_post(post, xs, sends, z_keep)
    stream_back(info, fbar, local, xs, sends, z_keep, work, y_two, z_two)
    put_z_rows(info, sends, z_keep)
    copies.wait()


def third_kernel(place, source, level, quadrant, f0, local1, swapped, x_got, z_got, far, passed,
                 w_in_t, w_mid_t, w_out, grads2_far, h0_far, h1_far,
                 grads, fbar, pbar, h0, h1, a0, a1, x, e, x_four, y_two, sems):
    info = Tables(place, source, level, quadrant)
    copies = Copies(sems)
    for step in range(CHUNKS):
        for hbm, near in ((h1_far, h1), (h0_far, h0)):
            copies.start(hbm.at[step], near.at[:, span(step)])
    copies.start(grads2_far, grads)
    pbar[...] = local1[...]
    take_back(info, pbar, (swapped, x_got, z_got, far, passed), x_four, y_two)
    for step in range(CHUNKS):
        at = span(step)
        for copy in copies.made[2 * step : 2 * step + 2]:
            copy.wait()
        bar = cells_of(pbar, step)
        e_now, a1_now, a0_now = signals(bar, h0[:, at], h1[:, at], w_mid_t[...], w_out[...])
        put_cells(fbar, step, bar + dot(w_in_t[...], a0_now))
        x[:, at] = cells_of(f0, step).astype(BF16)
        e[:, at] = e_now
        a1[:, at] = a1_now
        a0[:, at] = a0_now
    copies.made[-1].wait()
    put_grads(grads, x, e, h0, h1, a0, a1, grads)


def final_kernel(place, source, level, quadrant, post2, swapped, x_got, z_got, far, passed,
                 out, work, x_four, y_two, z_two):
    info = Tables(place, source, level, quadrant)
    stream(info, post2, (swapped, x_got, z_got, far, passed), out, work, x_four, y_two, z_two)


def add_kernel(place, grads, arrived, mine):
    half = pl.ds(pl.multiple_of((place[0] & 1) * HALF, HALF), HALF)
    mine[...] = grads[half, :] + arrived[...]


def unpack_kernel(place, mine, other, g_in, g_mid, g_out, whole):
    scale = float(NB * NZ * CELLS) ** -0.5
    core = place[0] & 1
    whole[pl.ds(pl.multiple_of(core * HALF, HALF), HALF), :] = mine[...]
    whole[pl.ds(pl.multiple_of((1 - core) * HALF, HALF), HALF), :] = other[...]
    for j in range(4):
        cols = pl.ds(j * 128, 128)
        g_mid[:, cols] = whole[pl.ds(j * HID, HID), :] * scale
        g_out[:, cols] = whole[pl.ds(OUT_AT + 24 * j, Q), :] * scale
        g_in[:, cols] = whole[pl.ds(IN_AT + 24 * j, Q), :] * scale


BLOCK = (Q, ROWS, 128)
HIDDEN = (HID, CELLS)
THIN = (Q, CELLS)
SENDS = (Z_AT + 64, 128)
X_TWO = (2, 2, 2, 8, 128)
FACES = [(2, 2, 8, 128), (2, 16, 128), (2, ROWS, 128)]


def run(kernel, tables, args, outs, scratch, mflops, megabytes, hbm=()):
    def shape(s):
        return jax.ShapeDtypeStruct(s, F32) if isinstance(s, tuple) else s

    def buffer(s):
        return pltpu.VMEM(s, F32) if isinstance(s, tuple) else s

    def out_spec(s):
        far = not isinstance(s, (tuple, jax.ShapeDtypeStruct))
        return pl.BlockSpec(memory_space=pltpu.HBM if far else pltpu.VMEM)

    args = list(args)
    in_specs = [pl.BlockSpec(memory_space=pltpu.SMEM)] * len(tables)
    for i in range(len(args)):
        if i in hbm:
            args[i] = pltpu.with_memory_space_constraint(args[i], pltpu.HBM)
        in_specs.append(pl.BlockSpec(memory_space=pltpu.HBM if i in hbm else pltpu.VMEM))
    return pl.pallas_call(
        kernel,
        out_shape=[shape(s) for s in outs],
        in_specs=in_specs,
        out_specs=[out_spec(s) for s in outs],
        scratch_shapes=[buffer(s) for s in scratch],
        compiler_params=pltpu.CompilerParams(vmem_limit_bytes=megabytes << 20),
        cost_estimate=pl.CostEstimate(
            flops=mflops * 1000000, bytes_accessed=1 << 20, transcendentals=0
        ),
    )(*tables, *args)


def send(value, target):
    pairs = [
        (b * NZ + z, nb % NB * NZ + nz % NZ)
        for b in range(NB)
        for z in range(NZ)
        for nb, nz in [target(b, z)]
    ]
    return lax.ppermute(value, AXES, pairs)


def exchange(sends):
    swapped = send(sends, lambda b, z: (b ^ 1, z))
    far = send(sends[:FAR_ROWS], lambda b, z: (b - 3 if b % 2 == 0 else b + 3, z))
    x_got = send(
        jnp.concatenate([sends[:Y_AT], swapped[:Y_AT]]),
        lambda b, z: (b + 2 if b % 2 == 0 else b - 2, z),
    )
    z_got = send(
        jnp.concatenate([sends[Z_AT : Z_AT + 32], swapped[Z_AT + 32 :]]),
        lambda b, z: (b, z + 1 if b % 2 == 0 else z - 1),
    )
    x_got, z_got, far = lax.optimization_barrier((x_got, z_got, far))
    passed = send(jnp.concatenate([x_got, z_got[32:]]), lambda b, z: (b ^ 1, z))
    return swapped, x_got, z_got, far, passed


def total_over_devices(grads, place, beside):
    def other_core(v):
        return send(v, lambda b, z: (b ^ 1, z))

    halves = grads.reshape(2, HALF, 128)
    given = lax.dynamic_index_in_dim(halves, 1 - place[0] % 2, 0, keepdims=False)
    (mine,) = run(add_kernel, [place], [grads, other_core(given)], [(HALF, 128)], [], 10, 8)
    mine = mine.reshape(64, 1, HALF * 2)
    mine = lax.all_to_all(mine, CHIPS, 0, 0, tiled=True).sum(axis=0, keepdims=True)
    mine = jnp.broadcast_to(mine, (64, 1, HALF * 2))
    mine = lax.all_to_all(mine, CHIPS, 0, 0, tiled=True).reshape(HALF, 128)
    other, beside = lax.optimization_barrier((other_core(mine), beside))
    return mine, other, beside


def shards(populations, w_in, w_mid, w_out, cotangent, face_source, face_level, face_quadrant):
    f0 = populations.reshape(BLOCK)
    cot = cotangent.reshape(BLOCK)
    w_in_t = w_in.T
    w_mid = w_mid[0]
    w_mid_t = w_mid.T
    place = lax.axis_index(BLOCKS).astype(jnp.int32).reshape(1)
    tables = [place, face_source.T, face_level[0], face_quadrant[0]]
    hidden = pltpu.HBM((CHUNKS, HID, CHUNK), BF16)
    by_chunk = pltpu.VMEM((CHUNKS, HID, CHUNK), BF16)
    thin = jax.ShapeDtypeStruct(THIN, BF16)
    grad = (GROWS, 128)
    near = pltpu.VMEM(HIDDEN, BF16)
    near_thin = pltpu.VMEM(THIN, BF16)
    sems = pltpu.SemaphoreType.DMA

    post1, local2, sends, h0, h1 = run(
        first_kernel, tables[:1], [*tables[1:], f0, cot, w_in_t, w_mid, w_out],
        [BLOCK, BLOCK, SENDS, hidden, hidden],
        [pltpu.SMEM((4, NB), jnp.int32), pltpu.SMEM((1, 6), jnp.int32),
         pltpu.SMEM((1, 6), jnp.int32), X_TWO,
         BLOCK, BLOCK, pltpu.VMEM((Q, HID), BF16), pltpu.VMEM((HID, HID), BF16),
         pltpu.VMEM((Q, HID), BF16), by_chunk, by_chunk, BLOCK, *FACES[1:], FACES[2], sems((8,)),
         sems((2 * CHUNKS,))],
        4000, 32, range(8),
    )
    got = exchange(sends)
    post2, local1, sends, grads2 = run(
        second_kernel, tables, [post1, local2, *got, w_in_t, w_mid, w_mid_t, w_out],
        [BLOCK, BLOCK, SENDS, pltpu.HBM(grad, F32)],
        [grad, X_TWO, near_thin, near_thin, *[near] * 4, *[BLOCK] * 4, *FACES, FACES[2], sems((1,))],
        14000, 32,
    )
    got = exchange(sends)
    grads, fbar0 = run(
        third_kernel, tables, [f0, local1, *got, w_in_t, w_mid_t, w_out, grads2, h0, h1],
        [grad, BLOCK],
        [BLOCK, *[near] * 4, near_thin, near_thin, *FACES[:2], sems((2 * CHUNKS + 1,))],
        8000, 32, (10, 11, 12),
    )
    post2, grads = lax.optimization_barrier((post2, grads))
    (final,) = run(final_kernel, tables, [post2, *got], [BLOCK], [BLOCK, *FACES], 500, 8)
    mine, other, final = total_over_devices(grads, place, final)
    g_in, g_mid, g_out = run(
        unpack_kernel, [place], [mine, other], [(Q, HID), (HID, HID), (Q, HID)], [grad], 10, 8
    )
    whole = (Q, 1, 1, CELLS)
    return final.reshape(whole), fbar0.reshape(whole), g_in.T, g_mid[None], g_out


def solution(mesh):
    cells = P(None, "slab", BLOCKS, None)
    local = P("slab", BLOCKS, None)
    split = Mesh(mesh.devices.reshape(NX, NX, 2, NZ), AXES)
    return jax.shard_map(
        shards,
        mesh=split,
        in_specs=(cells, P(), P(), P(), cells, P(), local, local),
        out_specs=(cells, cells, P(), P(), P()),
        check_vma=False,
    )
```
